512 devices in a mesh: rows: 64 (over z, y), heads: 8 (over x, core).
Axes of the slice: x: 4, y: 4, z: 16, core: 2. Of those that a mesh axis runs over, the one named last changes fastest.
Arguments:
- query_proj: bfloat16 [64, 128, 2048], P('rows', None, 'heads'), may hold values from -6 to 6
- key_proj: bfloat16 [64, 128, 2048], P('rows', None, 'heads'), may hold values from -36 to 36
- value_proj: bfloat16 [64, 128, 2048], P('rows', None, 'heads'), may hold values from -6 to 6
- write_rate: bfloat16 [64, 128, 16], P('rows', None, 'heads'), may hold values from 0.099609375 to 0.8984375
- log_gate: bfloat16 [64, 128, 16, 4], P('rows', None, 'heads'), may hold values from -1 to 0
- tissue_lengths: int32 [64], P('rows'), may hold values from 32 to 128, as said below
- out_weight: bfloat16 [2048, 2048], P('heads'), may hold values from -0.125 to 0.125
- cotangent: bfloat16 [64, 128, 2048], P('rows', None, 'heads'), may hold values from -16 to 16
Outputs:
- encoded: bfloat16 [64, 128, 2048], P('rows', None, 'heads')
- query_grad: bfloat16 [64, 128, 2048], P('rows', None, 'heads')
- key_grad: bfloat16 [64, 128, 2048], P('rows', None, 'heads')
- value_grad: bfloat16 [64, 128, 2048], P('rows', None, 'heads')
- rate_grad: float32 [64, 128, 16], P('rows', None, 'heads')
- gate_grad: float32 [64, 128, 16, 4], P('rows', None, 'heads')
- weight_grad: float32 [2048, 2048], P('rows', 'heads')
The draws below stay inside these ranges and needn't reach their ends.
Inputs may be any that keep to these rules, and one draw needn't show every extreme that they name: Row r holds tissue in its first tissue_lengths[r] patches; some row is tissue in all 128 patches.
All inputs are finite; a program needn't handle non-finite values.
Results may differ from the reference program's by a relative error of at most 0.017.
Values may be sent and summed in bfloat16 or wider, within the bound.
No kernel may reach another device: no remote copies, remote signals or barrier semaphores. Data moves between devices by JAX's collectives and lax.ppermute only.
A program may use at most 64 MiB of HBM per device.

```python
import math
import jax
import jax.numpy as jnp
from jax import lax

ATTENTION_HEADS = 16
PATCH_COLUMNS = 128
PATCH_ROWS = 64
D = 2048
N_HEADS = 8


def draw_key_proj(key, part):
    key = jax.random.fold_in(key, 5)
    first, second, third = jax.random.split(key, 3)
    normal_base = jnp.clip(jax.random.normal(first, (PATCH_ROWS, PATCH_COLUMNS, D), jnp.float32), -4.0, 4.0)
    token_scale = jnp.exp(jax.random.uniform(second, (PATCH_ROWS, PATCH_COLUMNS, 1), jnp.float32, math.log(0.3), math.log(3.0)))
    channel_scale = jnp.exp(jax.random.uniform(third, (1, 1, D), jnp.float32, math.log(0.3), math.log(3.0)))
    return (normal_base * token_scale * channel_scale).astype(jnp.bfloat16)


def draw_log_gate(key, part):
    key = jax.random.fold_in(key, 9)
    direction_flows = jax.random.split(key, 7)
    linked_sequence = jnp.array([PATCH_COLUMNS, PATCH_COLUMNS, PATCH_ROWS, PATCH_ROWS], jnp.float32)
    share = 0.5
    quick_heads = jax.random.uniform(direction_flows[0], (ATTENTION_HEADS, 4), jnp.float32) < share
    quick_rate = 1.0 / jax.random.uniform(direction_flows[1], (ATTENTION_HEADS, 4), jnp.float32, 30.0, 50.0)
    slow_rate = jax.random.uniform(direction_flows[2], (ATTENTION_HEADS, 4), jnp.float32, 0.1, 0.5) * math.log(10.0) / linked_sequence
    baseline_rate = jnp.where(quick_heads, quick_rate, slow_rate)
    token_jitter = jnp.exp(jax.random.uniform(direction_flows[3], (PATCH_ROWS, PATCH_COLUMNS, ATTENTION_HEADS, 4), jnp.float32, -0.69, 0.69))
    row_multiplier = jnp.exp2(jax.random.uniform(direction_flows[4], (PATCH_ROWS, 1, 1, 1), jnp.float32, -1.0, 1.0))
    spike_mask = jax.random.uniform(direction_flows[5], (PATCH_ROWS, PATCH_COLUMNS, ATTENTION_HEADS, 4), jnp.float32) < 2.0 / linked_sequence
    spike_depth = jnp.log(jax.random.uniform(direction_flows[6], (PATCH_ROWS, PATCH_COLUMNS, ATTENTION_HEADS, 4), jnp.float32, 0.6, 0.8))
    return (-baseline_rate * token_jitter * row_multiplier + jnp.where(spike_mask, spike_depth, 0.0)).astype(jnp.bfloat16)


def draw_tissue_lengths(key, part):
    key = jax.random.fold_in(key, 13)
    first, second = jax.random.split(key)
    lengths = jax.random.randint(first, (PATCH_ROWS,), PATCH_COLUMNS // 4, PATCH_COLUMNS + 1, jnp.int32)
    full_row = jax.random.randint(second, (), 0, PATCH_ROWS, jnp.int32)
    return lengths.at[full_row].set(PATCH_COLUMNS)


def strengthened(values, key, source, target, blocks, factor):
    owner, partner = [(jnp.arange(values.shape[dim]) // (values.shape[dim] // blocks)).reshape([-1 if axis == dim else 1 for axis in range(values.ndim)]) for dim in (source, target)]
    chosen = jax.random.permutation(key, blocks)[partner]
    strong = (owner == chosen) | (owner == (partner + blocks // 2) % blocks)
    return jnp.where(strong, factor * values, values)


def shard_levels(rng, shape, cuts, least, top_value):
    level, own = 1.0, jax.random.fold_in(rng, 6)
    for position, shards_of in cuts:
        heights = jnp.exp(jax.random.uniform(jax.random.fold_in(own, position), (shards_of,), jnp.float32, least / len(cuts), top_value / len(cuts)))
        level = level * jnp.repeat(heights, shape[position] // shards_of).reshape([-1 if axis == position else 1 for axis in range(len(shape))])
    return level


def normal_values(own_key, shape, scale, bound, cuts=(), kind=jnp.bfloat16):
    gain = shard_levels(own_key, shape, cuts, -0.22, 0.18) if cuts else 1.0
    entries = jax.random.normal(own_key, shape, jnp.float32) * scale * gain
    return jnp.minimum(jnp.maximum(entries, -bound), bound).astype(kind)


def heavy_noise(rng, dims, width, limit, shards, heavy, kind=jnp.bfloat16):
    entries = width * jax.random.normal(rng, dims, jnp.float32)
    if shards:
        entries = entries * shard_levels(rng, dims, shards, -0.22, 0.18)
    return jnp.clip(strengthened(entries, jax.random.fold_in(rng, 3), *heavy), -limit, limit).astype(kind)


def setup_inputs(seed: int = 0) -> dict:
    seeds = jax.random.split(jax.random.key(seed), 9)
    return {
        "query_proj": normal_values(seeds[0], (PATCH_ROWS, PATCH_COLUMNS, D), 1.0, 6.0, ((0, 64), (2, 8))),
        "key_proj": draw_key_proj(jax.random.fold_in(seeds[8], 71), 0),
        "value_proj": normal_values(seeds[2], (PATCH_ROWS, PATCH_COLUMNS, D), 1.0, 6.0, ((0, 64), (2, 8))),
        "write_rate": jnp.clip(0.099609375 + 0.7988281 * jax.random.uniform(seeds[3], (PATCH_ROWS, PATCH_COLUMNS, ATTENTION_HEADS), jnp.float32) ** shard_levels(seeds[3], (PATCH_ROWS, PATCH_COLUMNS, ATTENTION_HEADS), ((0, 64), (2, 8)), -0.2, 0.2), 0.099609375, 0.8984375).astype(jnp.bfloat16),
        "log_gate": draw_log_gate(jax.random.fold_in(seeds[8], 71), 0),
        "tissue_lengths": draw_tissue_lengths(jax.random.fold_in(seeds[8], 71), 0),
        "out_weight": normal_values(seeds[6], (D, D), D ** -0.5, 0.125, ((0, 8),)),
        "cotangent": heavy_noise(seeds[7], (PATCH_ROWS, PATCH_COLUMNS, D), 1.0, 16.0, ((0, 64), (2, 8)), (0, 2, 64, 4.0)),
    }


def block_scan(queries, key_vecs, values, write_rates, log_gates):
    batch, length, features = queries.shape
    block_len = min(64, length)
    block_count = length // block_len

    def blocked(array):
        return jnp.swapaxes(array.reshape((batch, block_count, block_len) + array.shape[2:]), 0, 1)
    positions = lax.broadcasted_iota(jnp.int32, (block_len, block_len), 0)
    others = lax.broadcasted_iota(jnp.int32, (block_len, block_len), 1)
    strict_lower = positions > others
    inclusive = positions >= others
    identity = jnp.eye(block_len, dtype=jnp.float32)
    highest = lax.Precision.HIGHEST

    def advance(carried, parts):
        query_part, key_part, value_part, rate_part, gate_part = parts
        cumulated = jnp.cumsum(gate_part, axis=1)
        log_ratio = cumulated[:, :, None] - cumulated[:, None, :]
        earlier = jnp.exp(jnp.where(strict_lower, log_ratio, -jnp.inf))
        within = jnp.exp(jnp.where(inclusive, log_ratio, -jnp.inf))
        decays = jnp.exp(cumulated)
        key_gram = jnp.einsum('bik,bjk->bij', key_part, key_part, precision=highest)
        query_key = jnp.einsum('bik,bjk->bij', query_part, key_part, precision=highest)
        key_read = jnp.einsum('bik,bvk->biv', key_part, carried, precision=highest)
        query_read = jnp.einsum('bik,bvk->biv', query_part, carried, precision=highest)
        system = identity + earlier * key_gram * rate_part[:, None, :]
        targets = value_part - decays[:, :, None] * key_read
        errors = lax.linalg.triangular_solve(system, targets, left_side=True, lower=True, unit_diagonal=True)
        mixing = within * query_key * rate_part[:, None, :]
        outputs = decays[:, :, None] * query_read + jnp.einsum('bij,bjv->biv', mixing, errors, precision=highest)
        final_log = cumulated[:, -1:]
        tail_weight = jnp.exp(final_log - cumulated) * rate_part
        updated = jnp.exp(final_log)[:, :, None] * carried + jnp.einsum('biv,bik->bvk', errors * tail_weight[:, :, None], key_part, precision=highest)
        return (updated, outputs)
    start = jnp.zeros((batch, features, features), jnp.float32)
    unused, outputs = lax.scan(advance, start, (blocked(queries), blocked(key_vecs), blocked(values), blocked(write_rates), blocked(log_gates)))
    return jnp.swapaxes(outputs, 0, 1).reshape(batch, length, features)

def directions(queries, key_vecs, values, write_rates, log_gates, along):
    head_size = queries.shape[-1]
    scaled = queries.astype(jnp.float32) * head_size ** (-0.5)
    keyed = key_vecs.astype(jnp.float32)
    normed = keyed * lax.rsqrt(lax.optimization_barrier(jnp.sum(keyed * keyed, axis=-1, keepdims=True)) + 1e-06)
    order = (0, 2, 1) if along == 1 else (1, 2, 0)

    def to_seqs(array):
        moved = jnp.transpose(array, order + tuple(range(3, array.ndim)))
        return moved.reshape((-1, moved.shape[2]) + moved.shape[3:])
    seq_query = to_seqs(scaled)
    seq_key = to_seqs(normed)
    seq_value = to_seqs(values.astype(jnp.float32))
    seq_rate = to_seqs(write_rates.astype(jnp.float32))
    seq_gate = to_seqs(log_gates.astype(jnp.float32))
    forward = block_scan(seq_query, seq_key, seq_value, seq_rate, seq_gate[:, :, 0])
    backward = jnp.flip(block_scan(jnp.flip(seq_query, 1), jnp.flip(seq_key, 1), jnp.flip(seq_value, 1), jnp.flip(seq_rate, 1), jnp.flip(seq_gate[:, :, 1], 1)), 1)
    total = forward + backward
    dim_first, dim_second, head_count = write_rates.shape
    if along == 1:
        return total.reshape(dim_first, head_count, dim_second, head_size).transpose(0, 2, 1, 3)
    return total.reshape(dim_second, head_count, dim_first, head_size).transpose(2, 0, 1, 3)

def along_row(a, b, c, d, e):
    return directions(a, b, c, d, e, 1)

def along_column(a, b, c, d, e):
    return directions(a, b, c, d, e, 0)

def narrowed(array):
    return lax.optimization_barrier(array.astype(jnp.bfloat16)).astype(jnp.float32)

def reference(query_proj, key_proj, value_proj, write_rate, log_gate, tissue_lengths, out_weight, cotangent):
    rows_all, num_columns, model_dim = query_proj.shape
    head_count = write_rate.shape[2]
    head_size = model_dim // head_count
    columns = lax.broadcasted_iota(jnp.int32, (rows_all, num_columns), 1)
    tissue = (columns < tissue_lengths[:, None]).astype(jnp.float32)
    rate_m = (write_rate.astype(jnp.float32) * tissue[:, :, None]).astype(jnp.bfloat16)
    gate_m = (log_gate.astype(jnp.float32) * tissue[:, :, None, None]).astype(jnp.bfloat16)
    hidden_cot = lax.dot_general(cotangent.astype(jnp.float32), out_weight.astype(jnp.float32), (((2,), (1,)), ((), ())), preferred_element_type=jnp.float32)
    cot_m = (hidden_cot * tissue[:, :, None]).astype(jnp.bfloat16)

    def per_head(array):
        return jnp.moveaxis(array.reshape(rows_all, num_columns, head_count, head_size), 2, 0)[:, :, :, None, :]
    stacked = (per_head(query_proj), per_head(key_proj), per_head(value_proj), jnp.moveaxis(rate_m, 2, 0)[:, :, :, None], jnp.moveaxis(gate_m, 2, 0)[:, :, :, None, :], per_head(cot_m))

    def one_head(items):
        query_h, key_h, value_h, rate_h, gate_h, cot_h = [item.astype(jnp.float32) for item in items]
        row_out, row_pull = jax.vjp(along_row, query_h, key_h, value_h, rate_h, gate_h[..., 0:2])
        col_out, col_pull = jax.vjp(along_column, query_h, key_h, value_h, rate_h, gate_h[..., 2:4])
        row_grads = row_pull(cot_h)
        col_grads = [narrowed(item) for item in col_pull(cot_h)]
        return (row_out + narrowed(col_out), row_grads[0] + col_grads[0], row_grads[1] + col_grads[1], row_grads[2] + col_grads[2], row_grads[3] + col_grads[3], jnp.concatenate([row_grads[4], col_grads[4]], axis=-1))
    results = lax.map(one_head, stacked)

    def merge_heads(array):
        return jnp.moveaxis(array[:, :, :, 0, :], 0, 2).reshape(rows_all, num_columns, model_dim)
    hidden = (tissue[:, :, None] * merge_heads(results[0])).astype(jnp.bfloat16)
    group = model_dim // N_HEADS

    def add_group(total, index):
        start = (index * group).astype(jnp.int32)
        piece = lax.dynamic_slice_in_dim(hidden, start, group, 2)
        weight_rows = lax.dynamic_slice_in_dim(out_weight, start, group, 0)
        term = lax.dot_general(piece.astype(jnp.float32), weight_rows.astype(jnp.float32), (((2,), (0,)), ((), ())), preferred_element_type=jnp.float32)
        rounded = lax.optimization_barrier(term.astype(jnp.bfloat16))
        return (total + rounded.astype(jnp.float32), None)
    total, unused = lax.scan(add_group, jnp.zeros((rows_all, num_columns, model_dim), jnp.float32), jnp.arange(N_HEADS, dtype=jnp.int32))
    encoded = total.astype(jnp.bfloat16)
    weight_grad = lax.dot_general(cotangent.reshape(-1, model_dim).astype(jnp.float32), hidden.reshape(-1, model_dim).astype(jnp.float32), (((0,), (0,)), ((), ())), preferred_element_type=jnp.float32)
    query_grad = merge_heads(results[1]).astype(jnp.bfloat16)
    key_grad = merge_heads(results[2]).astype(jnp.bfloat16)
    value_grad = merge_heads(results[3]).astype(jnp.bfloat16)
    rate_grad = tissue[:, :, None] * jnp.moveaxis(results[4][:, :, :, 0], 0, 2)
    gate_grad = tissue[:, :, None, None] * jnp.moveaxis(results[5][:, :, :, 0, :], 0, 2)
    return (encoded, query_grad, key_grad, value_grad, rate_grad, gate_grad, weight_grad)
```

```python
import functools

import jax
import jax.numpy as jnp
from jax import lax
from jax.experimental import pallas as pl
from jax.experimental.pallas import tpu as pltpu
from jax.sharding import PartitionSpec as P

N = 128
F32 = jnp.float32
BF = jnp.bfloat16


def dot(a, b, ca=1, cb=0):
    return lax.dot_general(a.astype(BF), b.astype(BF), (((ca,), (cb,)), ((), ())), preferred_element_type=F32)


def iotas(rows=N, cols=N):
    return lax.broadcasted_iota(jnp.int32, (rows, cols), 0), lax.broadcasted_iota(jnp.int32, (rows, cols), 1)


def shr(x, n):
    return lax.shift_right_logical(x, jnp.int32(n))


def invert(systems, length):
    i, j = iotas()
    apart = i ^ j
    eye = jnp.where(apart == 0, 1.0, 0.0)
    solved = [eye - jnp.where(apart == 1, a, 0.0) for a in systems]
    level = 1
    while (2 << level) <= length:
        mask = shr(apart, level) == 1
        crossing = [jnp.where(mask, a, 0.0).astype(BF) for a in systems]
        halves = [t.astype(BF) for t in solved]
        inner = [dot(c, t) for c, t in zip(crossing, halves)]
        solved = [t - dot(h, m) for t, h, m in zip(solved, halves, inner)]
        level += 1
    return solved


def split3(x):
    hi = x.astype(BF)
    rest = x - hi.astype(F32)
    mid = rest.astype(BF)
    return hi, mid, (rest - mid.astype(F32)).astype(BF)


def prepare(q, k, small, length):
    i, j = iotas()
    shift = length.bit_length() - 1
    same = shr(i, shift) == shr(j, shift)
    before = [same & (i >= j), same & (i <= j)]
    sums = [jnp.where(m, 1.0, 0.0).astype(BF) for m in before]
    eye = i == j
    cum = [dot(m, small) for m in sums]
    cum_t = [c.T for c in cum]
    small_t = small.astype(F32).T
    heads = []
    for h in range(2):
        lanes = slice(h * N, (h + 1) * N)
        kh, qh = k[:, lanes], q[:, lanes]
        gram = dot(kh, kh, 1, 1)
        cross = dot(qh, kh, 1, 1)
        diag = jnp.where(eye, gram, 0.0)
        s_col = lax.rsqrt(jnp.sum(diag, axis=1, keepdims=True) + 1e-6)
        s_row = lax.rsqrt(jnp.sum(diag, axis=0, keepdims=True) + 1e-6)
        gram = gram * (s_col * s_row)
        cross = cross * (s_row * (N ** -0.5))
        rate_row = small_t[h : h + 1, :]
        per = []
        for d in range(2):
            lane = 2 + 2 * h + d
            ratio = cum[d][:, lane : lane + 1] - cum_t[d][lane : lane + 1, :]
            weight = jnp.exp(jnp.where(before[d], ratio, -jnp.inf)) * rate_row
            strict = jnp.where(eye, 0.0, weight)
            per.append((weight, strict, strict * gram, weight * cross))
        heads.append((s_col, s_row, per))
    return sums, heads


def forward(prepared, v, length):
    sums, heads = prepared
    systems = [p[2] for hd in heads for p in hd[2]]
    solved = [t.astype(BF) for t in invert(systems, length)]
    outs, errors = [], []
    for h in range(2):
        vh = v[:, h * N : (h + 1) * N]
        es = [dot(solved[2 * h + d], vh).astype(BF) for d in range(2)]
        mix = jnp.concatenate([heads[h][2][0][3].astype(BF), heads[h][2][1][3].astype(BF)], axis=1)
        outs.append(dot(mix, jnp.concatenate(es, axis=0)))
        errors += es
    return outs, solved, errors


def backward(prepared, solved, errors, q, k, small, cot):
    sums, heads = prepared
    i, j = iotas()
    gq, gk, gv, rowsums, colsums = [], [], [], [], []
    for h in range(2):
        lanes = slice(h * N, (h + 1) * N)
        s_col, s_row, per = heads[h]
        c, kh, qh = cot[:, lanes], k[:, lanes], q[:, lanes]
        es = errors[2 * h : 2 * h + 2]
        d_mix = dot(c, jnp.concatenate(es, axis=0), 1, 1)
        mix = jnp.concatenate([per[0][3].astype(BF), per[1][3].astype(BF)], axis=1)
        d_err = dot(mix, c, 0, 0)
        d_val = [dot(solved[2 * h + d], d_err[d * N : (d + 1) * N], 0, 0) for d in range(2)]
        d_sys = [-dot(d_val[d], es[d], 1, 1) for d in range(2)]
        d_gram, d_cross = 0.0, 0.0
        for d in range(2):
            weight, strict, system, mixing = per[d]
            dm = d_mix[:, d * N : (d + 1) * N]
            d_gram = d_gram + d_sys[d] * strict
            d_cross = d_cross + dm * weight
            total = d_sys[d] * system + dm * mixing
            rowsums.append(jnp.sum(total, axis=1, keepdims=True))
            colsums.append(jnp.sum(total, axis=0, keepdims=True))
        both = d_gram + d_gram.T
        gq.append(dot(d_cross * (s_row * (N ** -0.5)), kh))
        kf = kh.astype(F32)
        d_kn = dot(both * s_row, kh) + dot(d_cross, qh, 0, 0) * (N ** -0.5)
        along = s_col * jnp.sum(kf * d_kn, axis=1, keepdims=True)
        gk.append(s_col * (d_kn - kf * (s_col * along)))
        gv.append(d_val[0] + d_val[1])
    padded = jnp.concatenate(colsums + [jnp.zeros((N - 4, N), F32)], axis=0).T
    lane = j
    d_cum = -padded
    for s in range(4):
        d_cum = d_cum + jnp.where(lane == s, rowsums[s], 0.0)
    pieces = split3(d_cum)
    gates = [sum(dot(sums[1 - d], p) for p in pieces) for d in range(2)]
    rates = small.astype(F32)
    out = jnp.zeros((N, N), F32)
    for h in range(2):
        rate = rates[:, h : h + 1]
        whole = padded[:, 2 * h : 2 * h + 1] + padded[:, 2 * h + 1 : 2 * h + 2]
        g_rate = jnp.where(rate > 0, whole / jnp.where(rate > 0, rate, 1.0), 0.0)
        out = jnp.where(lane == h, g_rate, out)
        for d in range(2):
            s = 2 * h + d
            out = jnp.where(lane == 2 + s, gates[d][:, s : s + 1], out)
    return jnp.concatenate(gq, axis=1), jnp.concatenate(gk, axis=1), jnp.concatenate(gv, axis=1), out


VMEM = pl.BlockSpec(memory_space=pltpu.VMEM)
SMEM = pl.BlockSpec(memory_space=pltpu.SMEM)


def one_hot(mask):
    return jnp.where(mask, 1.0, 0.0).astype(BF)


def call(kernel, outs, args, specs=None, flops=100_000_000, name=None):
    return pl.pallas_call(
        kernel,
        out_shape=[jax.ShapeDtypeStruct(shape, dtype) for shape, dtype in outs],
        in_specs=specs or [VMEM] * len(args),
        out_specs=[VMEM] * len(outs),
        compiler_params=pltpu.CompilerParams(vmem_limit_bytes=48 * 1024 * 1024),
        cost_estimate=pl.CostEstimate(flops=flops, bytes_accessed=2_000_000, transcendentals=0),
        name=name,
    )(*args)


def pack_four(parts):
    out, patch = iotas(4 * N, N)
    total = 0.0
    for a, part in enumerate(parts):
        pick = ((shr(out, 1) & 3) == a) & (patch == 2 * shr(out, 3) + (out & 1))
        total = total + dot(one_hot(pick), part)
    return total.astype(BF)


def pack_four_back(parts):
    out, patch = iotas(4 * N, N)
    total = 0.0
    for a, part in enumerate(parts):
        pick = ((shr(out, 1) & 3) == a) & (patch == 64 * (out & 1) + shr(out, 3))
        total = total + dot(one_hot(pick), part)
    return total.astype(BF)


def to_columns(received, a):
    out, row = iotas(N, 4 * N)
    return dot(one_hot(row == 8 * (out & 63) + 2 * a + shr(out, 6)), received)


def to_rows(received, a):
    out, row = iotas(N, 4 * N)
    return dot(one_hot(row == 8 * shr(out, 1) + 2 * a + (out & 1)), received)


def pack_kernel(q_ref, k_ref, v_ref, small_ref, out_ref):
    out_ref[...] = pack_four([q_ref[...], k_ref[...], v_ref[...], small_ref[...]])


def row_kernel(
    info_ref, q_ref, k_ref, v_ref, small_ref, cot_ref, w_ref, o_ref, gq_ref, gk_ref, gv_ref, gs_ref, cm_ref
):
    patch, unused = iotas(N, 2 * N)
    cot = jnp.where(patch < info_ref[0], dot(cot_ref[...], w_ref[...], 1, 1), 0.0).astype(BF)
    cm_ref[...] = cot
    q, k, v, small = q_ref[...], k_ref[...], v_ref[...], small_ref[...]
    ready = prepare(q, k, small, N)
    outs, solved, errors = forward(ready, v, N)
    o_ref[...] = jnp.concatenate(outs, axis=1)
    gq_ref[...], gk_ref[...], gv_ref[...], gs_ref[...] = backward(ready, solved, errors, q, k, small, cot)


def col_forward_kernel(got_ref, cm_ref, send_ref, q_ref, k_ref, v_ref, small_ref, t_ref, e_ref):
    got = got_ref[...]
    q, k, v, small = [to_columns(got, a).astype(BF) for a in range(4)]
    small = small[:, :N]
    q_ref[...], k_ref[...], v_ref[...], small_ref[...] = q, k, v, small
    outs, solved, errors = forward(prepare(q, k, small, 64), v, 64)
    for s in range(4):
        t_ref[s * N : (s + 1) * N, :] = solved[s]
        e_ref[s * N : (s + 1) * N, :] = errors[s]
    out, patch = iotas(4 * N, N)
    head = out & 1
    column = shr(out, 1) & 1
    peer = shr(out, 3)
    late = (shr(out, 2) & 1) == 1
    total = 0.0
    for h in range(2):
        first = one_hot(~late & (head == h) & (patch == 2 * peer + column))
        second = one_hot(late & (head == h) & (patch == 64 * column + peer))
        total = total + dot(first, cm_ref[:, h * N : (h + 1) * N]) + dot(second, outs[h])
    send_ref[...] = total.astype(BF)


def hidden_kernel(info_ref, got_ref, o_ref, cot_ref, w_ref, own_ref, other_ref, wg_ref):
    got = got_ref[...]
    out, row = iotas(N, 4 * N)
    col = jnp.concatenate(
        [dot(one_hot(row == 8 * shr(out, 1) + 4 + 2 * (out & 1) + h), got) for h in range(2)], axis=1
    )
    patch, unused = iotas(N, 2 * N)
    hidden = jnp.where(patch < info_ref[0], o_ref[...] + col, 0.0).astype(BF)
    for z in range(16):
        part = dot(cot_ref[:, z * N : (z + 1) * N], hidden, 0, 0).astype(BF)
        for y in range(4):
            start = y * 512 + z * 32
            wg_ref[start : start + 32, :] = part[y * 32 : (y + 1) * 32, :]
    place, core = info_ref[1], info_ref[2]
    for step in range(4):
        for ref, side in ((own_ref, core), (other_ref, 1 - core)):
            block = 2 * ((place + step) & 3) + side
            lanes = pl.ds(pl.multiple_of(block * 2 * N, 2 * N), 2 * N)
            ref[step * N : (step + 1) * N, :] = dot(hidden, w_ref[:, lanes]).astype(BF)


def col_backward_kernel(got_ref, q_ref, k_ref, v_ref, small_ref, t_ref, e_ref, send_ref):
    got = got_ref[...]
    out, row = iotas(N, 4 * N)
    cot = jnp.concatenate(
        [dot(one_hot(row == 8 * (out & 63) + 2 * shr(out, 6) + h), got) for h in range(2)], axis=1
    ).astype(BF)
    q, k, small = q_ref[...], k_ref[...], small_ref[...]
    ready = prepare(q, k, small, 64)
    solved = [t_ref[s * N : (s + 1) * N, :] for s in range(4)]
    errors = [e_ref[s * N : (s + 1) * N, :] for s in range(4)]
    gq, gk, gv, gs = backward(ready, solved, errors, q, k, small, cot)
    send_ref[...] = pack_four_back([gq, gk, gv, jnp.concatenate([gs, jnp.zeros_like(gs)], axis=1)])


def final_kernel(info_ref, got_ref, gq_ref, gk_ref, gv_ref, gs_ref, q_ref, k_ref, v_ref, s_ref):
    got = got_ref[...]
    for a, (row_ref, out_ref) in enumerate(((gq_ref, q_ref), (gk_ref, k_ref), (gv_ref, v_ref))):
        out_ref[...] = (row_ref[...] + to_rows(got, a)).astype(BF)
    col = to_rows(got, 3)[:, :N]
    row = gs_ref[...]
    patch, lane = iotas()
    placed = jnp.where(lane < 2, row + col, 0.0)
    placed = jnp.where((lane >= 2) & (lane < 4), row, placed)
    placed = jnp.where((lane >= 4) & (lane < 6), pltpu.roll(col, 2, 1), placed)
    placed = jnp.where((lane >= 6) & (lane < 8), pltpu.roll(row, 2, 1), placed)
    placed = jnp.where((lane >= 8) & (lane < 10), pltpu.roll(col, 4, 1), placed)
    s_ref[...] = jnp.where(patch < info_ref[0], placed, 0.0)


def exchange(x, axis, groups=None):
    return lax.all_to_all(x, axis, split_axis=0, concat_axis=0, tiled=True, axis_index_groups=groups)


def per_device(
    query_proj, key_proj, value_proj, write_rate, log_gate, tissue_lengths, out_weight, cotangent
):
    q, k, v = query_proj[0], key_proj[0], value_proj[0]
    patch = lax.broadcasted_iota(jnp.int32, (N, 1), 0)
    tissue = patch < tissue_lengths[0]
    rate_m = jnp.where(tissue, write_rate[0], 0)
    gate_m = jnp.where(tissue[:, :, None], log_gate[0], 0)
    me = lax.axis_index("heads")
    info = jnp.stack([tissue_lengths[0], me // 2, me % 2]).astype(jnp.int32)
    small_row = jnp.concatenate([rate_m, gate_m[:, :, 0:2].reshape(N, 4), jnp.zeros((N, N - 6), BF)], axis=1)
    small_col = jnp.concatenate([rate_m, gate_m[:, :, 2:4].reshape(N, 4), jnp.zeros((N, 2 * N - 6), BF)], axis=1)
    wide, half, square = (N, 2 * N), (4 * N, N), (N, N)

    (send,) = call(pack_kernel, [((4 * N, 2 * N), BF)], [q, k, v, small_col], name="pack")
    got = exchange(send, "rows")
    full_cot = lax.all_gather(cotangent[0], "heads", axis=1, tiled=True)
    o_row, gq, gk, gv, gs, cot_m = call(
        row_kernel,
        [(wide, F32)] * 4 + [(square, F32), (wide, BF)],
        [info, q, k, v, small_row, full_cot, out_weight],
        [SMEM] + [VMEM] * 6,
        flops=6_000_000_000,
        name="row_directions",
    )
    send, qc, kc, vc, sc, tc, ec = call(
        col_forward_kernel,
        [(half, BF)] + [(wide, BF)] * 3 + [(square, BF)] + [(half, BF)] * 2,
        [got, cot_m],
        flops=3_000_000_000,
        name="column_forward",
    )
    got = exchange(send, "rows")
    own, other, partial_wg = call(
        hidden_kernel,
        [((4 * N, 2 * N), BF)] * 2 + [((2048, 2 * N), BF)],
        [info, got, o_row, full_cot, out_weight],
        [SMEM] + [VMEM] * 4,
        flops=2_000_000_000,
        name="hidden",
    )
    (send,) = call(
        col_backward_kernel,
        [((4 * N, 2 * N), BF)],
        [got, qc, kc, vc, sc, tc, ec],
        flops=3_000_000_000,
        name="column_backward",
    )
    y_groups = [[z * 4 + y for y in range(4)] for z in range(16)]
    z_groups = [[z * 4 + y for z in range(16)] for y in range(4)]
    summed = lax.psum_scatter(
        partial_wg, "rows", scatter_dimension=0, axis_index_groups=y_groups, tiled=True
    )
    got = exchange(send, "rows")
    grad_q, grad_k, grad_v, grad_s = call(
        final_kernel,
        [(wide, BF)] * 3 + [(square, F32)],
        [info, got, gq, gk, gv, gs],
        [SMEM] + [VMEM] * 5,
        flops=1_000_000_000,
        name="gradients",
    )
    swapped = lax.ppermute(other, "heads", [(i, i ^ 1) for i in range(8)])
    pairs = (own.astype(F32) + swapped.astype(F32)).astype(BF).reshape(4, N, 2 * N)
    encoded = own[:N].astype(F32) + swapped[:N].astype(F32)
    for step in range(1, 4):
        moves = [(i, ((i // 2 + step) % 4) * 2 + i % 2) for i in range(8)]
        encoded = encoded + lax.ppermute(pairs[step], "heads", moves).astype(F32)
    encoded = encoded.astype(BF)[None]

    pieces = exchange(summed, "rows", z_groups)
    weight_grad = jnp.sum(pieces.reshape(16, 32, 2 * N).astype(F32), axis=0)
    rate_grad = grad_s[None, :, 0:2]
    gate_grad = grad_s[:, 2:10].reshape(1, N, 2, 4)
    return (encoded, grad_q[None], grad_k[None], grad_v[None], rate_grad, gate_grad, weight_grad)


def solution(mesh):
    in_specs = (
        P("rows", None, "heads"),
        P("rows", None, "heads"),
        P("rows", None, "heads"),
        P("rows", None, "heads"),
        P("rows", None, "heads", None),
        P("rows"),
        P("heads", None),
        P("rows", None, "heads"),
    )
    out_specs = (
        P("rows", None, "heads"),
        P("rows", None, "heads"),
        P("rows", None, "heads"),
        P("rows", None, "heads"),
        P("rows", None, "heads"),
        P("rows", None, "heads", None),
        P("rows", "heads"),
    )
    return jax.shard_map(
        per_device, mesh=mesh, in_specs=in_specs, out_specs=out_specs, check_vma=False
    )
```

```python
import functools

import jax
import jax.numpy as jnp
from jax import lax
from jax.experimental import pallas as pl
from jax.experimental.pallas import tpu as pltpu
from jax.sharding import PartitionSpec as P

N = 128
F32 = jnp.float32
BF = jnp.bfloat16


def dot(a, b, ca=1, cb=0):
    return lax.dot_general(a.astype(BF), b.astype(BF), (((ca,), (cb,)), ((), ())), preferred_element_type=F32)


def iotas(rows=N, cols=N):
    return lax.broadcasted_iota(jnp.int32, (rows, cols), 0), lax.broadcasted_iota(jnp.int32, (rows, cols), 1)


def shr(x, n):
    return lax.shift_right_logical(x, jnp.int32(n))


def invert(systems, length):
    i, j = iotas()
    apart = i ^ j
    eye = jnp.where(apart == 0, 1.0, 0.0)
    solved = [eye - jnp.where(apart == 1, a, 0.0) for a in systems]
    level = 1
    while (2 << level) <= length:
        mask = shr(apart, level) == 1
        crossing = [jnp.where(mask, a, 0.0).astype(BF) for a in systems]
        halves = [t.astype(BF) for t in solved]
        inner = [dot(c, t) for c, t in zip(crossing, halves)]
        solved = [t - dot(h, m) for t, h, m in zip(solved, halves, inner)]
        level += 1
    return solved


def split3(x):
    hi = x.astype(BF)
    rest = x - hi.astype(F32)
    mid = rest.astype(BF)
    return hi, mid, (rest - mid.astype(F32)).astype(BF)


def prepare(q, k, small, length, first):
    i, j = iotas()
    shift = length.bit_length() - 1
    same = shr(i, shift) == shr(j, shift)
    before = [same & (i >= j), same & (i <= j)]
    sums = [jnp.where(m, 1.0, 0.0).astype(BF) for m in before]
    eye = i == j
    cum = [dot(m, small, 1, 1) for m in sums]
    cum_t = [dot(small, m, 1, 1) for m in sums]
    heads = []
    for h in range(2):
        lanes = slice(h * N, (h + 1) * N)
        kh, qh = k[:, lanes], q[:, lanes]
        gram = dot(kh, kh, 1, 1)
        cross = dot(qh, kh, 1, 1)
        diag = jnp.where(eye, gram, 0.0)
        s_col = lax.rsqrt(jnp.sum(diag, axis=1, keepdims=True) + 1e-6)
        s_row = lax.rsqrt(jnp.sum(diag, axis=0, keepdims=True) + 1e-6)
        gram = gram * (s_col * s_row)
        cross = cross * (s_row * (N ** -0.5))
        rate_row = small[8 + h : 9 + h, :]
        per = []
        for d in range(2):
            g = 4 * h + first + d
            ratio = cum[d][:, g : g + 1] - cum_t[d][g : g + 1, :]
            weight = jnp.exp(jnp.where(before[d], ratio, -jnp.inf)) * rate_row
            strict = jnp.where(eye, 0.0, weight)
            per.append((weight, strict, strict * gram, weight * cross))
        heads.append((s_col, s_row, per))
    return sums, heads


def forward(prepared, v, length):
    sums, heads = prepared
    systems = [p[2] for hd in heads for p in hd[2]]
    solved = [t.astype(BF) for t in invert(systems, length)]
    outs, errors = [], []
    for h in range(2):
        vh = v[:, h * N : (h + 1) * N]
        es = [dot(solved[2 * h + d], vh).astype(BF) for d in range(2)]
        mix = jnp.concatenate([heads[h][2][0][3].astype(BF), heads[h][2][1][3].astype(BF)], axis=1)
        outs.append(dot(mix, jnp.concatenate(es, axis=0)))
        errors += es
    return outs, solved, errors


def backward(prepared, solved, errors, q, k, small, cot, first):
    sums, heads = prepared
    i, j = iotas()
    gq, gk, gv, rowsums, colsums = [], [], [], [], []
    for h in range(2):
        lanes = slice(h * N, (h + 1) * N)
        s_col, s_row, per = heads[h]
        c, kh, qh = cot[:, lanes], k[:, lanes], q[:, lanes]
        es = errors[2 * h : 2 * h + 2]
        d_mix = dot(c, jnp.concatenate(es, axis=0), 1, 1)
        mix = jnp.concatenate([per[0][3].astype(BF), per[1][3].astype(BF)], axis=1)
        d_err = dot(mix, c, 0, 0)
        d_val = [dot(solved[2 * h + d], d_err[d * N : (d + 1) * N], 0, 0) for d in range(2)]
        d_sys = [-dot(d_val[d], es[d], 1, 1) for d in range(2)]
        d_gram, d_cross = 0.0, 0.0
        for d in range(2):
            weight, strict, system, mixing = per[d]
            dm = d_mix[:, d * N : (d + 1) * N]
            d_gram = d_gram + d_sys[d] * strict
            d_cross = d_cross + dm * weight
            total = d_sys[d] * system + dm * mixing
            rowsums.append(jnp.sum(total, axis=1, keepdims=True))
            colsums.append(jnp.sum(total, axis=0, keepdims=True))
        both = d_gram + d_gram.T
        gq.append(dot(d_cross * (s_row * (N ** -0.5)), kh))
        kf = kh.astype(F32)
        d_kn = dot(both * s_row, kh) + dot(d_cross, qh, 0, 0) * (N ** -0.5)
        along = s_col * jnp.sum(kf * d_kn, axis=1, keepdims=True)
        gk.append(s_col * (d_kn - kf * (s_col * along)))
        gv.append(d_val[0] + d_val[1])
    across = jnp.zeros((N, N), F32)
    for s in range(4):
        across = jnp.where(j == s, rowsums[s], across)
    d_cum = across.T[:8, :] - jnp.concatenate(colsums + [jnp.zeros((4, N), F32)], axis=0)
    pieces = split3(d_cum)
    gates = [sum(dot(p, sums[1 - d], 1, 1) for p in pieces) for d in range(2)]
    zero = jnp.zeros((1, N), F32)
    out = [zero] * 16
    for h in range(2):
        rate = small[8 + h : 9 + h, :]
        whole = colsums[2 * h] + colsums[2 * h + 1]
        out[8 + h] = jnp.where(rate > 0, whole / jnp.where(rate > 0, rate, 1.0), 0.0)
        for d in range(2):
            s = 2 * h + d
            out[4 * h + first + d] = gates[d][s : s + 1, :]
    out = jnp.concatenate(out, axis=0)
    return jnp.concatenate(gq, axis=1), jnp.concatenate(gk, axis=1), jnp.concatenate(gv, axis=1), out


VMEM = pl.BlockSpec(memory_space=pltpu.VMEM)
SMEM = pl.BlockSpec(memory_space=pltpu.SMEM)


def one_hot(mask):
    return jnp.where(mask, 1.0, 0.0).astype(BF)


def call(kernel, outs, args, specs=None, flops=100_000_000, name=None):
    return pl.pallas_call(
        kernel,
        out_shape=[jax.ShapeDtypeStruct(shape, dtype) for shape, dtype in outs],
        in_specs=specs or [VMEM] * len(args),
        out_specs=[VMEM] * len(outs),
        compiler_params=pltpu.CompilerParams(vmem_limit_bytes=48 * 1024 * 1024),
        cost_estimate=pl.CostEstimate(flops=flops, bytes_accessed=2_000_000, transcendentals=0),
        name=name,
    )(*args)


def small_rows(info_ref, rate_ref, gate_ref):
    rows = jnp.concatenate(
        [gate_ref[...].astype(F32), rate_ref[...].astype(F32), jnp.zeros((6, N), F32)], axis=0
    )
    unused, patch = iotas(16, N)
    return jnp.where(patch < info_ref[0], rows, 0.0)


def pack_four(parts, small, back):
    out, patch = iotas(4 * N, N)
    wanted = patch == (64 * (out & 1) + shr(out, 3) if back else 2 * shr(out, 3) + (out & 1))
    total = 0.0
    for a, part in enumerate(parts):
        total = total + dot(one_hot(wanted & ((shr(out, 1) & 3) == a)), part)
    pick = one_hot(wanted & ((shr(out, 1) & 3) == 3))
    scalars = dot(pick, jnp.concatenate([small, jnp.zeros((N - 16, N), F32)], axis=0), 1, 1)
    return (total + jnp.concatenate([scalars, jnp.zeros_like(scalars)], axis=1)).astype(BF)


def to_columns(received, a):
    out, row = iotas(N, 4 * N)
    return dot(one_hot(row == 8 * (out & 63) + 2 * a + shr(out, 6)), received)


def to_rows(received, a):
    out, row = iotas(N, 4 * N)
    return dot(one_hot(row == 8 * shr(out, 1) + 2 * a + (out & 1)), received)


def pack_kernel(info_ref, q_ref, k_ref, v_ref, rate_ref, gate_ref, out_ref):
    small = small_rows(info_ref, rate_ref, gate_ref)
    out_ref[...] = pack_four([q_ref[...], k_ref[...], v_ref[...]], small, False)


def cotangent_kernel(info_ref, cot_ref, w_ref, cm_ref):
    patch, unused = iotas(N, 2 * N)
    cm_ref[...] = jnp.where(patch < info_ref[0], dot(cot_ref[...], w_ref[...], 1, 1), 0.0).astype(BF)


def row_kernel(
    info_ref, q_ref, k_ref, v_ref, rate_ref, gate_ref, cm_ref, o_ref, gq_ref, gk_ref, gv_ref, gs_ref
):
    q, k, v, cot = q_ref[...], k_ref[...], v_ref[...], cm_ref[...]
    small = small_rows(info_ref, rate_ref, gate_ref)
    ready = prepare(q, k, small, N, 0)
    outs, solved, errors = forward(ready, v, N)
    o_ref[...] = jnp.concatenate(outs, axis=1)
    gq_ref[...], gk_ref[...], gv_ref[...], gs_ref[...] = backward(ready, solved, errors, q, k, small, cot, 0)


def col_forward_kernel(got_ref, cm_ref, send_ref, q_ref, k_ref, v_ref, small_ref, t_ref, e_ref):
    got = got_ref[...]
    q, k, v = [to_columns(got, a).astype(BF) for a in range(3)]
    small = to_columns(got[:, :N], 3).T[:16, :]
    q_ref[...], k_ref[...], v_ref[...], small_ref[...] = q, k, v, small
    outs, solved, errors = forward(prepare(q, k, small, 64, 2), v, 64)
    for s in range(4):
        t_ref[s * N : (s + 1) * N, :] = solved[s]
        e_ref[s * N : (s + 1) * N, :] = errors[s]
    out, patch = iotas(4 * N, N)
    head = out & 1
    column = shr(out, 1) & 1
    peer = shr(out, 3)
    late = (shr(out, 2) & 1) == 1
    total = 0.0
    for h in range(2):
        first = one_hot(~late & (head == h) & (patch == 2 * peer + column))
        second = one_hot(late & (head == h) & (patch == 64 * column + peer))
        total = total + dot(first, cm_ref[:, h * N : (h + 1) * N]) + dot(second, outs[h])
    send_ref[...] = total.astype(BF)


def hidden_kernel(info_ref, got_ref, o_ref, cot_ref, w_ref, own_ref, other_ref, wg_ref):
    got = got_ref[...]
    out, row = iotas(N, 4 * N)
    col = jnp.concatenate(
        [dot(one_hot(row == 8 * shr(out, 1) + 4 + 2 * (out & 1) + h), got) for h in range(2)], axis=1
    )
    patch, unused = iotas(N, 2 * N)
    hidden = jnp.where(patch < info_ref[0], o_ref[...] + col, 0.0).astype(BF)
    for z in range(16):
        part = dot(cot_ref[:, z * N : (z + 1) * N], hidden, 0, 0).astype(BF)
        for y in range(4):
            start = y * 512 + z * 32
            wg_ref[start : start + 32, :] = part[y * 32 : (y + 1) * 32, :]
    place, core = info_ref[1], info_ref[2]
    for step in range(4):
        for ref, side in ((own_ref, core), (other_ref, 1 - core)):
            block = 2 * ((place + step) & 3) + side
            lanes = pl.ds(pl.multiple_of(block * 2 * N, 2 * N), 2 * N)
            ref[step * N : (step + 1) * N, :] = dot(hidden, w_ref[:, lanes]).astype(BF)


def col_backward_kernel(got_ref, q_ref, k_ref, v_ref, small_ref, t_ref, e_ref, send_ref):
    got = got_ref[...]
    out, row = iotas(N, 4 * N)
    cot = jnp.concatenate(
        [dot(one_hot(row == 8 * (out & 63) + 2 * shr(out, 6) + h), got) for h in range(2)], axis=1
    ).astype(BF)
    q, k, small = q_ref[...], k_ref[...], small_ref[...]
    ready = prepare(q, k, small, 64, 2)
    solved = [t_ref[s * N : (s + 1) * N, :] for s in range(4)]
    errors = [e_ref[s * N : (s + 1) * N, :] for s in range(4)]
    gq, gk, gv, gs = backward(ready, solved, errors, q, k, small, cot, 2)
    send_ref[...] = pack_four([gq, gk, gv], gs, True)


def final_kernel(info_ref, got_ref, gq_ref, gk_ref, gv_ref, gs_ref, q_ref, k_ref, v_ref, rate_ref, gate_ref):
    got = got_ref[...]
    for a, (row_ref, out_ref) in enumerate(((gq_ref, q_ref), (gk_ref, k_ref), (gv_ref, v_ref))):
        out_ref[...] = (row_ref[...] + to_rows(got, a)).astype(BF)
    unused, patch = iotas(16, N)
    small = jnp.where(patch < info_ref[0], gs_ref[...] + to_rows(got[:, :N], 3).T[:16, :], 0.0)
    gate_ref[...] = small[:8, :]
    rate_ref[...] = small[8:10, :]


def exchange(x, axis, groups=None):
    return lax.all_to_all(x, axis, split_axis=0, concat_axis=0, tiled=True, axis_index_groups=groups)


def per_device(
    query_proj, key_proj, value_proj, write_rate, log_gate, tissue_lengths, out_weight, cotangent
):
    q, k, v = query_proj[0], key_proj[0], value_proj[0]
    rate = write_rate[0].T
    gate = log_gate[0].transpose(1, 2, 0).reshape(8, N)
    me = lax.axis_index("heads")
    info = jnp.stack([tissue_lengths[0], lax.shift_right_logical(me, 1), me & 1])
    wide, half, few = (N, 2 * N), (4 * N, N), (16, N)

    (send,) = call(
        pack_kernel,
        [((4 * N, 2 * N), BF)],
        [tissue_lengths, q, k, v, rate, gate],
        [SMEM] + [VMEM] * 5,
        name="pack",
    )
    got = exchange(send, "rows")
    full_cot = lax.all_gather(cotangent[0], "heads", axis=1, tiled=True)
    (cot_m,) = call(
        cotangent_kernel,
        [(wide, BF)],
        [info, full_cot, out_weight],
        [SMEM] + [VMEM] * 2,
        flops=1_000_000_000,
        name="cotangent",
    )
    send, qc, kc, vc, sc, tc, ec = call(
        col_forward_kernel,
        [(half, BF)] + [(wide, BF)] * 3 + [(few, F32)] + [(half, BF)] * 2,
        [got, cot_m],
        flops=3_000_000_000,
        name="column_forward",
    )
    got = exchange(send, "rows")
    rate, unused = lax.optimization_barrier((rate, sc))
    o_row, gq, gk, gv, gs = call(
        row_kernel,
        [(wide, F32)] * 4 + [(few, F32)],
        [info, q, k, v, rate, gate, cot_m],
        [SMEM] + [VMEM] * 6,
        flops=6_000_000_000,
        name="row_directions",
    )
    got = exchange(send, "rows")
    own, other, partial_wg = call(
        hidden_kernel,
        [((4 * N, 2 * N), BF)] * 2 + [((2048, 2 * N), BF)],
        [info, got, o_row, full_cot, out_weight],
        [SMEM] + [VMEM] * 4,
        flops=2_000_000_000,
        name="hidden",
    )
    (send,) = call(
        col_backward_kernel,
        [((4 * N, 2 * N), BF)],
        [got, qc, kc, vc, sc, tc, ec],
        flops=3_000_000_000,
        name="column_backward",
    )
    y_groups = [[z * 4 + y for y in range(4)] for z in range(16)]
    z_groups = [[z * 4 + y for z in range(16)] for y in range(4)]
    summed = lax.psum_scatter(
        partial_wg, "rows", scatter_dimension=0, axis_index_groups=y_groups, tiled=True
    )
    got = exchange(send, "rows")
    grad_q, grad_k, grad_v, grad_rate, grad_gate = call(
        final_kernel,
        [(wide, BF)] * 3 + [((2, N), F32), ((8, N), F32)],
        [info, got, gq, gk, gv, gs],
        [SMEM] + [VMEM] * 5,
        flops=1_000_000_000,
        name="gradients",
    )
    swapped = lax.ppermute(other, "heads", [(i, i ^ 1) for i in range(8)])
    pairs = (own.astype(F32) + swapped.astype(F32)).astype(BF).reshape(4, N, 2 * N)
    encoded = own[:N].astype(F32) + swapped[:N].astype(F32)
    for step in range(1, 4):
        moves = [(i, ((i // 2 + step) % 4) * 2 + i % 2) for i in range(8)]
        encoded = encoded + lax.ppermute(pairs[step], "heads", moves).astype(F32)
    encoded = encoded.astype(BF)[None]

    encoded, summed = lax.optimization_barrier((encoded, summed))
    pieces = exchange(summed, "rows", z_groups)
    weight_grad = jnp.sum(pieces.reshape(16, 32, 2 * N).astype(F32), axis=0)
    rate_grad = grad_rate.T[None]
    gate_grad = grad_gate.reshape(2, 4, N).transpose(2, 0, 1)[None]
    return (encoded, grad_q[None], grad_k[None], grad_v[None], rate_grad, gate_grad, weight_grad)


def solution(mesh):
    in_specs = (
        P("rows", None, "heads"),
        P("rows", None, "heads"),
        P("rows", None, "heads"),
        P("rows", None, "heads"),
        P("rows", None, "heads", None),
        P("rows"),
        P("heads", None),
        P("rows", None, "heads"),
    )
    out_specs = (
        P("rows", None, "heads"),
        P("rows", None, "heads"),
        P("rows", None, "heads"),
        P("rows", None, "heads"),
        P("rows", None, "heads"),
        P("rows", None, "heads", None),
        P("rows", "heads"),
    )
    return jax.shard_map(
        per_device, mesh=mesh, in_specs=in_specs, out_specs=out_specs, check_vma=False
    )
```

```python
import functools

import jax
import jax.numpy as jnp
from jax import lax
from jax.experimental import pallas as pl
from jax.experimental.pallas import tpu as pltpu
from jax.sharding import PartitionSpec as P

N = 128
F32 = jnp.float32
BF = jnp.bfloat16


def dot(a, b, ca=1, cb=0):
    return lax.dot_general(a.astype(BF), b.astype(BF), (((ca,), (cb,)), ((), ())), preferred_element_type=F32)


def iotas(rows=N, cols=N):
    return lax.broadcasted_iota(jnp.int32, (rows, cols), 0), lax.broadcasted_iota(jnp.int32, (rows, cols), 1)


def shr(x, n):
    return lax.shift_right_logical(x, jnp.int32(n))


def invert(systems, length):
    i, j = iotas()
    apart = i ^ j
    eye = jnp.where(apart == 0, 1.0, 0.0)
    solved = [eye - jnp.where(apart == 1, a, 0.0) for a in systems]
    level = 1
    while (2 << level) <= length:
        mask = shr(apart, level) == 1
        crossing = [jnp.where(mask, a, 0.0).astype(BF) for a in systems]
        halves = [t.astype(BF) for t in solved]
        inner = [dot(c, t) for c, t in zip(crossing, halves)]
        solved = [t - dot(h, m) for t, h, m in zip(solved, halves, inner)]
        level += 1
    return solved


def split3(x):
    hi = x.astype(BF)
    rest = x - hi.astype(F32)
    mid = rest.astype(BF)
    return hi, mid, (rest - mid.astype(F32)).astype(BF)


def prepare(q, k, small, length, first):
    i, j = iotas()
    shift = length.bit_length() - 1
    same = shr(i, shift) == shr(j, shift)
    before = [same & (i >= j), same & (i <= j)]
    sums = [jnp.where(m, 1.0, 0.0).astype(BF) for m in before]
    eye = i == j
    cum = [dot(m, small, 1, 1) for m in sums]
    cum_t = [dot(small, m, 1, 1) for m in sums]
    heads = []
    for h in range(2):
        lanes = slice(h * N, (h + 1) * N)
        kh, qh = k[:, lanes], q[:, lanes]
        gram = dot(kh, kh, 1, 1)
        cross = dot(qh, kh, 1, 1)
        diag = jnp.where(eye, gram, 0.0)
        s_col = lax.rsqrt(jnp.sum(diag, axis=1, keepdims=True) + 1e-6)
        s_row = lax.rsqrt(jnp.sum(diag, axis=0, keepdims=True) + 1e-6)
        gram = gram * (s_col * s_row)
        cross = cross * (s_row * (N ** -0.5))
        rate_row = small[8 + h : 9 + h, :]
        per = []
        for d in range(2):
            g = 4 * h + first + d
            ratio = cum[d][:, g : g + 1] - cum_t[d][g : g + 1, :]
            weight = jnp.exp(jnp.where(before[d], ratio, -jnp.inf)) * rate_row
            strict = jnp.where(eye, 0.0, weight)
            per.append((weight, strict, strict * gram, weight * cross))
        heads.append((s_col, s_row, per))
    return sums, heads


def forward(prepared, v, length):
    sums, heads = prepared
    systems = [p[2] for hd in heads for p in hd[2]]
    solved = [t.astype(BF) for t in invert(systems, length)]
    outs, errors = [], []
    for h in range(2):
        vh = v[:, h * N : (h + 1) * N]
        es = [dot(solved[2 * h + d], vh).astype(BF) for d in range(2)]
        mix = jnp.concatenate([heads[h][2][0][3].astype(BF), heads[h][2][1][3].astype(BF)], axis=1)
        outs.append(dot(mix, jnp.concatenate(es, axis=0)))
        errors += es
    return outs, solved, errors


def backward(prepared, solved, errors, q, k, small, cot, first):
    sums, heads = prepared
    i, j = iotas()
    gq, gk, gv, rowsums, colsums = [], [], [], [], []
    for h in range(2):
        lanes = slice(h * N, (h + 1) * N)
        s_col, s_row, per = heads[h]
        c, kh, qh = cot[:, lanes], k[:, lanes], q[:, lanes]
        es = errors[2 * h : 2 * h + 2]
        d_mix = dot(c, jnp.concatenate(es, axis=0), 1, 1)
        mix = jnp.concatenate([per[0][3].astype(BF), per[1][3].astype(BF)], axis=1)
        d_err = dot(mix, c, 0, 0)
        d_val = [dot(solved[2 * h + d], d_err[d * N : (d + 1) * N], 0, 0) for d in range(2)]
        d_sys = [-dot(d_val[d], es[d], 1, 1) for d in range(2)]
        d_gram, d_cross = 0.0, 0.0
        for d in range(2):
            weight, strict, system, mixing = per[d]
            dm = d_mix[:, d * N : (d + 1) * N]
            d_gram = d_gram + d_sys[d] * strict
            d_cross = d_cross + dm * weight
            total = d_sys[d] * system + dm * mixing
            rowsums.append(jnp.sum(total, axis=1, keepdims=True))
            colsums.append(jnp.sum(total, axis=0, keepdims=True))
        both = d_gram + d_gram.T
        gq.append(dot(d_cross * (s_row * (N ** -0.5)), kh))
        kf = kh.astype(F32)
        d_kn = dot(both * s_row, kh) + dot(d_cross, qh, 0, 0) * (N ** -0.5)
        along = s_col * jnp.sum(kf * d_kn, axis=1, keepdims=True)
        gk.append(s_col * (d_kn - kf * (s_col * along)))
        gv.append(d_val[0] + d_val[1])
    across = jnp.zeros((N, N), F32)
    for s in range(4):
        across = jnp.where(j == s, rowsums[s], across)
    d_cum = across.T[:8, :] - jnp.concatenate(colsums + [jnp.zeros((4, N), F32)], axis=0)
    pieces = split3(d_cum)
    gates = [sum(dot(p, sums[1 - d], 1, 1) for p in pieces) for d in range(2)]
    zero = jnp.zeros((1, N), F32)
    out = [zero] * 16
    for h in range(2):
        rate = small[8 + h : 9 + h, :]
        whole = colsums[2 * h] + colsums[2 * h + 1]
        out[8 + h] = jnp.where(rate > 0, whole / jnp.where(rate > 0, rate, 1.0), 0.0)
        for d in range(2):
            s = 2 * h + d
            out[4 * h + first + d] = gates[d][s : s + 1, :]
    out = jnp.concatenate(out, axis=0)
    return jnp.concatenate(gq, axis=1), jnp.concatenate(gk, axis=1), jnp.concatenate(gv, axis=1), out


VMEM = pl.BlockSpec(memory_space=pltpu.VMEM)
SMEM = pl.BlockSpec(memory_space=pltpu.SMEM)


def one_hot(mask):
    return jnp.where(mask, 1.0, 0.0).astype(BF)


def call(kernel, outs, args, specs=None, flops=100_000_000, name=None, scratch=()):
    return pl.pallas_call(
        kernel,
        out_shape=[jax.ShapeDtypeStruct(shape, dtype) for shape, dtype in outs],
        in_specs=specs or [VMEM] * len(args),
        out_specs=[VMEM] * len(outs),
        scratch_shapes=list(scratch),
        compiler_params=pltpu.CompilerParams(vmem_limit_bytes=48 * 1024 * 1024),
        cost_estimate=pl.CostEstimate(flops=flops, bytes_accessed=2_000_000, transcendentals=0),
        name=name,
    )(*args)


def small_rows(info_ref, rate_ref, gate_ref):
    rows = jnp.concatenate(
        [gate_ref[...].astype(F32), rate_ref[...].astype(F32), jnp.ones((6, N), F32)], axis=0
    )
    row, patch = iotas(16, N)
    return jnp.where((patch < info_ref[0]) & (row < 11), rows, 0.0)


def pack_four(parts, small, back):
    out, patch = iotas(4 * N, N)
    wanted = patch == (64 * (out & 1) + shr(out, 3) if back else 2 * shr(out, 3) + (out & 1))
    picks = [one_hot(wanted & ((shr(out, 1) & 3) == a)) for a in range(4)]
    total = sum(dot(pick, part) for pick, part in zip(picks, parts))
    scalars = dot(picks[0], jnp.concatenate([small, jnp.zeros((N - 16, N), F32)], axis=0), 1, 1)
    return jnp.concatenate([total, scalars], axis=1).astype(BF)


def to_columns(received, a):
    out, row = iotas(N, 4 * N)
    return dot(one_hot(row == 8 * (out & 63) + 2 * a + shr(out, 6)), received)


def to_rows(received, a):
    out, row = iotas(N, 4 * N)
    return dot(one_hot(row == 8 * shr(out, 1) + 2 * a + (out & 1)), received)


def pack_kernel(info_ref, rate_ref, gate_ref, q_ref, k_ref, v_ref, cot_ref, out_ref, held, sems):
    copies = [
        pltpu.make_async_copy(ref, held.at[a], sems.at[a])
        for a, ref in enumerate((q_ref, k_ref, v_ref, cot_ref))
    ]
    for copy in copies:
        copy.start()
    small = small_rows(info_ref, rate_ref, gate_ref)
    for copy in copies:
        copy.wait()
    out_ref[...] = pack_four([held[a] for a in range(4)], small, False)


def row_kernel(
    info_ref, q_ref, k_ref, v_ref, rate_ref, gate_ref, cot_ref, w_ref, o_ref, gq_ref, gk_ref, gv_ref, gs_ref
):
    patch, unused = iotas(N, 2 * N)
    cot = jnp.where(patch < info_ref[0], dot(cot_ref[...], w_ref[...], 1, 1), 0.0).astype(BF)
    q, k, v = q_ref[...], k_ref[...], v_ref[...]
    small = small_rows(info_ref, rate_ref, gate_ref)
    ready = prepare(q, k, small, N, 0)
    outs, solved, errors = forward(ready, v, N)
    o_ref[...] = jnp.where(patch < info_ref[0], jnp.concatenate(outs, axis=1), 0.0)
    gq_ref[...], gk_ref[...], gv_ref[...], gs_ref[...] = backward(ready, solved, errors, q, k, small, cot, 0)


def column_cotangent_kernel(got_ref, cot_ref):
    cot_ref[...] = to_columns(got_ref[:, : 2 * N], 3).astype(BF)


def column_kernel(got_ref, cot_ref, w_ref, send_ref, o_ref):
    got = got_ref[...]
    q, k, v = [to_columns(got[:, : 2 * N], a).astype(BF) for a in range(3)]
    scalars = to_columns(got[:, 2 * N :], 0)
    small = scalars.T[:16, :]
    tissue = scalars[:, 10:11] > 0.5
    cot = jnp.where(tissue, dot(cot_ref[...], w_ref[...], 1, 1), 0.0).astype(BF)
    ready = prepare(q, k, small, 64, 2)
    outs, solved, errors = forward(ready, v, 64)
    out = jnp.where(tissue, jnp.concatenate(outs, axis=1), 0.0).astype(BF)
    o_ref[...] = out
    gq, gk, gv, gs = backward(ready, solved, errors, q, k, small, cot, 2)
    send_ref[...] = pack_four([out, gq, gk, gv], gs, True)


def weight_kernel(row_cot_ref, row_o_ref, col_cot_ref, col_o_ref, wg_ref):
    hidden = jnp.concatenate([row_o_ref[...].astype(BF), col_o_ref[...]], axis=0)
    for z in range(16):
        lanes = slice(z * N, (z + 1) * N)
        cot = jnp.concatenate([row_cot_ref[:, lanes], col_cot_ref[:, lanes]], axis=0)
        part = dot(cot, hidden, 0, 0).astype(BF)
        for y in range(4):
            start = y * 512 + z * 32
            wg_ref[start : start + 32, :] = part[y * 32 : (y + 1) * 32, :]


def hidden_kernel(info_ref, got_ref, o_ref, w_ref, own_ref, other_ref):
    hidden = (o_ref[...] + to_rows(got_ref[:, : 2 * N], 0)).astype(BF)
    place, core = info_ref[1], info_ref[2]
    for step in range(4):
        for ref, side in ((own_ref, core), (other_ref, 1 - core)):
            block = 2 * ((place + step) & 3) + side
            lanes = pl.ds(pl.multiple_of(block * 2 * N, 2 * N), 2 * N)
            ref[step * N : (step + 1) * N, :] = dot(hidden, w_ref[:, lanes]).astype(BF)


def final_kernel(info_ref, got_ref, gq_ref, gk_ref, gv_ref, gs_ref, q_ref, k_ref, v_ref, rate_ref, gate_ref):
    got = got_ref[...]
    for a, (row_ref, out_ref) in enumerate(((gq_ref, q_ref), (gk_ref, k_ref), (gv_ref, v_ref))):
        out_ref[...] = (row_ref[...] + to_rows(got[:, : 2 * N], a + 1)).astype(BF)
    unused, patch = iotas(16, N)
    small = jnp.where(patch < info_ref[0], gs_ref[...] + to_rows(got[:, 2 * N :], 0).T[:16, :], 0.0)
    gate_ref[...] = small[:8, :]
    rate_ref[...] = small[8:10, :]


def exchange(x, axis, groups=None):
    return lax.all_to_all(x, axis, split_axis=0, concat_axis=0, tiled=True, axis_index_groups=groups)


def per_device(
    query_proj, key_proj, value_proj, write_rate, log_gate, tissue_lengths, out_weight, cotangent
):
    q, k, v = query_proj[0], key_proj[0], value_proj[0]
    rate = write_rate[0].T
    gate = log_gate[0].transpose(1, 2, 0).reshape(8, N)
    me = lax.axis_index("heads")
    info = jnp.stack([tissue_lengths[0], lax.shift_right_logical(me, 1), me & 1])
    wide, few = (N, 2 * N), (16, N)

    (send,) = call(
        pack_kernel,
        [((4 * N, 3 * N), BF)],
        [tissue_lengths, rate, gate, q, k, v, cotangent[0]],
        [SMEM, VMEM, VMEM] + [pl.BlockSpec(memory_space=pl.ANY)] * 4,
        name="pack",
        scratch=[pltpu.VMEM((4, N, 2 * N), BF), pltpu.SemaphoreType.DMA((4,))],
    )
    got = exchange(send, "rows")
    row_cot = lax.all_gather(cotangent[0], "heads", axis=1, tiled=True)
    o_row, gq, gk, gv, gs = call(
        row_kernel,
        [(wide, F32)] * 4 + [(few, F32)],
        [info, q, k, v, rate, gate, row_cot, out_weight],
        [SMEM] + [VMEM] * 7,
        flops=6_000_000_000,
        name="row_directions",
    )
    (col_cot,) = call(column_cotangent_kernel, [(wide, BF)], [got], name="column_cotangent")
    col_cot = lax.all_gather(col_cot, "heads", axis=1, tiled=True)
    send, o_col = call(
        column_kernel,
        [((4 * N, 3 * N), BF), (wide, BF)],
        [got, col_cot, out_weight],
        flops=6_000_000_000,
        name="column_directions",
    )
    got = exchange(send, "rows")
    (partial_wg,) = call(
        weight_kernel,
        [((2048, 2 * N), BF)],
        [row_cot, o_row, col_cot, o_col],
        flops=2_000_000_000,
        name="weight_gradient",
    )
    y_groups = [[z * 4 + y for y in range(4)] for z in range(16)]
    z_groups = [[z * 4 + y for z in range(16)] for y in range(4)]
    summed = lax.psum_scatter(
        partial_wg, "rows", scatter_dimension=0, axis_index_groups=y_groups, tiled=True
    )
    own, other = call(
        hidden_kernel,
        [((4 * N, 2 * N), BF)] * 2,
        [info, got, o_row, out_weight],
        [SMEM] + [VMEM] * 3,
        flops=1_000_000_000,
        name="hidden",
    )
    grad_q, grad_k, grad_v, grad_rate, grad_gate = call(
        final_kernel,
        [(wide, BF)] * 3 + [((2, N), F32), ((8, N), F32)],
        [info, got, gq, gk, gv, gs],
        [SMEM] + [VMEM] * 5,
        flops=1_000_000_000,
        name="gradients",
    )
    swapped = lax.ppermute(other, "heads", [(i, i ^ 1) for i in range(8)])
    pairs = (own.astype(F32) + swapped.astype(F32)).astype(BF).reshape(4, N, 2 * N)
    encoded = own[:N].astype(F32) + swapped[:N].astype(F32)
    for step in range(1, 4):
        moves = [(i, ((i // 2 + step) % 4) * 2 + i % 2) for i in range(8)]
        encoded = encoded + lax.ppermute(pairs[step], "heads", moves).astype(F32)
    encoded = encoded.astype(BF)[None]

    pieces = exchange(summed, "rows", z_groups)
    weight_grad = jnp.sum(pieces.reshape(16, 32, 2 * N).astype(F32), axis=0)
    rate_grad = grad_rate.T[None]
    gate_grad = grad_gate.reshape(2, 4, N).transpose(2, 0, 1)[None]
    return (encoded, grad_q[None], grad_k[None], grad_v[None], rate_grad, gate_grad, weight_grad)


def solution(mesh):
    in_specs = (
        P("rows", None, "heads"),
        P("rows", None, "heads"),
        P("rows", None, "heads"),
        P("rows", None, "heads"),
        P("rows", None, "heads", None),
        P("rows"),
        P("heads", None),
        P("rows", None, "heads"),
    )
    out_specs = (
        P("rows", None, "heads"),
        P("rows", None, "heads"),
        P("rows", None, "heads"),
        P("rows", None, "heads"),
        P("rows", None, "heads"),
        P("rows", None, "heads", None),
        P("rows", "heads"),
    )
    return jax.shard_map(
        per_device, mesh=mesh, in_specs=in_specs, out_specs=out_specs, check_vma=False
    )
```

```python
import functools

import jax
import jax.numpy as jnp
from jax import lax
from jax.experimental import pallas as pl
from jax.experimental.pallas import tpu as pltpu
from jax.sharding import PartitionSpec as P

N = 128
F32 = jnp.float32
BF = jnp.bfloat16


def dot(a, b, ca=1, cb=0):
    return lax.dot_general(a.astype(BF), b.astype(BF), (((ca,), (cb,)), ((), ())), preferred_element_type=F32)


def iotas(rows=N, cols=N):
    return lax.broadcasted_iota(jnp.int32, (rows, cols), 0), lax.broadcasted_iota(jnp.int32, (rows, cols), 1)


def shr(x, n):
    return lax.shift_right_logical(x, jnp.int32(n))


def invert(systems, length):
    i, j = iotas()
    apart = i ^ j
    eye = jnp.where(apart == 0, 1.0, 0.0)
    solved = [eye - jnp.where(apart == 1, a, 0.0) for a in systems]
    level = 1
    while (2 << level) <= length:
        mask = shr(apart, level) == 1
        crossing = [jnp.where(mask, a, 0.0).astype(BF) for a in systems]
        halves = [t.astype(BF) for t in solved]
        inner = [dot(c, t) for c, t in zip(crossing, halves)]
        solved = [t - dot(h, m) for t, h, m in zip(solved, halves, inner)]
        level += 1
    return solved


def split3(x):
    hi = x.astype(BF)
    rest = x - hi.astype(F32)
    mid = rest.astype(BF)
    return hi, mid, (rest - mid.astype(F32)).astype(BF)


def prepare(q, k, small, length, first):
    i, j = iotas()
    shift = length.bit_length() - 1
    same = shr(i, shift) == shr(j, shift)
    before = [same & (i >= j), same & (i <= j)]
    sums = [jnp.where(m, 1.0, 0.0).astype(BF) for m in before]
    eye = i == j
    cum = [dot(m, small, 1, 1) for m in sums]
    cum_t = [dot(small, m, 1, 1) for m in sums]
    heads = []
    for h in range(2):
        lanes = slice(h * N, (h + 1) * N)
        kh, qh = k[:, lanes], q[:, lanes]
        gram = dot(kh, kh, 1, 1)
        cross = dot(qh, kh, 1, 1)
        diag = jnp.where(eye, gram, 0.0)
        s_col = lax.rsqrt(jnp.sum(diag, axis=1, keepdims=True) + 1e-6)
        s_row = lax.rsqrt(jnp.sum(diag, axis=0, keepdims=True) + 1e-6)
        gram = gram * (s_col * s_row)
        cross = cross * (s_row * (N ** -0.5))
        rate_row = small[8 + h : 9 + h, :]
        per = []
        for d in range(2):
            g = 4 * h + first + d
            ratio = cum[d][:, g : g + 1] - cum_t[d][g : g + 1, :]
            weight = jnp.exp(jnp.where(before[d], ratio, -jnp.inf)) * rate_row
            strict = jnp.where(eye, 0.0, weight)
            per.append((weight, strict, strict * gram, weight * cross))
        heads.append((s_col, s_row, per))
    return sums, heads


def forward(prepared, v, length):
    sums, heads = prepared
    systems = [p[2] for hd in heads for p in hd[2]]
    solved = [t.astype(BF) for t in invert(systems, length)]
    outs, errors = [], []
    for h in range(2):
        vh = v[:, h * N : (h + 1) * N]
        es = [dot(solved[2 * h + d], vh).astype(BF) for d in range(2)]
        mix = jnp.concatenate([heads[h][2][0][3].astype(BF), heads[h][2][1][3].astype(BF)], axis=1)
        outs.append(dot(mix, jnp.concatenate(es, axis=0)))
        errors += es
    return outs, solved, errors


def backward(prepared, solved, errors, q, k, small, cot, first):
    sums, heads = prepared
    i, j = iotas()
    gq, gk, gv, rowsums, colsums = [], [], [], [], []
    for h in range(2):
        lanes = slice(h * N, (h + 1) * N)
        s_col, s_row, per = heads[h]
        c, kh, qh = cot[:, lanes], k[:, lanes], q[:, lanes]
        es = errors[2 * h : 2 * h + 2]
        d_mix = dot(c, jnp.concatenate(es, axis=0), 1, 1)
        mix = jnp.concatenate([per[0][3].astype(BF), per[1][3].astype(BF)], axis=1)
        d_err = dot(mix, c, 0, 0)
        d_val = [dot(solved[2 * h + d], d_err[d * N : (d + 1) * N], 0, 0) for d in range(2)]
        d_sys = [-dot(d_val[d], es[d], 1, 1) for d in range(2)]
        d_gram, d_cross = 0.0, 0.0
        for d in range(2):
            weight, strict, system, mixing = per[d]
            dm = d_mix[:, d * N : (d + 1) * N]
            d_gram = d_gram + d_sys[d] * strict
            d_cross = d_cross + dm * weight
            total = d_sys[d] * system + dm * mixing
            rowsums.append(jnp.sum(total, axis=1, keepdims=True))
            colsums.append(jnp.sum(total, axis=0, keepdims=True))
        both = d_gram + d_gram.T
        gq.append(dot(d_cross * (s_row * (N ** -0.5)), kh))
        kf = kh.astype(F32)
        d_kn = dot(both * s_row, kh) + dot(d_cross, qh, 0, 0) * (N ** -0.5)
        along = s_col * jnp.sum(kf * d_kn, axis=1, keepdims=True)
        gk.append(s_col * (d_kn - kf * (s_col * along)))
        gv.append(d_val[0] + d_val[1])
    across = jnp.zeros((N, N), F32)
    for s in range(4):
        across = jnp.where(j == s, rowsums[s], across)
    d_cum = across.T[:8, :] - jnp.concatenate(colsums + [jnp.zeros((4, N), F32)], axis=0)
    pieces = split3(d_cum)
    gates = [sum(dot(p, sums[1 - d], 1, 1) for p in pieces) for d in range(2)]
    zero = jnp.zeros((1, N), F32)
    out = [zero] * 16
    for h in range(2):
        rate = small[8 + h : 9 + h, :]
        whole = colsums[2 * h] + colsums[2 * h + 1]
        out[8 + h] = jnp.where(rate > 0, whole / jnp.where(rate > 0, rate, 1.0), 0.0)
        for d in range(2):
            s = 2 * h + d
            out[4 * h + first + d] = gates[d][s : s + 1, :]
    out = jnp.concatenate(out, axis=0)
    return jnp.concatenate(gq, axis=1), jnp.concatenate(gk, axis=1), jnp.concatenate(gv, axis=1), out


VMEM = pl.BlockSpec(memory_space=pltpu.VMEM)
SMEM = pl.BlockSpec(memory_space=pltpu.SMEM)


def one_hot(mask):
    return jnp.where(mask, 1.0, 0.0).astype(BF)


def call(kernel, outs, args, specs=None, flops=100_000_000, name=None, scratch=(), limit=48):
    return pl.pallas_call(
        kernel,
        out_shape=[jax.ShapeDtypeStruct(shape, dtype) for shape, dtype in outs],
        in_specs=specs or [VMEM] * len(args),
        out_specs=[VMEM] * len(outs),
        scratch_shapes=list(scratch),
        compiler_params=pltpu.CompilerParams(vmem_limit_bytes=limit * 1024 * 1024),
        cost_estimate=pl.CostEstimate(flops=flops, bytes_accessed=2_000_000, transcendentals=0),
        name=name,
    )(*args)


def small_rows(info_ref, rate_ref, gate_ref):
    rows = jnp.concatenate(
        [gate_ref[...].astype(F32), rate_ref[...].astype(F32), jnp.ones((6, N), F32)], axis=0
    )
    row, patch = iotas(16, N)
    return jnp.where((patch < info_ref[0]) & (row < 11), rows, 0.0)


def shuffle(by_column, inverse):
    i, j = iotas(144, 144)
    packed, plain = (j, i) if inverse else (i, j)
    peer = shr(packed * 3641, 16)
    rest = packed - 18 * peer
    c = rest & 1
    within = 8 * c + peer if by_column else 2 * peer + c
    return one_hot(plain == 16 * shr(rest, 1) + within)


def pack(parts, small, by_column, out_ref):
    parts = [part[:, h * N : (h + 1) * N].astype(F32) for part in parts for h in range(2)]
    parts.append(jnp.concatenate([small, jnp.zeros((N - 16, N), F32)], axis=0).T)
    order = shuffle(by_column, False)
    for b in range(8):
        if by_column:
            rows = [part[start + 8 * b : start + 8 * b + 8] for part in parts for start in (0, 64)]
        else:
            rows = [part[16 * b : 16 * b + 16] for part in parts]
        out_ref[144 * b : 144 * b + 144, :] = dot(order, jnp.concatenate(rows, axis=0)).astype(BF)


def unpack(got_ref, by_column):
    order = shuffle(by_column, True)
    blocks = [dot(order, got_ref[144 * b : 144 * b + 144, :]) for b in range(8)]
    parts = []
    for s in range(9):
        if by_column:
            rows = [block[16 * s + 8 * c : 16 * s + 8 * c + 8] for c in range(2) for block in blocks]
        else:
            rows = [block[16 * s : 16 * s + 16] for block in blocks]
        parts.append(jnp.concatenate(rows, axis=0))
    return [jnp.concatenate(parts[2 * a : 2 * a + 2], axis=1) for a in range(4)], parts[8]


def pack_kernel(info_ref, rate_ref, gate_ref, q_ref, k_ref, v_ref, cot_ref, out_ref, held, sems):
    copies = [
        pltpu.make_async_copy(ref, held.at[a], sems.at[a])
        for a, ref in enumerate((q_ref, k_ref, v_ref, cot_ref))
    ]
    for copy in copies:
        copy.start()
    small = small_rows(info_ref, rate_ref, gate_ref)
    for copy in copies:
        copy.wait()
    pack([held[a] for a in range(4)], small, False, out_ref)


def row_kernel(
    info_ref, q_ref, k_ref, v_ref, rate_ref, gate_ref, cot_ref, w_ref, o_ref, gq_ref, gk_ref, gv_ref, gs_ref
):
    patch, unused = iotas(N, 2 * N)
    cot = jnp.where(patch < info_ref[0], dot(cot_ref[...], w_ref[...], 1, 1), 0.0).astype(BF)
    q, k, v = q_ref[...], k_ref[...], v_ref[...]
    small = small_rows(info_ref, rate_ref, gate_ref)
    ready = prepare(q, k, small, N, 0)
    outs, solved, errors = forward(ready, v, N)
    o_ref[...] = jnp.where(patch < info_ref[0], jnp.concatenate(outs, axis=1), 0.0)
    gq_ref[...], gk_ref[...], gv_ref[...], gs_ref[...] = backward(ready, solved, errors, q, k, small, cot, 0)


def unpack_kernel(got_ref, q_ref, k_ref, v_ref, cot_ref, small_ref, tissue_ref):
    parts, scalars = unpack(got_ref, True)
    for part, ref in zip(parts, (q_ref, k_ref, v_ref, cot_ref)):
        ref[...] = part.astype(BF)
    small_ref[...] = scalars.T[:16, :]
    tissue_ref[...] = jnp.broadcast_to(scalars[:, 10:11], (N, 2 * N))


def column_kernel(q_ref, k_ref, v_ref, small_ref, tissue_ref, cot_ref, w_ref, send_ref, o_ref):
    q, k, v, small = q_ref[...], k_ref[...], v_ref[...], small_ref[...]
    tissue = tissue_ref[...] > 0.5
    cot = jnp.where(tissue, dot(cot_ref[...], w_ref[...], 1, 1), 0.0).astype(BF)
    ready = prepare(q, k, small, 64, 2)
    outs, solved, errors = forward(ready, v, 64)
    out = jnp.where(tissue, jnp.concatenate(outs, axis=1), 0.0).astype(BF)
    o_ref[...] = out
    gq, gk, gv, gs = backward(ready, solved, errors, q, k, small, cot, 2)
    pack([out, gq, gk, gv], gs, True, send_ref)


def weight_kernel(row_cot_ref, row_o_ref, col_cot_ref, col_o_ref, wg_ref):
    hidden = jnp.concatenate([row_o_ref[...].astype(BF), col_o_ref[...]], axis=0)
    for z in range(16):
        lanes = slice(z * N, (z + 1) * N)
        cot = jnp.concatenate([row_cot_ref[:, lanes], col_cot_ref[:, lanes]], axis=0)
        part = dot(cot, hidden, 0, 0).astype(BF)
        for y in range(4):
            start = y * 512 + z * 32
            wg_ref[start : start + 32, :] = part[y * 32 : (y + 1) * 32, :]


def projection_kernel(info_ref, w_ref, own_ref, other_ref):
    place, core = info_ref[1], info_ref[2]
    for step in range(4):
        for ref, side in ((own_ref, core), (other_ref, 1 - core)):
            block = 2 * ((place + step) & 3) + side
            lanes = pl.ds(pl.multiple_of(block * 2 * N, 2 * N), 2 * N)
            ref[step] = w_ref[:, lanes]


def gradient_kernel(
    info_ref, got_ref, o_ref, gq_ref, gk_ref, gv_ref, gs_ref, hidden_ref, q_ref, k_ref, v_ref, rate_ref, gate_ref
):
    parts, scalars = unpack(got_ref, False)
    hidden_ref[...] = (o_ref[...] + parts[0]).astype(BF)
    for part, row_ref, out_ref in zip(parts[1:], (gq_ref, gk_ref, gv_ref), (q_ref, k_ref, v_ref)):
        out_ref[...] = (row_ref[...] + part).astype(BF)
    unused, patch = iotas(16, N)
    small = jnp.where(patch < info_ref[0], gs_ref[...] + scalars.T[:16, :], 0.0)
    gate_ref[...] = small[:8, :]
    rate_ref[...] = small[8:10, :]


def encode_kernel(info_ref, hidden_ref, own_ref, swapped_ref, first_ref, second_ref, third_ref, out_ref):
    place, core = info_ref[1], info_ref[2]
    total = 0.0
    rows = [(own_ref[0], swapped_ref[0])]
    rows += [(ref[0], ref[1]) for ref in (first_ref, second_ref, third_ref)]
    for step, pair in enumerate(rows):
        for side, weights in zip((core, 1 - core), pair):
            block = 2 * ((place - step) & 3) + side
            lanes = pl.ds(pl.multiple_of(block * 2 * N, 2 * N), 2 * N)
            total = total + dot(hidden_ref[:, lanes], weights)
    out_ref[...] = total.astype(BF)


def exchange(x, axis, groups=None):
    return lax.all_to_all(x, axis, split_axis=0, concat_axis=0, tiled=True, axis_index_groups=groups)


def swap_rows(x):
    return exchange(x.reshape(64, 9, 2, N), "rows").reshape(18 * 64, N)


def per_device(
    query_proj, key_proj, value_proj, write_rate, log_gate, tissue_lengths, out_weight, cotangent
):
    q, k, v = query_proj[0], key_proj[0], value_proj[0]
    rate = write_rate[0].T
    gate = log_gate[0].transpose(1, 2, 0).reshape(8, N)
    me = lax.axis_index("heads")
    info = jnp.stack([tissue_lengths[0], lax.shift_right_logical(me, 1), me & 1])
    wide, few = (N, 2 * N), (16, N)

    (send,) = call(
        pack_kernel,
        [((18 * 64, N), BF)],
        [tissue_lengths, rate, gate, q, k, v, cotangent[0]],
        [SMEM, VMEM, VMEM] + [pl.BlockSpec(memory_space=pl.ANY)] * 4,
        name="pack",
        scratch=[pltpu.VMEM((4, N, 2 * N), BF), pltpu.SemaphoreType.DMA((4,))],
        limit=62,
    )
    got = swap_rows(send)
    row_cot = lax.all_gather(cotangent[0], "heads", axis=1, tiled=True)
    o_row, gq, gk, gv, gs = call(
        row_kernel,
        [(wide, F32)] * 4 + [(few, F32)],
        [info, q, k, v, rate, gate, row_cot, out_weight],
        [SMEM] + [VMEM] * 7,
        flops=6_000_000_000,
        name="row_directions",
    )
    qc, kc, vc, col_cot, sc, tissue = call(
        unpack_kernel, [(wide, BF)] * 4 + [(few, F32), (wide, F32)], [got], name="unpack"
    )
    col_cot = lax.all_gather(col_cot, "heads", axis=1, tiled=True)
    send, o_col = call(
        column_kernel,
        [((18 * 64, N), BF), (wide, BF)],
        [qc, kc, vc, sc, tissue, col_cot, out_weight],
        flops=6_000_000_000,
        name="column_directions",
    )
    got = swap_rows(send)
    (partial_wg,) = call(
        weight_kernel,
        [((2048, 2 * N), BF)],
        [row_cot, o_row, col_cot, o_col],
        flops=2_000_000_000,
        name="weight_gradient",
    )
    y_groups = [[z * 4 + y for y in range(4)] for z in range(16)]
    z_groups = [[z * 4 + y for z in range(16)] for y in range(4)]
    summed = lax.psum_scatter(
        partial_wg, "rows", scatter_dimension=0, axis_index_groups=y_groups, tiled=True
    )
    weight, unused = lax.optimization_barrier((out_weight, o_col))
    block = (4, 2 * N, 2 * N)
    own, other = call(projection_kernel, [(block, BF)] * 2, [info, weight], [SMEM, VMEM], name="projection")
    swapped = lax.ppermute(other, "heads", [(i, i ^ 1) for i in range(8)])
    arrived = []
    for step in range(1, 4):
        moves = [(i, ((i // 2 + step) % 4) * 2 + i % 2) for i in range(8)]
        arrived.append(lax.ppermute(jnp.stack([own[step], swapped[step]]), "heads", moves))
    hidden, grad_q, grad_k, grad_v, grad_rate, grad_gate = call(
        gradient_kernel,
        [(wide, BF)] * 4 + [((2, N), F32), ((8, N), F32)],
        [info, got, o_row, gq, gk, gv, gs],
        [SMEM] + [VMEM] * 6,
        name="gradients",
    )
    hidden = lax.all_gather(hidden, "heads", axis=1, tiled=True)
    (encoded,) = call(
        encode_kernel,
        [(wide, BF)],
        [info, hidden, own, swapped] + arrived,
        [SMEM] + [VMEM] * 6,
        flops=1_000_000_000,
        name="encode",
    )
    encoded = encoded[None]

    pieces = exchange(summed, "rows", z_groups)
    weight_grad = jnp.sum(pieces.reshape(16, 32, 2 * N).astype(F32), axis=0)
    rate_grad = grad_rate.T[None]
    gate_grad = grad_gate.reshape(2, 4, N).transpose(2, 0, 1)[None]
    return (encoded, grad_q[None], grad_k[None], grad_v[None], rate_grad, gate_grad, weight_grad)


def solution(mesh):
    in_specs = (
        P("rows", None, "heads"),
        P("rows", None, "heads"),
        P("rows", None, "heads"),
        P("rows", None, "heads"),
        P("rows", None, "heads", None),
        P("rows"),
        P("heads", None),
        P("rows", None, "heads"),
    )
    out_specs = (
        P("rows", None, "heads"),
        P("rows", None, "heads"),
        P("rows", None, "heads"),
        P("rows", None, "heads"),
        P("rows", None, "heads"),
        P("rows", None, "heads", None),
        P("rows", "heads"),
    )
    return jax.shard_map(
        per_device, mesh=mesh, in_specs=in_specs, out_specs=out_specs, check_vma=False
    )
```

```python
import functools

import jax
import jax.numpy as jnp
from jax import lax
from jax.experimental import pallas as pl
from jax.experimental.pallas import tpu as pltpu
from jax.sharding import PartitionSpec as P

N = 128
F32 = jnp.float32
BF = jnp.bfloat16


def dot(a, b, ca=1, cb=0):
    return lax.dot_general(a.astype(BF), b.astype(BF), (((ca,), (cb,)), ((), ())), preferred_element_type=F32)


def iotas(rows=N, cols=N):
    return lax.broadcasted_iota(jnp.int32, (rows, cols), 0), lax.broadcasted_iota(jnp.int32, (rows, cols), 1)


def shr(x, n):
    return lax.shift_right_logical(x, jnp.int32(n))


def invert(systems, length):
    i, j = iotas()
    apart = i ^ j
    eye = jnp.where(apart == 0, 1.0, 0.0)
    solved = [eye - jnp.where(apart == 1, a, 0.0) for a in systems]
    level = 1
    while (2 << level) <= length:
        mask = shr(apart, level) == 1
        crossing = [jnp.where(mask, a, 0.0).astype(BF) for a in systems]
        halves = [t.astype(BF) for t in solved]
        inner = [dot(c, t) for c, t in zip(crossing, halves)]
        solved = [t - dot(h, m) for t, h, m in zip(solved, halves, inner)]
        level += 1
    return solved


def split3(x):
    hi = x.astype(BF)
    rest = x - hi.astype(F32)
    mid = rest.astype(BF)
    return hi, mid, (rest - mid.astype(F32)).astype(BF)


def prefix_sums(length):
    i, j = iotas()
    shift = length.bit_length() - 1
    same = shr(i, shift) == shr(j, shift)
    before = [same & (i >= j), same & (i <= j)]
    return [jnp.where(m, 1.0, 0.0).astype(BF) for m in before], before, i == j


def prepare(q, k, small, length, first):
    sums, before, eye = prefix_sums(length)
    cum = [dot(m, small, 1, 1) for m in sums]
    cum_t = [dot(small, m, 1, 1) for m in sums]
    heads = []
    for h in range(2):
        lanes = slice(h * N, (h + 1) * N)
        kh, qh = k[:, lanes], q[:, lanes]
        gram = dot(kh, kh, 1, 1)
        cross = dot(qh, kh, 1, 1)
        diag = jnp.where(eye, gram, 0.0)
        s_col = lax.rsqrt(jnp.sum(diag, axis=1, keepdims=True) + 1e-6)
        s_row = lax.rsqrt(jnp.sum(diag, axis=0, keepdims=True) + 1e-6)
        gram = gram * (s_col * s_row)
        cross = cross * (s_row * (N ** -0.5))
        rate_row = small[8 + h : 9 + h, :]
        per = []
        for d in range(2):
            g = 4 * h + first + d
            ratio = cum[d][:, g : g + 1] - cum_t[d][g : g + 1, :]
            weight = jnp.exp(jnp.where(before[d], ratio, -jnp.inf)) * rate_row
            strict = jnp.where(eye, 0.0, weight)
            per.append((weight, strict, strict * gram, weight * cross))
        heads.append((s_col, s_row, per))
    return sums, heads


def forward(prepared, v, length):
    sums, heads = prepared
    systems = [p[2] for hd in heads for p in hd[2]]
    solved = [t.astype(BF) for t in invert(systems, length)]
    outs, errors = [], []
    for h in range(2):
        vh = v[:, h * N : (h + 1) * N]
        es = [dot(solved[2 * h + d], vh).astype(BF) for d in range(2)]
        mix = jnp.concatenate([heads[h][2][0][3].astype(BF), heads[h][2][1][3].astype(BF)], axis=1)
        outs.append(dot(mix, jnp.concatenate(es, axis=0)))
        errors += es
    return outs, solved, errors


def backward(prepared, solved, errors, q, k, small, cot, first):
    sums, heads = prepared
    i, j = iotas()
    gq, gk, gv, rowsums, colsums = [], [], [], [], []
    for h in range(2):
        lanes = slice(h * N, (h + 1) * N)
        s_col, s_row, per = heads[h]
        c, kh, qh = cot[:, lanes], k[:, lanes], q[:, lanes]
        es = errors[2 * h : 2 * h + 2]
        d_mix = dot(c, jnp.concatenate(es, axis=0), 1, 1)
        mix = jnp.concatenate([per[0][3].astype(BF), per[1][3].astype(BF)], axis=1)
        d_err = dot(mix, c, 0, 0)
        d_val = [dot(solved[2 * h + d], d_err[d * N : (d + 1) * N], 0, 0) for d in range(2)]
        d_sys = [-dot(d_val[d], es[d], 1, 1) for d in range(2)]
        d_gram, d_cross = 0.0, 0.0
        for d in range(2):
            weight, strict, system, mixing = per[d]
            dm = d_mix[:, d * N : (d + 1) * N]
            d_gram = d_gram + d_sys[d] * strict
            d_cross = d_cross + dm * weight
            total = d_sys[d] * system + dm * mixing
            rowsums.append(jnp.sum(total, axis=1, keepdims=True))
            colsums.append(jnp.sum(total, axis=0, keepdims=True))
        both = d_gram + d_gram.T
        gq.append(dot(d_cross * (s_row * (N ** -0.5)), kh))
        kf = kh.astype(F32)
        d_kn = dot(both * s_row, kh) + dot(d_cross, qh, 0, 0) * (N ** -0.5)
        along = s_col * jnp.sum(kf * d_kn, axis=1, keepdims=True)
        gk.append(s_col * (d_kn - kf * (s_col * along)))
        gv.append(d_val[0] + d_val[1])
    across = jnp.zeros((N, N), F32)
    for s in range(4):
        across = jnp.where(j == s, rowsums[s], across)
    d_cum = across.T[:8, :] - jnp.concatenate(colsums + [jnp.zeros((4, N), F32)], axis=0)
    pieces = split3(d_cum)
    gates = [sum(dot(p, sums[1 - d], 1, 1) for p in pieces) for d in range(2)]
    zero = jnp.zeros((1, N), F32)
    out = [zero] * 16
    for h in range(2):
        rate = small[8 + h : 9 + h, :]
        whole = colsums[2 * h] + colsums[2 * h + 1]
        out[8 + h] = jnp.where(rate > 0, whole / jnp.where(rate > 0, rate, 1.0), 0.0)
        for d in range(2):
            s = 2 * h + d
            out[4 * h + first + d] = gates[d][s : s + 1, :]
    out = jnp.concatenate(out, axis=0)
    return jnp.concatenate(gq, axis=1), jnp.concatenate(gk, axis=1), jnp.concatenate(gv, axis=1), out


VMEM = pl.BlockSpec(memory_space=pltpu.VMEM)
SMEM = pl.BlockSpec(memory_space=pltpu.SMEM)


def one_hot(mask):
    return jnp.where(mask, 1.0, 0.0).astype(BF)


def call(kernel, outs, args, specs=None, flops=100_000_000, name=None, scratch=(), limit=48):
    return pl.pallas_call(
        kernel,
        out_shape=[jax.ShapeDtypeStruct(shape, dtype) for shape, dtype in outs],
        in_specs=specs or [VMEM] * len(args),
        out_specs=[VMEM] * len(outs),
        scratch_shapes=list(scratch),
        compiler_params=pltpu.CompilerParams(vmem_limit_bytes=limit * 1024 * 1024),
        cost_estimate=pl.CostEstimate(flops=flops, bytes_accessed=2_000_000, transcendentals=0),
        name=name,
    )(*args)


def small_rows(info_ref, rate_ref, gate_ref):
    rows = jnp.concatenate(
        [gate_ref[...].astype(F32), rate_ref[...].astype(F32), jnp.ones((6, N), F32)], axis=0
    )
    row, patch = iotas(16, N)
    return jnp.where((patch < info_ref[0]) & (row < 11), rows, 0.0)


def shuffle(by_column, inverse):
    i, j = iotas(144, 144)
    packed, plain = (j, i) if inverse else (i, j)
    peer = shr(packed * 3641, 16)
    rest = packed - 18 * peer
    c = rest & 1
    within = 8 * c + peer if by_column else 2 * peer + c
    return one_hot(plain == 16 * shr(rest, 1) + within)


def pack(parts, small, by_column, out_ref):
    parts = [part[:, h * N : (h + 1) * N].astype(F32) for part in parts for h in range(2)]
    parts.append(jnp.concatenate([small, jnp.zeros((N - 16, N), F32)], axis=0).T)
    order = shuffle(by_column, False)
    for b in range(8):
        if by_column:
            rows = [part[start + 8 * b : start + 8 * b + 8] for part in parts for start in (0, 64)]
        else:
            rows = [part[16 * b : 16 * b + 16] for part in parts]
        out_ref[144 * b : 144 * b + 144, :] = dot(order, jnp.concatenate(rows, axis=0)).astype(BF)


def unpack(got_ref, by_column):
    order = shuffle(by_column, True)
    blocks = [dot(order, got_ref[144 * b : 144 * b + 144, :]) for b in range(8)]
    parts = []
    for s in range(9):
        if by_column:
            rows = [block[16 * s + 8 * c : 16 * s + 8 * c + 8] for c in range(2) for block in blocks]
        else:
            rows = [block[16 * s : 16 * s + 16] for block in blocks]
        parts.append(jnp.concatenate(rows, axis=0))
    return [jnp.concatenate(parts[2 * a : 2 * a + 2], axis=1) for a in range(4)], parts[8]


def pack_kernel(info_ref, rate_ref, gate_ref, q_ref, k_ref, v_ref, cot_ref, out_ref, held, sems):
    copies = [
        pltpu.make_async_copy(ref, held.at[a], sems.at[a])
        for a, ref in enumerate((q_ref, k_ref, v_ref, cot_ref))
    ]
    for copy in copies:
        copy.start()
    small = small_rows(info_ref, rate_ref, gate_ref)
    for copy in copies:
        copy.wait()
    pack([held[a] for a in range(4)], small, False, out_ref)


def row_kernel(
    info_ref, q_ref, k_ref, v_ref, rate_ref, gate_ref, cot_ref, w_ref, o_ref, gq_ref, gk_ref, gv_ref, gs_ref
):
    patch, unused = iotas(N, 2 * N)
    cot = jnp.where(patch < info_ref[0], dot(cot_ref[...], w_ref[...], 1, 1), 0.0).astype(BF)
    q, k, v = q_ref[...], k_ref[...], v_ref[...]
    small = small_rows(info_ref, rate_ref, gate_ref)
    ready = prepare(q, k, small, N, 0)
    outs, solved, errors = forward(ready, v, N)
    o_ref[...] = jnp.where(patch < info_ref[0], jnp.concatenate(outs, axis=1), 0.0)
    gq_ref[...], gk_ref[...], gv_ref[...], gs_ref[...] = backward(ready, solved, errors, q, k, small, cot, 0)


def unpack_kernel(got_ref, q_ref, k_ref, v_ref, copies_ref, small_ref, tissue_ref):
    parts, scalars = unpack(got_ref, True)
    for part, ref in zip(parts, (q_ref, k_ref, v_ref)):
        ref[...] = part.astype(BF)
    for x in range(4):
        copies_ref[x * N : (x + 1) * N, :] = parts[3].astype(BF)
    small_ref[...] = scalars.T[:16, :]
    tissue_ref[...] = jnp.broadcast_to(scalars[:, 10:11], (N, 2 * N))


def column_forward_kernel(
    q_ref, k_ref, v_ref, small_ref, tissue_ref, o_ref, weight_ref, system_ref, mixing_ref, scale_ref, t_ref, e_ref
):
    sums, heads = ready = prepare(q_ref[...], k_ref[...], small_ref[...], 64, 2)
    outs, solved, errors = forward(ready, v_ref[...], 64)
    o_ref[...] = jnp.where(tissue_ref[...] > 0.5, jnp.concatenate(outs, axis=1), 0.0).astype(BF)
    for h in range(2):
        scale_ref[h] = jnp.broadcast_to(heads[h][0], (N, N))
        for d in range(2):
            s = 2 * h + d
            weight, strict, system, mixing = heads[h][2][d]
            weight_ref[s], system_ref[s], mixing_ref[s] = weight, system, mixing
            t_ref[s], e_ref[s] = solved[s], errors[s]


def column_backward_kernel(
    q_ref, k_ref, small_ref, tissue_ref, o_ref, weight_ref, system_ref, mixing_ref, scale_ref, t_ref, e_ref,
    cot_ref, w_ref, send_ref
):
    total = 0.0
    for block in range(8):
        part = cot_ref[((block & 1) * 4 + (block >> 1)) * N : ((block & 1) * 4 + (block >> 1) + 1) * N, :]
        total = total + dot(part, w_ref[:, block * 2 * N : (block + 1) * 2 * N], 1, 1)
    cot = jnp.where(tissue_ref[...] > 0.5, total, 0.0).astype(BF)
    i, j = iotas()
    heads = []
    for h in range(2):
        scale = scale_ref[h]
        per = []
        for d in range(2):
            s = 2 * h + d
            weight = weight_ref[s]
            per.append((weight, jnp.where(i == j, 0.0, weight), system_ref[s], mixing_ref[s]))
        heads.append((scale[:, :1], jnp.sum(jnp.where(i == j, scale, 0.0), axis=0, keepdims=True), per))
    solved = [t_ref[s] for s in range(4)]
    errors = [e_ref[s] for s in range(4)]
    ready = (prefix_sums(64)[0], heads)
    gq, gk, gv, gs = backward(ready, solved, errors, q_ref[...], k_ref[...], small_ref[...], cot, 2)
    pack([o_ref[...], gq, gk, gv], gs, True, send_ref)


def weight_kernel(row_cot_ref, row_o_ref, col_cot_ref, col_o_ref, wg_ref):
    hidden = jnp.concatenate([row_o_ref[...].astype(BF), col_o_ref[...]], axis=0)
    for z in range(16):
        block, half = z >> 1, z & 1
        rows = ((block & 1) * 4 + (block >> 1)) * N
        col_cot = col_cot_ref[rows : rows + N, half * N : (half + 1) * N]
        cot = jnp.concatenate([row_cot_ref[:, z * N : (z + 1) * N], col_cot], axis=0)
        part = dot(cot, hidden, 0, 0).astype(BF)
        for y in range(4):
            start = y * 512 + z * 32
            wg_ref[start : start + 32, :] = part[y * 32 : (y + 1) * 32, :]


def projection_kernel(info_ref, w_ref, own_ref, other_ref):
    place, core = info_ref[1], info_ref[2]
    for step in range(4):
        for ref, side in ((own_ref, core), (other_ref, 1 - core)):
            block = 2 * ((place + step) & 3) + side
            lanes = pl.ds(pl.multiple_of(block * 2 * N, 2 * N), 2 * N)
            ref[step] = w_ref[:, lanes]


def gradient_kernel(
    info_ref, got_ref, o_ref, gq_ref, gk_ref, gv_ref, gs_ref, hidden_ref, q_ref, k_ref, v_ref, rate_ref, gate_ref
):
    parts, scalars = unpack(got_ref, False)
    hidden_ref[...] = (o_ref[...] + parts[0]).astype(BF)
    for part, row_ref, out_ref in zip(parts[1:], (gq_ref, gk_ref, gv_ref), (q_ref, k_ref, v_ref)):
        out_ref[...] = (row_ref[...] + part).astype(BF)
    unused, patch = iotas(16, N)
    small = jnp.where(patch < info_ref[0], gs_ref[...] + scalars.T[:16, :], 0.0)
    gate_ref[...] = small[:8, :]
    rate_ref[...] = small[8:10, :]


def encode_kernel(info_ref, hidden_ref, own_ref, swapped_ref, first_ref, second_ref, third_ref, out_ref):
    place, core = info_ref[1], info_ref[2]
    total = 0.0
    rows = [(own_ref[0], swapped_ref[0])]
    rows += [(ref[0], ref[1]) for ref in (first_ref, second_ref, third_ref)]
    for step, pair in enumerate(rows):
        for side, weights in zip((core, 1 - core), pair):
            block = 2 * ((place - step) & 3) + side
            lanes = pl.ds(pl.multiple_of(block * 2 * N, 2 * N), 2 * N)
            total = total + dot(hidden_ref[:, lanes], weights)
    out_ref[...] = total.astype(BF)


def exchange(x, axis, groups=None):
    return lax.all_to_all(x, axis, split_axis=0, concat_axis=0, tiled=True, axis_index_groups=groups)


def swap_rows(x):
    return exchange(x.reshape(64, 9, 2, N), "rows").reshape(18 * 64, N)


def per_device(
    query_proj, key_proj, value_proj, write_rate, log_gate, tissue_lengths, out_weight, cotangent
):
    q, k, v = query_proj[0], key_proj[0], value_proj[0]
    rate = write_rate[0].T
    gate = log_gate[0].transpose(1, 2, 0).reshape(8, N)
    me = lax.axis_index("heads")
    info = jnp.stack([tissue_lengths[0], lax.shift_right_logical(me, 1), me & 1])
    wide, few = (N, 2 * N), (16, N)

    (send,) = call(
        pack_kernel,
        [((18 * 64, N), BF)],
        [tissue_lengths, rate, gate, q, k, v, cotangent[0]],
        [SMEM, VMEM, VMEM] + [pl.BlockSpec(memory_space=pl.ANY)] * 4,
        name="pack",
        scratch=[pltpu.VMEM((4, N, 2 * N), BF), pltpu.SemaphoreType.DMA((4,))],
        limit=62,
    )
    got = swap_rows(send)
    row_cot = lax.all_gather(cotangent[0], "heads", axis=1, tiled=True)
    o_row, gq, gk, gv, gs = call(
        row_kernel,
        [(wide, F32)] * 4 + [(few, F32)],
        [info, q, k, v, rate, gate, row_cot, out_weight],
        [SMEM] + [VMEM] * 7,
        flops=6_000_000_000,
        name="row_directions",
    )
    qc, kc, vc, copies, sc, tissue = call(
        unpack_kernel,
        [(wide, BF)] * 3 + [((4 * N, 2 * N), BF), (few, F32), (wide, F32)],
        [got],
        name="unpack",
    )
    x_groups = [[2 * x + core for x in range(4)] for core in range(2)]
    pairs = [[2 * x, 2 * x + 1] for x in range(4)]
    along_x = exchange(copies, "heads", x_groups)
    col_cot = lax.all_gather(along_x, "heads", axis=0, tiled=True, axis_index_groups=pairs)
    four = (4, N, N)
    kept = call(
        column_forward_kernel,
        [(wide, BF)] + [(four, F32)] * 3 + [((2, N, N), F32)] + [(four, BF)] * 2,
        [qc, kc, vc, sc, tissue],
        flops=3_000_000_000,
        name="column_forward",
    )
    o_col = kept[0]
    (send,) = call(
        column_backward_kernel,
        [((18 * 64, N), BF)],
        [qc, kc, sc, tissue, *kept, col_cot, out_weight],
        flops=3_000_000_000,
        name="column_backward",
    )
    got = swap_rows(send)
    (partial_wg,) = call(
        weight_kernel,
        [((2048, 2 * N), BF)],
        [row_cot, o_row, col_cot, o_col],
        flops=2_000_000_000,
        name="weight_gradient",
    )
    y_groups = [[z * 4 + y for y in range(4)] for z in range(16)]
    z_groups = [[z * 4 + y for z in range(16)] for y in range(4)]
    summed = lax.psum_scatter(
        partial_wg, "rows", scatter_dimension=0, axis_index_groups=y_groups, tiled=True
    )
    weight, unused = lax.optimization_barrier((out_weight, send))
    block = (4, 2 * N, 2 * N)
    own, other = call(projection_kernel, [(block, BF)] * 2, [info, weight], [SMEM, VMEM], name="projection")
    swapped = lax.ppermute(other, "heads", [(i, i ^ 1) for i in range(8)])
    arrived = []
    for step in range(1, 4):
        moves = [(i, ((i // 2 + step) % 4) * 2 + i % 2) for i in range(8)]
        arrived.append(lax.ppermute(jnp.stack([own[step], swapped[step]]), "heads", moves))
    arrived, summed = lax.optimization_barrier((arrived, summed))
    hidden, grad_q, grad_k, grad_v, grad_rate, grad_gate = call(
        gradient_kernel,
        [(wide, BF)] * 4 + [((2, N), F32), ((8, N), F32)],
        [info, got, o_row, gq, gk, gv, gs],
        [SMEM] + [VMEM] * 6,
        name="gradients",
    )
    hidden = lax.all_gather(hidden, "heads", axis=1, tiled=True)
    (encoded,) = call(
        encode_kernel,
        [(wide, BF)],
        [info, hidden, own, swapped] + arrived,
        [SMEM] + [VMEM] * 6,
        flops=1_000_000_000,
        name="encode",
    )
    encoded = encoded[None]

    pieces = exchange(summed, "rows", z_groups)
    weight_grad = jnp.sum(pieces.reshape(16, 32, 2 * N).astype(F32), axis=0)
    rate_grad = grad_rate.T[None]
    gate_grad = grad_gate.reshape(2, 4, N).transpose(2, 0, 1)[None]
    return (encoded, grad_q[None], grad_k[None], grad_v[None], rate_grad, gate_grad, weight_grad)


def solution(mesh):
    in_specs = (
        P("rows", None, "heads"),
        P("rows", None, "heads"),
        P("rows", None, "heads"),
        P("rows", None, "heads"),
        P("rows", None, "heads", None),
        P("rows"),
        P("heads", None),
        P("rows", None, "heads"),
    )
    out_specs = (
        P("rows", None, "heads"),
        P("rows", None, "heads"),
        P("rows", None, "heads"),
        P("rows", None, "heads"),
        P("rows", None, "heads"),
        P("rows", None, "heads", None),
        P("rows", "heads"),
    )
    return jax.shard_map(
        per_device, mesh=mesh, in_specs=in_specs, out_specs=out_specs, check_vma=False
    )
```

```python
import functools

import jax
import jax.numpy as jnp
from jax import lax
from jax.experimental import pallas as pl
from jax.experimental.pallas import tpu as pltpu
from jax.sharding import PartitionSpec as P

N = 128
F32 = jnp.float32
BF = jnp.bfloat16


def dot(a, b, ca=1, cb=0):
    return lax.dot_general(a.astype(BF), b.astype(BF), (((ca,), (cb,)), ((), ())), preferred_element_type=F32)


def iotas(rows=N, cols=N):
    return lax.broadcasted_iota(jnp.int32, (rows, cols), 0), lax.broadcasted_iota(jnp.int32, (rows, cols), 1)


def shr(x, n):
    return lax.shift_right_logical(x, jnp.int32(n))


def invert(systems, length):
    i, j = iotas()
    apart = i ^ j
    eye = jnp.where(apart == 0, 1.0, 0.0)
    solved = [eye - jnp.where(apart == 1, a, 0.0) for a in systems]
    level = 1
    while (2 << level) <= length:
        mask = shr(apart, level) == 1
        crossing = [jnp.where(mask, a, 0.0).astype(BF) for a in systems]
        halves = [t.astype(BF) for t in solved]
        inner = [dot(c, t) for c, t in zip(crossing, halves)]
        solved = [t - dot(h, m) for t, h, m in zip(solved, halves, inner)]
        level += 1
    return solved


def split3(x):
    hi = x.astype(BF)
    rest = x - hi.astype(F32)
    mid = rest.astype(BF)
    return hi, mid, (rest - mid.astype(F32)).astype(BF)


def prefix_sums(length):
    i, j = iotas()
    shift = length.bit_length() - 1
    same = shr(i, shift) == shr(j, shift)
    before = [same & (i >= j), same & (i <= j)]
    return [jnp.where(m, 1.0, 0.0).astype(BF) for m in before], before, i == j


def prepare(q, k, small, length, first):
    sums, before, eye = prefix_sums(length)
    cum = [dot(m, small, 1, 1) for m in sums]
    cum_t = [dot(small, m, 1, 1) for m in sums]
    heads = []
    for h in range(2):
        lanes = slice(h * N, (h + 1) * N)
        kh, qh = k[:, lanes], q[:, lanes]
        gram = dot(kh, kh, 1, 1)
        cross = dot(qh, kh, 1, 1)
        diag = jnp.where(eye, gram, 0.0)
        s_col = lax.rsqrt(jnp.sum(diag, axis=1, keepdims=True) + 1e-6)
        s_row = lax.rsqrt(jnp.sum(diag, axis=0, keepdims=True) + 1e-6)
        gram = gram * (s_col * s_row)
        cross = cross * (s_row * (N ** -0.5))
        rate_row = small[8 + h : 9 + h, :]
        per = []
        for d in range(2):
            g = 4 * h + first + d
            ratio = cum[d][:, g : g + 1] - cum_t[d][g : g + 1, :]
            weight = jnp.exp(jnp.where(before[d], ratio, -jnp.inf)) * rate_row
            strict = jnp.where(eye, 0.0, weight)
            per.append((weight, strict, strict * gram, weight * cross))
        heads.append((s_col, s_row, per))
    return sums, heads


def forward(prepared, v, length):
    sums, heads = prepared
    systems = [p[2] for hd in heads for p in hd[2]]
    solved = [t.astype(BF) for t in invert(systems, length)]
    outs, errors = [], []
    for h in range(2):
        vh = v[:, h * N : (h + 1) * N]
        es = [dot(solved[2 * h + d], vh).astype(BF) for d in range(2)]
        mix = jnp.concatenate([heads[h][2][0][3].astype(BF), heads[h][2][1][3].astype(BF)], axis=1)
        outs.append(dot(mix, jnp.concatenate(es, axis=0)))
        errors += es
    return outs, solved, errors


def backward(prepared, solved, errors, q, k, small, cot, first):
    sums, heads = prepared
    i, j = iotas()
    gq, gk, gv, rowsums, colsums = [], [], [], [], []
    for h in range(2):
        lanes = slice(h * N, (h + 1) * N)
        s_col, s_row, per = heads[h]
        c, kh, qh = cot[:, lanes], k[:, lanes], q[:, lanes]
        es = errors[2 * h : 2 * h + 2]
        d_mix = dot(c, jnp.concatenate(es, axis=0), 1, 1)
        mix = jnp.concatenate([per[0][3].astype(BF), per[1][3].astype(BF)], axis=1)
        d_err = dot(mix, c, 0, 0)
        d_val = [dot(solved[2 * h + d], d_err[d * N : (d + 1) * N], 0, 0) for d in range(2)]
        d_sys = [-dot(d_val[d], es[d], 1, 1) for d in range(2)]
        d_gram, d_cross = 0.0, 0.0
        for d in range(2):
            weight, strict, system, mixing = per[d]
            dm = d_mix[:, d * N : (d + 1) * N]
            d_gram = d_gram + d_sys[d] * strict
            d_cross = d_cross + dm * weight
            total = d_sys[d] * system + dm * mixing
            rowsums.append(jnp.sum(total, axis=1, keepdims=True))
            colsums.append(jnp.sum(total, axis=0, keepdims=True))
        both = d_gram + d_gram.T
        gq.append(dot(d_cross * (s_row * (N ** -0.5)), kh))
        kf = kh.astype(F32)
        d_kn = dot(both * s_row, kh) + dot(d_cross, qh, 0, 0) * (N ** -0.5)
        along = s_col * jnp.sum(kf * d_kn, axis=1, keepdims=True)
        gk.append(s_col * (d_kn - kf * (s_col * along)))
        gv.append(d_val[0] + d_val[1])
    across = jnp.zeros((N, N), F32)
    for s in range(4):
        across = jnp.where(j == s, rowsums[s], across)
    d_cum = across.T[:8, :] - jnp.concatenate(colsums + [jnp.zeros((4, N), F32)], axis=0)
    pieces = split3(d_cum)
    gates = [sum(dot(p, sums[1 - d], 1, 1) for p in pieces) for d in range(2)]
    zero = jnp.zeros((1, N), F32)
    out = [zero] * 16
    for h in range(2):
        rate = small[8 + h : 9 + h, :]
        whole = colsums[2 * h] + colsums[2 * h + 1]
        out[8 + h] = jnp.where(rate > 0, whole / jnp.where(rate > 0, rate, 1.0), 0.0)
        for d in range(2):
            s = 2 * h + d
            out[4 * h + first + d] = gates[d][s : s + 1, :]
    out = jnp.concatenate(out, axis=0)
    return jnp.concatenate(gq, axis=1), jnp.concatenate(gk, axis=1), jnp.concatenate(gv, axis=1), out


VMEM = pl.BlockSpec(memory_space=pltpu.VMEM)
SMEM = pl.BlockSpec(memory_space=pltpu.SMEM)


def one_hot(mask):
    return jnp.where(mask, 1.0, 0.0).astype(BF)


def call(kernel, outs, args, specs=None, flops=100_000_000, name=None, scratch=(), limit=48):
    return pl.pallas_call(
        kernel,
        out_shape=[jax.ShapeDtypeStruct(shape, dtype) for shape, dtype in outs],
        in_specs=specs or [VMEM] * len(args),
        out_specs=[VMEM] * len(outs),
        scratch_shapes=list(scratch),
        compiler_params=pltpu.CompilerParams(vmem_limit_bytes=limit * 1024 * 1024),
        cost_estimate=pl.CostEstimate(flops=flops, bytes_accessed=2_000_000, transcendentals=0),
        name=name,
    )(*args)


def small_rows(info_ref, rate_ref, gate_ref):
    rows = jnp.concatenate(
        [gate_ref[...].astype(F32), rate_ref[...].astype(F32), jnp.ones((6, N), F32)], axis=0
    )
    row, patch = iotas(16, N)
    return jnp.where((patch < info_ref[0]) & (row < 11), rows, 0.0)


def shuffle(by_column, inverse):
    i, j = iotas(144, 144)
    packed, plain = (j, i) if inverse else (i, j)
    peer = shr(packed * 3641, 16)
    rest = packed - 18 * peer
    c = rest & 1
    within = 8 * c + peer if by_column else 2 * peer + c
    return one_hot(plain == 16 * shr(rest, 1) + within)


def pack(parts, small, by_column, out_ref):
    parts = [part[:, h * N : (h + 1) * N].astype(F32) for part in parts for h in range(2)]
    parts.append(jnp.concatenate([small, jnp.zeros((N - 16, N), F32)], axis=0).T)
    order = shuffle(by_column, False)
    for b in range(8):
        if by_column:
            rows = [part[start + 8 * b : start + 8 * b + 8] for part in parts for start in (0, 64)]
        else:
            rows = [part[16 * b : 16 * b + 16] for part in parts]
        out_ref[144 * b : 144 * b + 144, :] = dot(order, jnp.concatenate(rows, axis=0)).astype(BF)


def unpack(got_ref, by_column):
    order = shuffle(by_column, True)
    blocks = [dot(order, got_ref[144 * b : 144 * b + 144, :]) for b in range(8)]
    parts = []
    for s in range(9):
        if by_column:
            rows = [block[16 * s + 8 * c : 16 * s + 8 * c + 8] for c in range(2) for block in blocks]
        else:
            rows = [block[16 * s : 16 * s + 16] for block in blocks]
        parts.append(jnp.concatenate(rows, axis=0))
    return [jnp.concatenate(parts[2 * a : 2 * a + 2], axis=1) for a in range(4)], parts[8]


def pack_kernel(info_ref, rate_ref, gate_ref, q_ref, k_ref, v_ref, cot_ref, out_ref, held, sems):
    copies = [
        pltpu.make_async_copy(ref, held.at[a], sems.at[a])
        for a, ref in enumerate((q_ref, k_ref, v_ref, cot_ref))
    ]
    for copy in copies:
        copy.start()
    small = small_rows(info_ref, rate_ref, gate_ref)
    for copy in copies:
        copy.wait()
    pack([held[a] for a in range(4)], small, False, out_ref)


def row_kernel(
    info_ref, q_ref, k_ref, v_ref, rate_ref, gate_ref, cot_ref, w_ref, o_ref, gq_ref, gk_ref, gv_ref, gs_ref
):
    patch, unused = iotas(N, 2 * N)
    cot = jnp.where(patch < info_ref[0], dot(cot_ref[...], w_ref[...], 1, 1), 0.0).astype(BF)
    q, k, v = q_ref[...], k_ref[...], v_ref[...]
    small = small_rows(info_ref, rate_ref, gate_ref)
    ready = prepare(q, k, small, N, 0)
    outs, solved, errors = forward(ready, v, N)
    o_ref[...] = jnp.where(patch < info_ref[0], jnp.concatenate(outs, axis=1), 0.0)
    gq_ref[...], gk_ref[...], gv_ref[...], gs_ref[...] = backward(ready, solved, errors, q, k, small, cot, 0)


def unpack_kernel(got_ref, q_ref, k_ref, v_ref, copies_ref, small_ref):
    parts, scalars = unpack(got_ref, True)
    for part, ref in zip(parts, (q_ref, k_ref, v_ref)):
        ref[...] = part.astype(BF)
    for x in range(4):
        copies_ref[x * N : (x + 1) * N, :] = parts[3].astype(BF)
    small_ref[...] = scalars.T[:16, :]


def tissue_of(small):
    return jnp.concatenate([small, jnp.zeros((N - 16, N), F32)], axis=0).T[:, 10:11] > 0.5


def column_forward_kernel(q_ref, k_ref, v_ref, small_ref, o_ref, t_ref, e_ref):
    small = small_ref[...]
    outs, solved, errors = forward(prepare(q_ref[...], k_ref[...], small, 64, 2), v_ref[...], 64)
    o_ref[...] = jnp.where(tissue_of(small), jnp.concatenate(outs, axis=1), 0.0).astype(BF)
    for s in range(4):
        t_ref[s], e_ref[s] = solved[s], errors[s]


def column_backward_kernel(q_ref, k_ref, small_ref, o_ref, t_ref, e_ref, cot_ref, w_ref, send_ref):
    total = 0.0
    for block in range(8):
        rows = ((block & 1) * 4 + (block >> 1)) * N
        total = total + dot(cot_ref[rows : rows + N, :], w_ref[:, block * 2 * N : (block + 1) * 2 * N], 1, 1)
    q, k, small = q_ref[...], k_ref[...], small_ref[...]
    cot = jnp.where(tissue_of(small), total, 0.0).astype(BF)
    solved = [t_ref[s] for s in range(4)]
    errors = [e_ref[s] for s in range(4)]
    gq, gk, gv, gs = backward(prepare(q, k, small, 64, 2), solved, errors, q, k, small, cot, 2)
    pack([o_ref[...], gq, gk, gv], gs, True, send_ref)


def weight_kernel(row_cot_ref, row_o_ref, col_cot_ref, col_o_ref, wg_ref):
    hidden = jnp.concatenate([row_o_ref[...].astype(BF), col_o_ref[...]], axis=0)
    for z in range(16):
        block, half = z >> 1, z & 1
        rows = ((block & 1) * 4 + (block >> 1)) * N
        col_cot = col_cot_ref[rows : rows + N, half * N : (half + 1) * N]
        cot = jnp.concatenate([row_cot_ref[:, z * N : (z + 1) * N], col_cot], axis=0)
        part = dot(cot, hidden, 0, 0).astype(BF)
        for y in range(4):
            start = y * 512 + z * 32
            wg_ref[start : start + 32, :] = part[y * 32 : (y + 1) * 32, :]


def projection_kernel(info_ref, w_ref, own_ref, other_ref):
    place, core = info_ref[1], info_ref[2]
    for step in range(4):
        for ref, side in ((own_ref, core), (other_ref, 1 - core)):
            block = 2 * ((place + step) & 3) + side
            lanes = pl.ds(pl.multiple_of(block * 2 * N, 2 * N), 2 * N)
            ref[step] = w_ref[:, lanes]


def gradient_kernel(
    info_ref, got_ref, o_ref, gq_ref, gk_ref, gv_ref, gs_ref, hidden_ref, q_ref, k_ref, v_ref, rate_ref, gate_ref
):
    parts, scalars = unpack(got_ref, False)
    hidden_ref[...] = (o_ref[...] + parts[0]).astype(BF)
    for part, row_ref, out_ref in zip(parts[1:], (gq_ref, gk_ref, gv_ref), (q_ref, k_ref, v_ref)):
        out_ref[...] = (row_ref[...] + part).astype(BF)
    unused, patch = iotas(16, N)
    small = jnp.where(patch < info_ref[0], gs_ref[...] + scalars.T[:16, :], 0.0)
    gate_ref[...] = small[:8, :]
    rate_ref[...] = small[8:10, :]


def encode_kernel(info_ref, hidden_ref, own_ref, swapped_ref, first_ref, second_ref, third_ref, out_ref):
    place, core = info_ref[1], info_ref[2]
    total = 0.0
    rows = [(own_ref[0], swapped_ref[0])]
    rows += [(ref[0], ref[1]) for ref in (first_ref, second_ref, third_ref)]
    for step, pair in enumerate(rows):
        for side, weights in zip((core, 1 - core), pair):
            block = 2 * ((place - step) & 3) + side
            lanes = pl.ds(pl.multiple_of(block * 2 * N, 2 * N), 2 * N)
            total = total + dot(hidden_ref[:, lanes], weights)
    out_ref[...] = total.astype(BF)


def exchange(x, axis, groups=None):
    return lax.all_to_all(x, axis, split_axis=0, concat_axis=0, tiled=True, axis_index_groups=groups)


def swap_rows(x):
    return exchange(x.reshape(64, 9, 2, N), "rows").reshape(18 * 64, N)


def per_device(
    query_proj, key_proj, value_proj, write_rate, log_gate, tissue_lengths, out_weight, cotangent
):
    q, k, v = query_proj[0], key_proj[0], value_proj[0]
    rate = write_rate[0].T
    gate = log_gate[0].transpose(1, 2, 0).reshape(8, N)
    me = lax.axis_index("heads")
    info = jnp.stack([tissue_lengths[0], lax.shift_right_logical(me, 1), me & 1])
    wide, few = (N, 2 * N), (16, N)

    (send,) = call(
        pack_kernel,
        [((18 * 64, N), BF)],
        [tissue_lengths, rate, gate, q, k, v, cotangent[0]],
        [SMEM, VMEM, VMEM] + [pl.BlockSpec(memory_space=pl.ANY)] * 4,
        name="pack",
        scratch=[pltpu.VMEM((4, N, 2 * N), BF), pltpu.SemaphoreType.DMA((4,))],
        limit=62,
    )
    got = swap_rows(send)
    row_cot = lax.all_gather(cotangent[0], "heads", axis=1, tiled=True)
    o_row, gq, gk, gv, gs = call(
        row_kernel,
        [(wide, F32)] * 4 + [(few, F32)],
        [info, q, k, v, rate, gate, row_cot, out_weight],
        [SMEM] + [VMEM] * 7,
        flops=6_000_000_000,
        name="row_directions",
    )
    qc, kc, vc, copies, sc = call(
        unpack_kernel,
        [(wide, BF)] * 3 + [((4 * N, 2 * N), BF), (few, F32)],
        [got],
        name="unpack",
    )
    x_groups = [[2 * x + core for x in range(4)] for core in range(2)]
    pairs = [[2 * x, 2 * x + 1] for x in range(4)]
    along_x = exchange(copies, "heads", x_groups)
    col_cot = lax.all_gather(along_x, "heads", axis=0, tiled=True, axis_index_groups=pairs)
    o_col, tc, ec = call(
        column_forward_kernel,
        [(wide, BF)] + [((4, N, N), BF)] * 2,
        [qc, kc, vc, sc],
        flops=3_000_000_000,
        name="column_forward",
    )
    (send,) = call(
        column_backward_kernel,
        [((18 * 64, N), BF)],
        [qc, kc, sc, o_col, tc, ec, col_cot, out_weight],
        flops=3_000_000_000,
        name="column_backward",
    )
    got = swap_rows(send)
    (partial_wg,) = call(
        weight_kernel,
        [((2048, 2 * N), BF)],
        [row_cot, o_row, col_cot, o_col],
        flops=2_000_000_000,
        name="weight_gradient",
    )
    y_groups = [[z * 4 + y for y in range(4)] for z in range(16)]
    z_groups = [[z * 4 + y for z in range(16)] for y in range(4)]
    summed = lax.psum_scatter(
        partial_wg, "rows", scatter_dimension=0, axis_index_groups=y_groups, tiled=True
    )
    weight, unused = lax.optimization_barrier((out_weight, sc))
    block = (4, 2 * N, 2 * N)
    own, other = call(projection_kernel, [(block, BF)] * 2, [info, weight], [SMEM, VMEM], name="projection")
    swapped = lax.ppermute(other, "heads", [(i, i ^ 1) for i in range(8)])
    arrived = []
    for step in range(1, 4):
        moves = [(i, ((i // 2 + step) % 4) * 2 + i % 2) for i in range(8)]
        arrived.append(lax.ppermute(jnp.stack([own[step], swapped[step]]), "heads", moves))
    arrived, summed = lax.optimization_barrier((arrived, summed))
    hidden, grad_q, grad_k, grad_v, grad_rate, grad_gate = call(
        gradient_kernel,
        [(wide, BF)] * 4 + [((2, N), F32), ((8, N), F32)],
        [info, got, o_row, gq, gk, gv, gs],
        [SMEM] + [VMEM] * 6,
        name="gradients",
    )
    hidden = lax.all_gather(hidden, "heads", axis=1, tiled=True)
    (encoded,) = call(
        encode_kernel,
        [(wide, BF)],
        [info, hidden, own, swapped] + arrived,
        [SMEM] + [VMEM] * 6,
        flops=1_000_000_000,
        name="encode",
    )
    encoded = encoded[None]

    pieces = exchange(summed, "rows", z_groups)
    weight_grad = jnp.sum(pieces.reshape(16, 32, 2 * N).astype(F32), axis=0)
    rate_grad = grad_rate.T[None]
    gate_grad = grad_gate.reshape(2, 4, N).transpose(2, 0, 1)[None]
    return (encoded, grad_q[None], grad_k[None], grad_v[None], rate_grad, gate_grad, weight_grad)


def solution(mesh):
    in_specs = (
        P("rows", None, "heads"),
        P("rows", None, "heads"),
        P("rows", None, "heads"),
        P("rows", None, "heads"),
        P("rows", None, "heads", None),
        P("rows"),
        P("heads", None),
        P("rows", None, "heads"),
    )
    out_specs = (
        P("rows", None, "heads"),
        P("rows", None, "heads"),
        P("rows", None, "heads"),
        P("rows", None, "heads"),
        P("rows", None, "heads"),
        P("rows", None, "heads", None),
        P("rows", "heads"),
    )
    return jax.shard_map(
        per_device, mesh=mesh, in_specs=in_specs, out_specs=out_specs, check_vma=False
    )
```

```python
import functools

import jax
import jax.numpy as jnp
from jax import lax
from jax.experimental import pallas as pl
from jax.experimental.pallas import tpu as pltpu
from jax.sharding import PartitionSpec as P

N = 128
F32 = jnp.float32
BF = jnp.bfloat16


def dot(a, b, ca=1, cb=0):
    return lax.dot_general(a.astype(BF), b.astype(BF), (((ca,), (cb,)), ((), ())), preferred_element_type=F32)


def iotas(rows=N, cols=N):
    return lax.broadcasted_iota(jnp.int32, (rows, cols), 0), lax.broadcasted_iota(jnp.int32, (rows, cols), 1)


def shr(x, n):
    return lax.shift_right_logical(x, jnp.int32(n))


def invert(systems, length):
    i, j = iotas()
    apart = i ^ j
    eye = jnp.where(apart == 0, 1.0, 0.0)
    solved = [eye - jnp.where(apart == 1, a, 0.0) for a in systems]
    level = 1
    while (2 << level) <= length:
        mask = shr(apart, level) == 1
        crossing = [jnp.where(mask, a, 0.0).astype(BF) for a in systems]
        halves = [t.astype(BF) for t in solved]
        inner = [dot(c, t) for c, t in zip(crossing, halves)]
        solved = [t - dot(h, m) for t, h, m in zip(solved, halves, inner)]
        level += 1
    return solved


def split3(x):
    hi = x.astype(BF)
    rest = x - hi.astype(F32)
    mid = rest.astype(BF)
    return hi, mid, (rest - mid.astype(F32)).astype(BF)


def prefix_sums(length):
    i, j = iotas()
    shift = length.bit_length() - 1
    same = shr(i, shift) == shr(j, shift)
    before = [same & (i >= j), same & (i <= j)]
    return [jnp.where(m, 1.0, 0.0).astype(BF) for m in before], before, i == j


def prepare(q, k, small, length, first):
    sums, before, eye = prefix_sums(length)
    cum = [dot(m, small, 1, 1) for m in sums]
    cum_t = [dot(small, m, 1, 1) for m in sums]
    heads = []
    for h in range(2):
        lanes = slice(h * N, (h + 1) * N)
        kh, qh = k[:, lanes], q[:, lanes]
        gram = dot(kh, kh, 1, 1)
        cross = dot(qh, kh, 1, 1)
        diag = jnp.where(eye, gram, 0.0)
        s_col = lax.rsqrt(jnp.sum(diag, axis=1, keepdims=True) + 1e-6)
        s_row = lax.rsqrt(jnp.sum(diag, axis=0, keepdims=True) + 1e-6)
        gram = gram * (s_col * s_row)
        cross = cross * (s_row * (N ** -0.5))
        rate_row = small[8 + h : 9 + h, :]
        per = []
        for d in range(2):
            g = 4 * h + first + d
            ratio = cum[d][:, g : g + 1] - cum_t[d][g : g + 1, :]
            weight = jnp.exp(jnp.where(before[d], ratio, -jnp.inf)) * rate_row
            strict = jnp.where(eye, 0.0, weight)
            per.append((weight, strict, strict * gram, weight * cross))
        heads.append((s_col, s_row, per))
    return sums, heads


def forward(prepared, v, length):
    sums, heads = prepared
    systems = [p[2] for hd in heads for p in hd[2]]
    solved = [t.astype(BF) for t in invert(systems, length)]
    outs, errors = [], []
    for h in range(2):
        vh = v[:, h * N : (h + 1) * N]
        es = [dot(solved[2 * h + d], vh).astype(BF) for d in range(2)]
        mix = jnp.concatenate([heads[h][2][0][3].astype(BF), heads[h][2][1][3].astype(BF)], axis=1)
        outs.append(dot(mix, jnp.concatenate(es, axis=0)))
        errors += es
    return outs, solved, errors


def backward(prepared, solved, errors, q, k, small, cot, first):
    sums, heads = prepared
    i, j = iotas()
    gq, gk, gv, rowsums, colsums = [], [], [], [], []
    for h in range(2):
        lanes = slice(h * N, (h + 1) * N)
        s_col, s_row, per = heads[h]
        c, kh, qh = cot[:, lanes], k[:, lanes], q[:, lanes]
        es = errors[2 * h : 2 * h + 2]
        d_mix = dot(c, jnp.concatenate(es, axis=0), 1, 1)
        mix = jnp.concatenate([per[0][3].astype(BF), per[1][3].astype(BF)], axis=1)
        d_err = dot(mix, c, 0, 0)
        d_val = [dot(solved[2 * h + d], d_err[d * N : (d + 1) * N], 0, 0) for d in range(2)]
        d_sys = [-dot(d_val[d], es[d], 1, 1) for d in range(2)]
        d_gram, d_cross = 0.0, 0.0
        for d in range(2):
            weight, strict, system, mixing = per[d]
            dm = d_mix[:, d * N : (d + 1) * N]
            d_gram = d_gram + d_sys[d] * strict
            d_cross = d_cross + dm * weight
            total = d_sys[d] * system + dm * mixing
            rowsums.append(jnp.sum(total, axis=1, keepdims=True))
            colsums.append(jnp.sum(total, axis=0, keepdims=True))
        both = d_gram + d_gram.T
        gq.append(dot(d_cross * (s_row * (N ** -0.5)), kh))
        kf = kh.astype(F32)
        d_kn = dot(both * s_row, kh) + dot(d_cross, qh, 0, 0) * (N ** -0.5)
        along = s_col * jnp.sum(kf * d_kn, axis=1, keepdims=True)
        gk.append(s_col * (d_kn - kf * (s_col * along)))
        gv.append(d_val[0] + d_val[1])
    across = jnp.zeros((N, N), F32)
    for s in range(4):
        across = jnp.where(j == s, rowsums[s], across)
    d_cum = across.T[:8, :] - jnp.concatenate(colsums + [jnp.zeros((4, N), F32)], axis=0)
    pieces = split3(d_cum)
    gates = [sum(dot(p, sums[1 - d], 1, 1) for p in pieces) for d in range(2)]
    zero = jnp.zeros((1, N), F32)
    out = [zero] * 16
    for h in range(2):
        rate = small[8 + h : 9 + h, :]
        whole = colsums[2 * h] + colsums[2 * h + 1]
        out[8 + h] = jnp.where(rate > 0, whole / jnp.where(rate > 0, rate, 1.0), 0.0)
        for d in range(2):
            s = 2 * h + d
            out[4 * h + first + d] = gates[d][s : s + 1, :]
    out = jnp.concatenate(out, axis=0)
    return jnp.concatenate(gq, axis=1), jnp.concatenate(gk, axis=1), jnp.concatenate(gv, axis=1), out


VMEM = pl.BlockSpec(memory_space=pltpu.VMEM)
SMEM = pl.BlockSpec(memory_space=pltpu.SMEM)


def one_hot(mask):
    return jnp.where(mask, 1.0, 0.0).astype(BF)


def call(kernel, outs, args, specs=None, flops=100_000_000, name=None, scratch=(), limit=48):
    return pl.pallas_call(
        kernel,
        out_shape=[jax.ShapeDtypeStruct(shape, dtype) for shape, dtype in outs],
        in_specs=specs or [VMEM] * len(args),
        out_specs=[VMEM] * len(outs),
        scratch_shapes=list(scratch),
        compiler_params=pltpu.CompilerParams(vmem_limit_bytes=limit * 1024 * 1024),
        cost_estimate=pl.CostEstimate(flops=flops, bytes_accessed=2_000_000, transcendentals=0),
        name=name,
    )(*args)


def small_rows(info_ref, rate_ref, gate_ref):
    rows = jnp.concatenate(
        [gate_ref[...].astype(F32), rate_ref[...].astype(F32), jnp.ones((6, N), F32)], axis=0
    )
    row, patch = iotas(16, N)
    return jnp.where((patch < info_ref[0]) & (row < 11), rows, 0.0)


def shuffle(by_column, inverse):
    i, j = iotas(144, 144)
    packed, plain = (j, i) if inverse else (i, j)
    peer = shr(packed * 3641, 16)
    rest = packed - 18 * peer
    c = rest & 1
    within = 8 * c + peer if by_column else 2 * peer + c
    return one_hot(plain == 16 * shr(rest, 1) + within)


def pack(parts, small, by_column, out_ref):
    parts = [part[:, h * N : (h + 1) * N].astype(F32) for part in parts for h in range(2)]
    parts.append(jnp.concatenate([small, jnp.zeros((N - 16, N), F32)], axis=0).T)
    order = shuffle(by_column, False)
    for b in range(8):
        if by_column:
            rows = [part[start + 8 * b : start + 8 * b + 8] for part in parts for start in (0, 64)]
        else:
            rows = [part[16 * b : 16 * b + 16] for part in parts]
        out_ref[144 * b : 144 * b + 144, :] = dot(order, jnp.concatenate(rows, axis=0)).astype(BF)


def unpack(got_ref, by_column, first=0, last=9):
    order = shuffle(by_column, True)[16 * first : 16 * last]
    blocks = [dot(order, got_ref[144 * b : 144 * b + 144, :]) for b in range(8)]
    parts = []
    for s in range(last - first):
        if by_column:
            rows = [block[16 * s + 8 * c : 16 * s + 8 * c + 8] for c in range(2) for block in blocks]
        else:
            rows = [block[16 * s : 16 * s + 16] for block in blocks]
        parts.append(jnp.concatenate(rows, axis=0))
    return parts


def heads_of(parts):
    return [jnp.concatenate(parts[2 * a : 2 * a + 2], axis=1) for a in range(len(parts) // 2)]


def pack_kernel(info_ref, rate_ref, gate_ref, q_ref, k_ref, v_ref, cot_ref, out_ref, held, sems):
    copies = [
        pltpu.make_async_copy(ref, held.at[a], sems.at[a])
        for a, ref in enumerate((q_ref, k_ref, v_ref, cot_ref))
    ]
    for copy in copies:
        copy.start()
    small = small_rows(info_ref, rate_ref, gate_ref)
    for copy in copies:
        copy.wait()
    pack([held[a] for a in range(4)], small, False, out_ref)


def row_kernel(
    info_ref, q_ref, k_ref, v_ref, rate_ref, gate_ref, cot_ref, w_ref, o_ref, gq_ref, gk_ref, gv_ref, gs_ref
):
    patch, unused = iotas(N, 2 * N)
    cot = jnp.where(patch < info_ref[0], dot(cot_ref[...], w_ref[...], 1, 1), 0.0).astype(BF)
    q, k, v = q_ref[...], k_ref[...], v_ref[...]
    small = small_rows(info_ref, rate_ref, gate_ref)
    ready = prepare(q, k, small, N, 0)
    outs, solved, errors = forward(ready, v, N)
    o_ref[...] = jnp.where(patch < info_ref[0], jnp.concatenate(outs, axis=1), 0.0)
    gq_ref[...], gk_ref[...], gv_ref[...], gs_ref[...] = backward(ready, solved, errors, q, k, small, cot, 0)


def unpack_kernel(got_ref, q_ref, k_ref, v_ref, copies_ref, small_ref):
    pieces = unpack(got_ref, True)
    parts, scalars = heads_of(pieces), pieces[8]
    for part, ref in zip(parts, (q_ref, k_ref, v_ref)):
        ref[...] = part.astype(BF)
    for x in range(4):
        copies_ref[x * N : (x + 1) * N, :] = parts[3].astype(BF)
    small_ref[...] = scalars.T[:16, :]


def tissue_of(small):
    return jnp.concatenate([small, jnp.zeros((N - 16, N), F32)], axis=0).T[:, 10:11] > 0.5


def column_forward_kernel(q_ref, k_ref, v_ref, small_ref, o_ref, t_ref, e_ref):
    small = small_ref[...]
    outs, solved, errors = forward(prepare(q_ref[...], k_ref[...], small, 64, 2), v_ref[...], 64)
    o_ref[...] = jnp.where(tissue_of(small), jnp.concatenate(outs, axis=1), 0.0).astype(BF)
    for s in range(4):
        t_ref[s], e_ref[s] = solved[s], errors[s]


def column_backward_kernel(q_ref, k_ref, small_ref, o_ref, t_ref, e_ref, cot_ref, w_ref, send_ref):
    total = 0.0
    for block in range(8):
        rows = ((block & 1) * 4 + (block >> 1)) * N
        total = total + dot(cot_ref[rows : rows + N, :], w_ref[:, block * 2 * N : (block + 1) * 2 * N], 1, 1)
    q, k, small = q_ref[...], k_ref[...], small_ref[...]
    cot = jnp.where(tissue_of(small), total, 0.0).astype(BF)
    solved = [t_ref[s] for s in range(4)]
    errors = [e_ref[s] for s in range(4)]
    gq, gk, gv, gs = backward(prepare(q, k, small, 64, 2), solved, errors, q, k, small, cot, 2)
    pack([o_ref[...], gq, gk, gv], gs, True, send_ref)


def weight_kernel(row_cot_ref, row_o_ref, col_cot_ref, col_o_ref, wg_ref):
    hidden = jnp.concatenate([row_o_ref[...].astype(BF), col_o_ref[...]], axis=0)
    for z in range(16):
        block, half = z >> 1, z & 1
        rows = ((block & 1) * 4 + (block >> 1)) * N
        col_cot = col_cot_ref[rows : rows + N, half * N : (half + 1) * N]
        cot = jnp.concatenate([row_cot_ref[:, z * N : (z + 1) * N], col_cot], axis=0)
        part = dot(cot, hidden, 0, 0).astype(BF)
        for y in range(4):
            start = y * 512 + z * 32
            wg_ref[start : start + 32, :] = part[y * 32 : (y + 1) * 32, :]


def projection_kernel(info_ref, w_ref, own_ref, other_ref):
    place, core = info_ref[1], info_ref[2]
    for step in range(4):
        for ref, side in ((own_ref, core), (other_ref, 1 - core)):
            block = 2 * ((place + step) & 3) + side
            lanes = pl.ds(pl.multiple_of(block * 2 * N, 2 * N), 2 * N)
            ref[step] = w_ref[:, lanes]


def hidden_kernel(got_ref, o_ref, hidden_ref):
    (col,) = heads_of(unpack(got_ref, False, 0, 2))
    hidden_ref[...] = (o_ref[...] + col).astype(BF)


def gradient_kernel(
    info_ref, got_ref, gq_ref, gk_ref, gv_ref, gs_ref, q_ref, k_ref, v_ref, rate_ref, gate_ref
):
    pieces = unpack(got_ref, False, 2, 9)
    parts, scalars = heads_of(pieces), pieces[6]
    for part, row_ref, out_ref in zip(parts, (gq_ref, gk_ref, gv_ref), (q_ref, k_ref, v_ref)):
        out_ref[...] = (row_ref[...] + part).astype(BF)
    unused, patch = iotas(16, N)
    small = jnp.where(patch < info_ref[0], gs_ref[...] + scalars.T[:16, :], 0.0)
    gate_ref[...] = small[:8, :]
    rate_ref[...] = small[8:10, :]


def encode_kernel(info_ref, hidden_ref, own_ref, swapped_ref, kept_ref, sent_ref):
    core = info_ref[2]
    mine = hidden_ref[pl.ds(pl.multiple_of(core * N, N), N), :]
    other = hidden_ref[pl.ds(pl.multiple_of((1 - core) * N, N), N), :]
    for step in range(4):
        part = dot(mine, own_ref[step]) + dot(other, swapped_ref[step])
        if step == 0:
            kept_ref[...] = part
        else:
            sent_ref[step - 1] = part.astype(BF)


def exchange(x, axis, groups=None):
    return lax.all_to_all(x, axis, split_axis=0, concat_axis=0, tiled=True, axis_index_groups=groups)


def swap_rows(x):
    return exchange(x.reshape(64, 9, 2, N), "rows").reshape(18 * 64, N)


def per_device(
    query_proj, key_proj, value_proj, write_rate, log_gate, tissue_lengths, out_weight, cotangent
):
    q, k, v = query_proj[0], key_proj[0], value_proj[0]
    rate = write_rate[0].T
    gate = log_gate[0].transpose(1, 2, 0).reshape(8, N)
    me = lax.axis_index("heads")
    info = jnp.stack([tissue_lengths[0], lax.shift_right_logical(me, 1), me & 1])
    wide, few = (N, 2 * N), (16, N)

    (send,) = call(
        pack_kernel,
        [((18 * 64, N), BF)],
        [tissue_lengths, rate, gate, q, k, v, cotangent[0]],
        [SMEM, VMEM, VMEM] + [pl.BlockSpec(memory_space=pl.ANY)] * 4,
        name="pack",
        scratch=[pltpu.VMEM((4, N, 2 * N), BF), pltpu.SemaphoreType.DMA((4,))],
        limit=62,
    )
    got = swap_rows(send)
    row_cot = lax.all_gather(cotangent[0], "heads", axis=1, tiled=True)
    o_row, gq, gk, gv, gs = call(
        row_kernel,
        [(wide, F32)] * 4 + [(few, F32)],
        [info, q, k, v, rate, gate, row_cot, out_weight],
        [SMEM] + [VMEM] * 7,
        flops=6_000_000_000,
        name="row_directions",
    )
    qc, kc, vc, copies, sc = call(
        unpack_kernel,
        [(wide, BF)] * 3 + [((4 * N, 2 * N), BF), (few, F32)],
        [got],
        name="unpack",
    )
    x_groups = [[2 * x + core for x in range(4)] for core in range(2)]
    pairs = [[2 * x, 2 * x + 1] for x in range(4)]
    along_x = exchange(copies, "heads", x_groups)
    col_cot = lax.all_gather(along_x, "heads", axis=0, tiled=True, axis_index_groups=pairs)
    o_col, tc, ec = call(
        column_forward_kernel,
        [(wide, BF)] + [((4, N, N), BF)] * 2,
        [qc, kc, vc, sc],
        flops=3_000_000_000,
        name="column_forward",
    )
    (send,) = call(
        column_backward_kernel,
        [((18 * 64, N), BF)],
        [qc, kc, sc, o_col, tc, ec, col_cot, out_weight],
        flops=3_000_000_000,
        name="column_backward",
    )
    got = swap_rows(send)
    (partial_wg,) = call(
        weight_kernel,
        [((2048, 2 * N), BF)],
        [row_cot, o_row, col_cot, o_col],
        flops=2_000_000_000,
        name="weight_gradient",
    )
    y_groups = [[z * 4 + y for y in range(4)] for z in range(16)]
    z_groups = [[z * 4 + y for z in range(16)] for y in range(4)]
    summed = lax.psum_scatter(
        partial_wg, "rows", scatter_dimension=0, axis_index_groups=y_groups, tiled=True
    )
    weight, unused = lax.optimization_barrier((out_weight, summed))
    block = (4, 2 * N, 2 * N)
    own, other = call(projection_kernel, [(block, BF)] * 2, [info, weight], [SMEM, VMEM], name="projection")
    swapped = lax.ppermute(other, "heads", [(i, i ^ 1) for i in range(8)])
    (hidden,) = call(hidden_kernel, [(wide, BF)], [got, o_row], name="hidden")
    hidden = lax.all_gather(hidden, "heads", axis=0, tiled=True, axis_index_groups=pairs)
    encoded, sent = call(
        encode_kernel,
        [(wide, F32), ((3, N, 2 * N), BF)],
        [info, hidden, own, swapped],
        [SMEM] + [VMEM] * 3,
        flops=1_000_000_000,
        name="encode",
    )
    for step in range(1, 4):
        moves = [(i, ((i // 2 + step) % 4) * 2 + i % 2) for i in range(8)]
        encoded = encoded + lax.ppermute(sent[step - 1], "heads", moves).astype(F32)
    encoded = encoded.astype(BF)[None]
    grad_q, grad_k, grad_v, grad_rate, grad_gate = call(
        gradient_kernel,
        [(wide, BF)] * 3 + [((2, N), F32), ((8, N), F32)],
        [info, got, gq, gk, gv, gs],
        [SMEM] + [VMEM] * 5,
        flops=1_000_000_000,
        name="gradients",
    )

    pieces = exchange(summed, "rows", z_groups)
    weight_grad = jnp.sum(pieces.reshape(16, 32, 2 * N).astype(F32), axis=0)
    rate_grad = grad_rate.T[None]
    gate_grad = grad_gate.reshape(2, 4, N).transpose(2, 0, 1)[None]
    return (encoded, grad_q[None], grad_k[None], grad_v[None], rate_grad, gate_grad, weight_grad)


def solution(mesh):
    in_specs = (
        P("rows", None, "heads"),
        P("rows", None, "heads"),
        P("rows", None, "heads"),
        P("rows", None, "heads"),
        P("rows", None, "heads", None),
        P("rows"),
        P("heads", None),
        P("rows", None, "heads"),
    )
    out_specs = (
        P("rows", None, "heads"),
        P("rows", None, "heads"),
        P("rows", None, "heads"),
        P("rows", None, "heads"),
        P("rows", None, "heads"),
        P("rows", None, "heads", None),
        P("rows", "heads"),
    )
    return jax.shard_map(
        per_device, mesh=mesh, in_specs=in_specs, out_specs=out_specs, check_vma=False
    )
```

```python
import functools

import jax
import jax.numpy as jnp
from jax import lax
from jax.experimental import pallas as pl
from jax.experimental.pallas import tpu as pltpu
from jax.sharding import PartitionSpec as P

N = 128
F32 = jnp.float32
BF = jnp.bfloat16


def dot(a, b, ca=1, cb=0):
    return lax.dot_general(a.astype(BF), b.astype(BF), (((ca,), (cb,)), ((), ())), preferred_element_type=F32)


def iotas(rows=N, cols=N):
    return lax.broadcasted_iota(jnp.int32, (rows, cols), 0), lax.broadcasted_iota(jnp.int32, (rows, cols), 1)


def shr(x, n):
    return lax.shift_right_logical(x, jnp.int32(n))


def invert(systems, length):
    i, j = iotas()
    apart = i ^ j
    eye = jnp.where(apart == 0, 1.0, 0.0)
    solved = [eye - jnp.where(apart == 1, a, 0.0) for a in systems]
    level = 1
    while (2 << level) <= length:
        mask = shr(apart, level) == 1
        crossing = [jnp.where(mask, a, 0.0).astype(BF) for a in systems]
        halves = [t.astype(BF) for t in solved]
        inner = [dot(c, t) for c, t in zip(crossing, halves)]
        solved = [t - dot(h, m) for t, h, m in zip(solved, halves, inner)]
        level += 1
    return solved


def split3(x):
    hi = x.astype(BF)
    rest = x - hi.astype(F32)
    mid = rest.astype(BF)
    return hi, mid, (rest - mid.astype(F32)).astype(BF)


def prefix_sums(length):
    i, j = iotas()
    shift = length.bit_length() - 1
    same = shr(i, shift) == shr(j, shift)
    before = [same & (i >= j), same & (i <= j)]
    return [jnp.where(m, 1.0, 0.0).astype(BF) for m in before], before, i == j


def prepare(q, k, small, length, first):
    sums, before, eye = prefix_sums(length)
    cum = [dot(m, small, 1, 1) for m in sums]
    cum_t = [dot(small, m, 1, 1) for m in sums]
    heads = []
    for h in range(2):
        lanes = slice(h * N, (h + 1) * N)
        kh, qh = k[:, lanes], q[:, lanes]
        gram = dot(kh, kh, 1, 1)
        cross = dot(qh, kh, 1, 1)
        diag = jnp.where(eye, gram, 0.0)
        s_col = lax.rsqrt(jnp.sum(diag, axis=1, keepdims=True) + 1e-6)
        s_row = lax.rsqrt(jnp.sum(diag, axis=0, keepdims=True) + 1e-6)
        gram = gram * (s_col * s_row)
        cross = cross * (s_row * (N ** -0.5))
        rate_row = small[8 + h : 9 + h, :]
        per = []
        for d in range(2):
            g = 4 * h + first + d
            ratio = cum[d][:, g : g + 1] - cum_t[d][g : g + 1, :]
            weight = jnp.exp(jnp.where(before[d], ratio, -jnp.inf)) * rate_row
            strict = jnp.where(eye, 0.0, weight)
            per.append((weight, strict, strict * gram, weight * cross))
        heads.append((s_col, s_row, per))
    return sums, heads


def forward(prepared, v, length):
    sums, heads = prepared
    systems = [p[2] for hd in heads for p in hd[2]]
    solved = [t.astype(BF) for t in invert(systems, length)]
    outs, errors = [], []
    for h in range(2):
        vh = v[:, h * N : (h + 1) * N]
        es = [dot(solved[2 * h + d], vh).astype(BF) for d in range(2)]
        mix = jnp.concatenate([heads[h][2][0][3].astype(BF), heads[h][2][1][3].astype(BF)], axis=1)
        outs.append(dot(mix, jnp.concatenate(es, axis=0)))
        errors += es
    return outs, solved, errors


def backward(prepared, solved, errors, q, k, small, cot, first):
    sums, heads = prepared
    i, j = iotas()
    gq, gk, gv, rowsums, colsums = [], [], [], [], []
    for h in range(2):
        lanes = slice(h * N, (h + 1) * N)
        s_col, s_row, per = heads[h]
        c, kh, qh = cot[:, lanes], k[:, lanes], q[:, lanes]
        es = errors[2 * h : 2 * h + 2]
        d_mix = dot(c, jnp.concatenate(es, axis=0), 1, 1)
        mix = jnp.concatenate([per[0][3].astype(BF), per[1][3].astype(BF)], axis=1)
        d_err = dot(mix, c, 0, 0)
        d_val = [dot(solved[2 * h + d], d_err[d * N : (d + 1) * N], 0, 0) for d in range(2)]
        d_sys = [-dot(d_val[d], es[d], 1, 1) for d in range(2)]
        d_gram, d_cross = 0.0, 0.0
        for d in range(2):
            weight, strict, system, mixing = per[d]
            dm = d_mix[:, d * N : (d + 1) * N]
            d_gram = d_gram + d_sys[d] * strict
            d_cross = d_cross + dm * weight
            total = d_sys[d] * system + dm * mixing
            rowsums.append(jnp.sum(total, axis=1, keepdims=True))
            colsums.append(jnp.sum(total, axis=0, keepdims=True))
        both = d_gram + d_gram.T
        gq.append(dot(d_cross * (s_row * (N ** -0.5)), kh))
        kf = kh.astype(F32)
        d_kn = dot(both * s_row, kh) + dot(d_cross, qh, 0, 0) * (N ** -0.5)
        along = s_col * jnp.sum(kf * d_kn, axis=1, keepdims=True)
        gk.append(s_col * (d_kn - kf * (s_col * along)))
        gv.append(d_val[0] + d_val[1])
    across = jnp.zeros((N, N), F32)
    for s in range(4):
        across = jnp.where(j == s, rowsums[s], across)
    d_cum = across.T[:8, :] - jnp.concatenate(colsums + [jnp.zeros((4, N), F32)], axis=0)
    pieces = split3(d_cum)
    gates = [sum(dot(p, sums[1 - d], 1, 1) for p in pieces) for d in range(2)]
    zero = jnp.zeros((1, N), F32)
    out = [zero] * 16
    for h in range(2):
        rate = small[8 + h : 9 + h, :]
        whole = colsums[2 * h] + colsums[2 * h + 1]
        out[8 + h] = jnp.where(rate > 0, whole / jnp.where(rate > 0, rate, 1.0), 0.0)
        for d in range(2):
            s = 2 * h + d
            out[4 * h + first + d] = gates[d][s : s + 1, :]
    out = jnp.concatenate(out, axis=0)
    return jnp.concatenate(gq, axis=1), jnp.concatenate(gk, axis=1), jnp.concatenate(gv, axis=1), out


VMEM = pl.BlockSpec(memory_space=pltpu.VMEM)
SMEM = pl.BlockSpec(memory_space=pltpu.SMEM)


def one_hot(mask):
    return jnp.where(mask, 1.0, 0.0).astype(BF)


def call(kernel, outs, args, specs=None, flops=100_000_000, name=None, scratch=(), limit=48):
    return pl.pallas_call(
        kernel,
        out_shape=[jax.ShapeDtypeStruct(shape, dtype) for shape, dtype in outs],
        in_specs=specs or [VMEM] * len(args),
        out_specs=[VMEM] * len(outs),
        scratch_shapes=list(scratch),
        compiler_params=pltpu.CompilerParams(vmem_limit_bytes=limit * 1024 * 1024),
        cost_estimate=pl.CostEstimate(flops=flops, bytes_accessed=2_000_000, transcendentals=0),
        name=name,
    )(*args)


def small_rows(info_ref, rate_ref, gate_ref):
    rows = jnp.concatenate(
        [gate_ref[...].astype(F32), rate_ref[...].astype(F32), jnp.ones((6, N), F32)], axis=0
    )
    row, patch = iotas(16, N)
    return jnp.where((patch < info_ref[0]) & (row < 11), rows, 0.0)


def shuffle(by_column, inverse):
    i, j = iotas(144, 144)
    packed, plain = (j, i) if inverse else (i, j)
    peer = shr(packed * 3641, 16)
    rest = packed - 18 * peer
    c = rest & 1
    within = 8 * c + peer if by_column else 2 * peer + c
    return one_hot(plain == 16 * shr(rest, 1) + within)


def pack(parts, small, by_column, out_ref):
    parts = [part[:, h * N : (h + 1) * N].astype(F32) for part in parts for h in range(2)]
    parts.append(jnp.concatenate([small, jnp.zeros((N - 16, N), F32)], axis=0).T)
    order = shuffle(by_column, False)
    for b in range(8):
        if by_column:
            rows = [part[start + 8 * b : start + 8 * b + 8] for part in parts for start in (0, 64)]
        else:
            rows = [part[16 * b : 16 * b + 16] for part in parts]
        out_ref[144 * b : 144 * b + 144, :] = dot(order, jnp.concatenate(rows, axis=0)).astype(BF)


def unpack(got_ref, by_column, first=0, last=9):
    order = shuffle(by_column, True)[16 * first : 16 * last]
    blocks = [dot(order, got_ref[144 * b : 144 * b + 144, :]) for b in range(8)]
    parts = []
    for s in range(last - first):
        if by_column:
            rows = [block[16 * s + 8 * c : 16 * s + 8 * c + 8] for c in range(2) for block in blocks]
        else:
            rows = [block[16 * s : 16 * s + 16] for block in blocks]
        parts.append(jnp.concatenate(rows, axis=0))
    return parts


def heads_of(parts):
    return [jnp.concatenate(parts[2 * a : 2 * a + 2], axis=1) for a in range(len(parts) // 2)]


def pack_kernel(info_ref, rate_ref, gate_ref, q_ref, k_ref, v_ref, cot_ref, out_ref, held, sems):
    copies = [
        pltpu.make_async_copy(ref, held.at[a], sems.at[a])
        for a, ref in enumerate((q_ref, k_ref, v_ref, cot_ref))
    ]
    for copy in copies:
        copy.start()
    small = small_rows(info_ref, rate_ref, gate_ref)
    for copy in copies:
        copy.wait()
    pack([held[a] for a in range(4)], small, False, out_ref)


def row_kernel(
    info_ref, q_ref, k_ref, v_ref, rate_ref, gate_ref, cot_ref, w_ref, o_ref, gq_ref, gk_ref, gv_ref, gs_ref
):
    patch, unused = iotas(N, 2 * N)
    cot = jnp.where(patch < info_ref[0], dot(cot_ref[...], w_ref[...], 1, 1), 0.0).astype(BF)
    q, k, v = q_ref[...], k_ref[...], v_ref[...]
    small = small_rows(info_ref, rate_ref, gate_ref)
    ready = prepare(q, k, small, N, 0)
    outs, solved, errors = forward(ready, v, N)
    o_ref[...] = jnp.where(patch < info_ref[0], jnp.concatenate(outs, axis=1), 0.0)
    gq_ref[...], gk_ref[...], gv_ref[...], gs_ref[...] = backward(ready, solved, errors, q, k, small, cot, 0)


def unpack_kernel(got_ref, q_ref, k_ref, v_ref, copies_ref, small_ref):
    pieces = unpack(got_ref, True)
    parts, scalars = heads_of(pieces), pieces[8]
    for part, ref in zip(parts, (q_ref, k_ref, v_ref)):
        ref[...] = part.astype(BF)
    for x in range(4):
        copies_ref[x * N : (x + 1) * N, :] = parts[3].astype(BF)
    small_ref[...] = scalars.T[:16, :]


def tissue_of(small):
    return jnp.concatenate([small, jnp.zeros((N - 16, N), F32)], axis=0).T[:, 10:11] > 0.5


def column_forward_kernel(q_ref, k_ref, v_ref, small_ref, o_ref, t_ref, e_ref):
    small = small_ref[...]
    outs, solved, errors = forward(prepare(q_ref[...], k_ref[...], small, 64, 2), v_ref[...], 64)
    o_ref[...] = jnp.where(tissue_of(small), jnp.concatenate(outs, axis=1), 0.0).astype(BF)
    for s in range(4):
        t_ref[s], e_ref[s] = solved[s], errors[s]


def column_backward_kernel(q_ref, k_ref, small_ref, o_ref, t_ref, e_ref, cot_ref, w_ref, send_ref):
    total = 0.0
    for block in range(8):
        rows = ((block & 1) * 4 + (block >> 1)) * N
        total = total + dot(cot_ref[rows : rows + N, :], w_ref[:, block * 2 * N : (block + 1) * 2 * N], 1, 1)
    q, k, small = q_ref[...], k_ref[...], small_ref[...]
    cot = jnp.where(tissue_of(small), total, 0.0).astype(BF)
    solved = [t_ref[s] for s in range(4)]
    errors = [e_ref[s] for s in range(4)]
    gq, gk, gv, gs = backward(prepare(q, k, small, 64, 2), solved, errors, q, k, small, cot, 2)
    pack([o_ref[...], gq, gk, gv], gs, True, send_ref)


def weight_kernel(row_cot_ref, row_o_ref, col_cot_ref, col_o_ref, wg_ref):
    hidden = jnp.concatenate([row_o_ref[...].astype(BF), col_o_ref[...]], axis=0)
    for z in range(16):
        block, half = z >> 1, z & 1
        rows = ((block & 1) * 4 + (block >> 1)) * N
        col_cot = col_cot_ref[rows : rows + N, half * N : (half + 1) * N]
        cot = jnp.concatenate([row_cot_ref[:, z * N : (z + 1) * N], col_cot], axis=0)
        part = dot(cot, hidden, 0, 0).astype(BF)
        for y in range(4):
            start = y * 512 + z * 32
            wg_ref[start : start + 32, :] = part[y * 32 : (y + 1) * 32, :]


def projection_kernel(info_ref, w_ref, own_ref, other_ref):
    place, core = info_ref[1], info_ref[2]
    for step in range(4):
        for ref, side in ((own_ref, core), (other_ref, 1 - core)):
            block = 2 * ((place + step) & 3) + side
            lanes = pl.ds(pl.multiple_of(block * 2 * N, 2 * N), 2 * N)
            ref[step] = w_ref[:, lanes]


def hidden_kernel(got_ref, o_ref, hidden_ref):
    (col,) = heads_of(unpack(got_ref, False, 0, 2))
    hidden_ref[...] = (o_ref[...] + col).astype(BF)


def gradient_kernel(
    info_ref, got_ref, gq_ref, gk_ref, gv_ref, gs_ref, q_ref, k_ref, v_ref, rate_ref, gate_ref
):
    pieces = unpack(got_ref, False, 2, 9)
    parts, scalars = heads_of(pieces), pieces[6]
    for part, row_ref, out_ref in zip(parts, (gq_ref, gk_ref, gv_ref), (q_ref, k_ref, v_ref)):
        out_ref[...] = (row_ref[...] + part).astype(BF)
    unused, patch = iotas(16, N)
    small = jnp.where(patch < info_ref[0], gs_ref[...] + scalars.T[:16, :], 0.0)
    gate_ref[...] = small[:8, :]
    rate_ref[...] = small[8:10, :]


def encode_kernel(info_ref, hidden_ref, own_ref, swapped_ref, kept_ref, sent_ref):
    core = info_ref[2]
    mine = hidden_ref[pl.ds(pl.multiple_of(core * N, N), N), :]
    other = hidden_ref[pl.ds(pl.multiple_of((1 - core) * N, N), N), :]
    for step in range(4):
        part = dot(mine, own_ref[step]) + dot(other, swapped_ref[step])
        if step == 0:
            kept_ref[...] = part
        else:
            sent_ref[step - 1] = part.astype(BF)


def exchange(x, axis, groups=None):
    return lax.all_to_all(x, axis, split_axis=0, concat_axis=0, tiled=True, axis_index_groups=groups)


def swap_rows(x):
    return exchange(x.reshape(64, 9, 2, N), "rows").reshape(18 * 64, N)


def per_device(
    query_proj, key_proj, value_proj, write_rate, log_gate, tissue_lengths, out_weight, cotangent
):
    q, k, v = query_proj[0], key_proj[0], value_proj[0]
    rate = write_rate[0].T
    gate = log_gate[0].transpose(1, 2, 0).reshape(8, N)
    me = lax.axis_index("heads")
    info = jnp.stack([tissue_lengths[0], lax.shift_right_logical(me, 1), me & 1])
    wide, few = (N, 2 * N), (16, N)

    (send,) = call(
        pack_kernel,
        [((18 * 64, N), BF)],
        [tissue_lengths, rate, gate, q, k, v, cotangent[0]],
        [SMEM, VMEM, VMEM] + [pl.BlockSpec(memory_space=pl.ANY)] * 4,
        name="pack",
        scratch=[pltpu.VMEM((4, N, 2 * N), BF), pltpu.SemaphoreType.DMA((4,))],
        limit=62,
    )
    got = swap_rows(send)
    row_cot = lax.all_gather(cotangent[0], "heads", axis=1, tiled=True)
    weight, unused = lax.optimization_barrier((out_weight, row_cot))
    block = (4, 2 * N, 2 * N)
    own, other = call(projection_kernel, [(block, BF)] * 2, [info, weight], [SMEM, VMEM], name="projection")
    swapped = lax.ppermute(other, "heads", [(i, i ^ 1) for i in range(8)])
    o_row, gq, gk, gv, gs = call(
        row_kernel,
        [(wide, F32)] * 4 + [(few, F32)],
        [info, q, k, v, rate, gate, row_cot, out_weight],
        [SMEM] + [VMEM] * 7,
        flops=6_000_000_000,
        name="row_directions",
    )
    got, swapped = lax.optimization_barrier((got, swapped))
    qc, kc, vc, copies, sc = call(
        unpack_kernel,
        [(wide, BF)] * 3 + [((4 * N, 2 * N), BF), (few, F32)],
        [got],
        name="unpack",
    )
    x_groups = [[2 * x + core for x in range(4)] for core in range(2)]
    pairs = [[2 * x, 2 * x + 1] for x in range(4)]
    along_x = exchange(copies, "heads", x_groups)
    col_cot = lax.all_gather(along_x, "heads", axis=0, tiled=True, axis_index_groups=pairs)
    o_col, tc, ec = call(
        column_forward_kernel,
        [(wide, BF)] + [((4, N, N), BF)] * 2,
        [qc, kc, vc, sc],
        flops=3_000_000_000,
        name="column_forward",
    )
    (send,) = call(
        column_backward_kernel,
        [((18 * 64, N), BF)],
        [qc, kc, sc, o_col, tc, ec, col_cot, out_weight],
        flops=3_000_000_000,
        name="column_backward",
    )
    got = swap_rows(send)
    (partial_wg,) = call(
        weight_kernel,
        [((2048, 2 * N), BF)],
        [row_cot, o_row, col_cot, o_col],
        flops=2_000_000_000,
        name="weight_gradient",
    )
    y_groups = [[z * 4 + y for y in range(4)] for z in range(16)]
    z_groups = [[z * 4 + y for z in range(16)] for y in range(4)]
    summed = lax.psum_scatter(
        partial_wg, "rows", scatter_dimension=0, axis_index_groups=y_groups, tiled=True
    )
    (hidden,) = call(hidden_kernel, [(wide, BF)], [got, o_row], name="hidden")
    hidden = lax.all_gather(hidden, "heads", axis=0, tiled=True, axis_index_groups=pairs)
    encoded, sent = call(
        encode_kernel,
        [(wide, F32), ((3, N, 2 * N), BF)],
        [info, hidden, own, swapped],
        [SMEM] + [VMEM] * 3,
        flops=1_000_000_000,
        name="encode",
    )
    for step in range(1, 4):
        moves = [(i, ((i // 2 + step) % 4) * 2 + i % 2) for i in range(8)]
        encoded = encoded + lax.ppermute(sent[step - 1], "heads", moves).astype(F32)
    encoded = encoded.astype(BF)[None]
    grad_q, grad_k, grad_v, grad_rate, grad_gate = call(
        gradient_kernel,
        [(wide, BF)] * 3 + [((2, N), F32), ((8, N), F32)],
        [info, got, gq, gk, gv, gs],
        [SMEM] + [VMEM] * 5,
        flops=1_000_000_000,
        name="gradients",
    )

    pieces = exchange(summed, "rows", z_groups)
    weight_grad = jnp.sum(pieces.reshape(16, 32, 2 * N).astype(F32), axis=0)
    rate_grad = grad_rate.T[None]
    gate_grad = grad_gate.reshape(2, 4, N).transpose(2, 0, 1)[None]
    return (encoded, grad_q[None], grad_k[None], grad_v[None], rate_grad, gate_grad, weight_grad)


def solution(mesh):
    in_specs = (
        P("rows", None, "heads"),
        P("rows", None, "heads"),
        P("rows", None, "heads"),
        P("rows", None, "heads"),
        P("rows", None, "heads", None),
        P("rows"),
        P("heads", None),
        P("rows", None, "heads"),
    )
    out_specs = (
        P("rows", None, "heads"),
        P("rows", None, "heads"),
        P("rows", None, "heads"),
        P("rows", None, "heads"),
        P("rows", None, "heads"),
        P("rows", None, "heads", None),
        P("rows", "heads"),
    )
    return jax.shard_map(
        per_device, mesh=mesh, in_specs=in_specs, out_specs=out_specs, check_vma=False
    )
```

```python
import functools

import jax
import jax.numpy as jnp
from jax import lax
from jax.experimental import pallas as pl
from jax.experimental.pallas import tpu as pltpu
from jax.sharding import PartitionSpec as P

N = 128
F32 = jnp.float32
BF = jnp.bfloat16


def dot(a, b, ca=1, cb=0):
    return lax.dot_general(a.astype(BF), b.astype(BF), (((ca,), (cb,)), ((), ())), preferred_element_type=F32)


def iotas(rows=N, cols=N):
    return lax.broadcasted_iota(jnp.int32, (rows, cols), 0), lax.broadcasted_iota(jnp.int32, (rows, cols), 1)


def shr(x, n):
    return lax.shift_right_logical(x, jnp.int32(n))


def invert(systems, length):
    i, j = iotas()
    apart = i ^ j
    eye = jnp.where(apart == 0, 1.0, 0.0)
    solved = [eye - jnp.where(apart == 1, a, 0.0) for a in systems]
    level = 1
    while (2 << level) <= length:
        mask = shr(apart, level) == 1
        crossing = [jnp.where(mask, a, 0.0).astype(BF) for a in systems]
        halves = [t.astype(BF) for t in solved]
        inner = [dot(c, t) for c, t in zip(crossing, halves)]
        solved = [t - dot(h, m) for t, h, m in zip(solved, halves, inner)]
        level += 1
    return solved


def split3(x):
    hi = x.astype(BF)
    rest = x - hi.astype(F32)
    mid = rest.astype(BF)
    return hi, mid, (rest - mid.astype(F32)).astype(BF)


def prefix_sums(length):
    i, j = iotas()
    shift = length.bit_length() - 1
    same = shr(i, shift) == shr(j, shift)
    before = [same & (i >= j), same & (i <= j)]
    return [jnp.where(m, 1.0, 0.0).astype(BF) for m in before], before, i == j


def prepare(q, k, small, length, first):
    sums, before, eye = prefix_sums(length)
    cum = [dot(m, small, 1, 1) for m in sums]
    cum_t = [dot(small, m, 1, 1) for m in sums]
    heads = []
    for h in range(2):
        lanes = slice(h * N, (h + 1) * N)
        kh, qh = k[:, lanes], q[:, lanes]
        gram = dot(kh, kh, 1, 1)
        cross = dot(qh, kh, 1, 1)
        diag = jnp.where(eye, gram, 0.0)
        s_col = lax.rsqrt(jnp.sum(diag, axis=1, keepdims=True) + 1e-6)
        s_row = lax.rsqrt(jnp.sum(diag, axis=0, keepdims=True) + 1e-6)
        gram = gram * (s_col * s_row)
        cross = cross * (s_row * (N ** -0.5))
        rate_row = small[8 + h : 9 + h, :]
        per = []
        for d in range(2):
            g = 4 * h + first + d
            ratio = cum[d][:, g : g + 1] - cum_t[d][g : g + 1, :]
            weight = jnp.exp(jnp.where(before[d], ratio, -jnp.inf)) * rate_row
            strict = jnp.where(eye, 0.0, weight)
            per.append((weight, strict, strict * gram, weight * cross))
        heads.append((s_col, s_row, per))
    return sums, heads


def forward(prepared, v, length):
    sums, heads = prepared
    systems = [p[2] for hd in heads for p in hd[2]]
    solved = [t.astype(BF) for t in invert(systems, length)]
    outs, errors = [], []
    for h in range(2):
        vh = v[:, h * N : (h + 1) * N]
        es = [dot(solved[2 * h + d], vh).astype(BF) for d in range(2)]
        mix = jnp.concatenate([heads[h][2][0][3].astype(BF), heads[h][2][1][3].astype(BF)], axis=1)
        outs.append(dot(mix, jnp.concatenate(es, axis=0)))
        errors += es
    return outs, solved, errors


def backward(prepared, solved, errors, q, k, small, cot, first):
    sums, heads = prepared
    i, j = iotas()
    gq, gk, gv, rowsums, colsums = [], [], [], [], []
    for h in range(2):
        lanes = slice(h * N, (h + 1) * N)
        s_col, s_row, per = heads[h]
        c, kh, qh = cot[:, lanes], k[:, lanes], q[:, lanes]
        es = errors[2 * h : 2 * h + 2]
        d_mix = dot(c, jnp.concatenate(es, axis=0), 1, 1)
        mix = jnp.concatenate([per[0][3].astype(BF), per[1][3].astype(BF)], axis=1)
        d_err = dot(mix, c, 0, 0)
        d_val = [dot(solved[2 * h + d], d_err[d * N : (d + 1) * N], 0, 0) for d in range(2)]
        d_sys = [-dot(d_val[d], es[d], 1, 1) for d in range(2)]
        d_gram, d_cross = 0.0, 0.0
        for d in range(2):
            weight, strict, system, mixing = per[d]
            dm = d_mix[:, d * N : (d + 1) * N]
            d_gram = d_gram + d_sys[d] * strict
            d_cross = d_cross + dm * weight
            total = d_sys[d] * system + dm * mixing
            rowsums.append(jnp.sum(total, axis=1, keepdims=True))
            colsums.append(jnp.sum(total, axis=0, keepdims=True))
        both = d_gram + d_gram.T
        gq.append(dot(d_cross * (s_row * (N ** -0.5)), kh))
        kf = kh.astype(F32)
        d_kn = dot(both * s_row, kh) + dot(d_cross, qh, 0, 0) * (N ** -0.5)
        along = s_col * jnp.sum(kf * d_kn, axis=1, keepdims=True)
        gk.append(s_col * (d_kn - kf * (s_col * along)))
        gv.append(d_val[0] + d_val[1])
    across = jnp.zeros((N, N), F32)
    for s in range(4):
        across = jnp.where(j == s, rowsums[s], across)
    d_cum = across.T[:8, :] - jnp.concatenate(colsums + [jnp.zeros((4, N), F32)], axis=0)
    pieces = split3(d_cum)
    gates = [sum(dot(p, sums[1 - d], 1, 1) for p in pieces) for d in range(2)]
    zero = jnp.zeros((1, N), F32)
    out = [zero] * 16
    for h in range(2):
        rate = small[8 + h : 9 + h, :]
        whole = colsums[2 * h] + colsums[2 * h + 1]
        out[8 + h] = jnp.where(rate > 0, whole / jnp.where(rate > 0, rate, 1.0), 0.0)
        for d in range(2):
            s = 2 * h + d
            out[4 * h + first + d] = gates[d][s : s + 1, :]
    out = jnp.concatenate(out, axis=0)
    return jnp.concatenate(gq, axis=1), jnp.concatenate(gk, axis=1), jnp.concatenate(gv, axis=1), out


VMEM = pl.BlockSpec(memory_space=pltpu.VMEM)
SMEM = pl.BlockSpec(memory_space=pltpu.SMEM)


def one_hot(mask):
    return jnp.where(mask, 1.0, 0.0).astype(BF)


def call(kernel, outs, args, specs=None, flops=100_000_000, name=None, scratch=(), limit=48):
    return pl.pallas_call(
        kernel,
        out_shape=[jax.ShapeDtypeStruct(shape, dtype) for shape, dtype in outs],
        in_specs=specs or [VMEM] * len(args),
        out_specs=[VMEM] * len(outs),
        scratch_shapes=list(scratch),
        compiler_params=pltpu.CompilerParams(vmem_limit_bytes=limit * 1024 * 1024),
        cost_estimate=pl.CostEstimate(flops=flops, bytes_accessed=2_000_000, transcendentals=0),
        name=name,
    )(*args)


def small_rows(info_ref, rate_ref, gate_ref):
    rows = jnp.concatenate(
        [gate_ref[...].astype(F32), rate_ref[...].astype(F32), jnp.ones((6, N), F32)], axis=0
    )
    row, patch = iotas(16, N)
    return jnp.where((patch < info_ref[0]) & (row < 11), rows, 0.0)


def shuffle(by_column, inverse):
    i, j = iotas(144, 144)
    packed, plain = (j, i) if inverse else (i, j)
    peer = shr(packed * 3641, 16)
    rest = packed - 18 * peer
    c = rest & 1
    within = 8 * c + peer if by_column else 2 * peer + c
    return one_hot(plain == 16 * shr(rest, 1) + within)


def pack(parts, small, by_column, out_ref):
    parts = [part[:, h * N : (h + 1) * N].astype(F32) for part in parts for h in range(2)]
    parts.append(jnp.concatenate([small, jnp.zeros((N - 16, N), F32)], axis=0).T)
    order = shuffle(by_column, False)
    for b in range(8):
        if by_column:
            rows = [part[start + 8 * b : start + 8 * b + 8] for part in parts for start in (0, 64)]
        else:
            rows = [part[16 * b : 16 * b + 16] for part in parts]
        out_ref[144 * b : 144 * b + 144, :] = dot(order, jnp.concatenate(rows, axis=0)).astype(BF)


def unpack(got_ref, by_column, first=0, last=9):
    order = shuffle(by_column, True)[16 * first : 16 * last]
    blocks = [dot(order, got_ref[144 * b : 144 * b + 144, :]) for b in range(8)]
    parts = []
    for s in range(last - first):
        if by_column:
            rows = [block[16 * s + 8 * c : 16 * s + 8 * c + 8] for c in range(2) for block in blocks]
        else:
            rows = [block[16 * s : 16 * s + 16] for block in blocks]
        parts.append(jnp.concatenate(rows, axis=0))
    return parts


def heads_of(parts):
    return [jnp.concatenate(parts[2 * a : 2 * a + 2], axis=1) for a in range(len(parts) // 2)]


def pack_kernel(info_ref, rate_ref, gate_ref, q_ref, k_ref, v_ref, cot_ref, out_ref, held, sems):
    copies = [
        pltpu.make_async_copy(ref, held.at[a], sems.at[a])
        for a, ref in enumerate((q_ref, k_ref, v_ref, cot_ref))
    ]
    for copy in copies:
        copy.start()
    small = small_rows(info_ref, rate_ref, gate_ref)
    for copy in copies:
        copy.wait()
    pack([held[a] for a in range(4)], small, False, out_ref)


def row_kernel(
    info_ref, q_ref, k_ref, v_ref, rate_ref, gate_ref, cot_ref, w_ref, o_ref, gq_ref, gk_ref, gv_ref, gs_ref
):
    patch, unused = iotas(N, 2 * N)
    cot = jnp.where(patch < info_ref[0], dot(cot_ref[...], w_ref[...], 1, 1), 0.0).astype(BF)
    q, k, v = q_ref[...], k_ref[...], v_ref[...]
    small = small_rows(info_ref, rate_ref, gate_ref)
    ready = prepare(q, k, small, N, 0)
    outs, solved, errors = forward(ready, v, N)
    o_ref[...] = jnp.where(patch < info_ref[0], jnp.concatenate(outs, axis=1), 0.0)
    gq_ref[...], gk_ref[...], gv_ref[...], gs_ref[...] = backward(ready, solved, errors, q, k, small, cot, 0)


def unpack_kernel(got_ref, q_ref, k_ref, v_ref, copies_ref, small_ref):
    pieces = unpack(got_ref, True)
    parts, scalars = heads_of(pieces), pieces[8]
    for part, ref in zip(parts, (q_ref, k_ref, v_ref)):
        ref[...] = part.astype(BF)
    for x in range(4):
        copies_ref[x * N : (x + 1) * N, :] = parts[3].astype(BF)
    small_ref[...] = scalars.T[:16, :]


def tissue_of(small):
    return jnp.concatenate([small, jnp.zeros((N - 16, N), F32)], axis=0).T[:, 10:11] > 0.5


def column_forward_kernel(q_ref, k_ref, v_ref, small_ref, o_ref, t_ref, e_ref):
    small = small_ref[...]
    outs, solved, errors = forward(prepare(q_ref[...], k_ref[...], small, 64, 2), v_ref[...], 64)
    o_ref[...] = jnp.where(tissue_of(small), jnp.concatenate(outs, axis=1), 0.0).astype(BF)
    for s in range(4):
        t_ref[s], e_ref[s] = solved[s], errors[s]


def column_backward_kernel(q_ref, k_ref, small_ref, o_ref, t_ref, e_ref, cot_ref, w_ref, send_ref):
    total = 0.0
    for block in range(8):
        rows = ((block & 1) * 4 + (block >> 1)) * N
        total = total + dot(cot_ref[rows : rows + N, :], w_ref[:, block * 2 * N : (block + 1) * 2 * N], 1, 1)
    q, k, small = q_ref[...], k_ref[...], small_ref[...]
    cot = jnp.where(tissue_of(small), total, 0.0).astype(BF)
    solved = [t_ref[s] for s in range(4)]
    errors = [e_ref[s] for s in range(4)]
    gq, gk, gv, gs = backward(prepare(q, k, small, 64, 2), solved, errors, q, k, small, cot, 2)
    pack([o_ref[...], gq, gk, gv], gs, True, send_ref)


def weight_kernel(
    info_ref, row_cot_ref, row_o_ref, col_cot_ref, col_o_ref, own_ref, first_ref, second_ref, third_ref, part_ref
):
    hidden = jnp.concatenate([row_o_ref[...].astype(BF), col_o_ref[...]], axis=0)
    for z in range(16):
        block, half = z >> 1, z & 1
        rows = ((block & 1) * 4 + (block >> 1)) * N
        col_cot = col_cot_ref[rows : rows + N, half * N : (half + 1) * N]
        cot = jnp.concatenate([row_cot_ref[:, z * N : (z + 1) * N], col_cot], axis=0)
        part_ref[z] = dot(cot, hidden, 0, 0)
    for step, ref in enumerate((own_ref, first_ref, second_ref, third_ref)):
        start = pl.multiple_of(((info_ref[3] + step) & 3) * 32, 32)
        for z in range(16):
            ref[z * 32 : (z + 1) * 32, :] = part_ref[z, pl.ds(start, 32), :].astype(BF)


def projection_kernel(info_ref, w_ref, own_ref, other_ref):
    place, core = info_ref[1], info_ref[2]
    for step in range(4):
        for ref, side in ((own_ref, core), (other_ref, 1 - core)):
            block = 2 * ((place + step) & 3) + side
            lanes = pl.ds(pl.multiple_of(block * 2 * N, 2 * N), 2 * N)
            ref[step] = w_ref[:, lanes]


def hidden_kernel(got_ref, o_ref, hidden_ref):
    (col,) = heads_of(unpack(got_ref, False, 0, 2))
    hidden_ref[...] = (o_ref[...] + col).astype(BF)


def gradient_kernel(
    info_ref, got_ref, gq_ref, gk_ref, gv_ref, gs_ref, q_ref, k_ref, v_ref, rate_ref, gate_ref
):
    pieces = unpack(got_ref, False, 2, 9)
    parts, scalars = heads_of(pieces), pieces[6]
    for part, row_ref, out_ref in zip(parts, (gq_ref, gk_ref, gv_ref), (q_ref, k_ref, v_ref)):
        out_ref[...] = (row_ref[...] + part).astype(BF)
    unused, patch = iotas(16, N)
    small = jnp.where(patch < info_ref[0], gs_ref[...] + scalars.T[:16, :], 0.0)
    gate_ref[...] = small[:8, :]
    rate_ref[...] = small[8:10, :]


def encode_kernel(info_ref, hidden_ref, own_ref, swapped_ref, kept_ref, sent_ref):
    core = info_ref[2]
    mine = hidden_ref[pl.ds(pl.multiple_of(core * N, N), N), :]
    other = hidden_ref[pl.ds(pl.multiple_of((1 - core) * N, N), N), :]
    for step in range(4):
        part = dot(mine, own_ref[step]) + dot(other, swapped_ref[step])
        if step == 0:
            kept_ref[...] = part
        else:
            sent_ref[step - 1] = part.astype(BF)


def exchange(x, axis, groups=None):
    return lax.all_to_all(x, axis, split_axis=0, concat_axis=0, tiled=True, axis_index_groups=groups)


def swap_rows(x):
    return exchange(x.reshape(64, 9, 2, N), "rows").reshape(18 * 64, N)


def per_device(
    query_proj, key_proj, value_proj, write_rate, log_gate, tissue_lengths, out_weight, cotangent
):
    q, k, v = query_proj[0], key_proj[0], value_proj[0]
    rate = write_rate[0].T
    gate = log_gate[0].transpose(1, 2, 0).reshape(8, N)
    me = lax.axis_index("heads")
    info = jnp.stack([tissue_lengths[0], lax.shift_right_logical(me, 1), me & 1, lax.axis_index("rows") & 3])
    wide, few = (N, 2 * N), (16, N)

    (send,) = call(
        pack_kernel,
        [((18 * 64, N), BF)],
        [tissue_lengths, rate, gate, q, k, v, cotangent[0]],
        [SMEM, VMEM, VMEM] + [pl.BlockSpec(memory_space=pl.ANY)] * 4,
        name="pack",
        scratch=[pltpu.VMEM((4, N, 2 * N), BF), pltpu.SemaphoreType.DMA((4,))],
        limit=62,
    )
    got = swap_rows(send)
    row_cot = lax.all_gather(cotangent[0], "heads", axis=1, tiled=True)
    weight, unused = lax.optimization_barrier((out_weight, row_cot))
    block = (4, 2 * N, 2 * N)
    own, other = call(projection_kernel, [(block, BF)] * 2, [info, weight], [SMEM, VMEM], name="projection")
    swapped = lax.ppermute(other, "heads", [(i, i ^ 1) for i in range(8)])
    o_row, gq, gk, gv, gs = call(
        row_kernel,
        [(wide, F32)] * 4 + [(few, F32)],
        [info, q, k, v, rate, gate, row_cot, out_weight],
        [SMEM] + [VMEM] * 7,
        flops=6_000_000_000,
        name="row_directions",
    )
    got, swapped = lax.optimization_barrier((got, swapped))
    qc, kc, vc, copies, sc = call(
        unpack_kernel,
        [(wide, BF)] * 3 + [((4 * N, 2 * N), BF), (few, F32)],
        [got],
        name="unpack",
    )
    x_groups = [[2 * x + core for x in range(4)] for core in range(2)]
    pairs = [[2 * x, 2 * x + 1] for x in range(4)]
    along_x = exchange(copies, "heads", x_groups)
    col_cot = lax.all_gather(along_x, "heads", axis=0, tiled=True, axis_index_groups=pairs)
    o_col, tc, ec = call(
        column_forward_kernel,
        [(wide, BF)] + [((4, N, N), BF)] * 2,
        [qc, kc, vc, sc],
        flops=3_000_000_000,
        name="column_forward",
    )
    (send,) = call(
        column_backward_kernel,
        [((18 * 64, N), BF)],
        [qc, kc, sc, o_col, tc, ec, col_cot, out_weight],
        flops=3_000_000_000,
        name="column_backward",
    )
    got = swap_rows(send)
    own_wg, *sent_wg = call(
        weight_kernel,
        [((4 * N, 2 * N), BF)] * 4,
        [info, row_cot, o_row, col_cot, o_col],
        [SMEM] + [VMEM] * 4,
        flops=2_000_000_000,
        name="weight_gradient",
        scratch=[pltpu.VMEM((16, N, 2 * N), F32)],
    )
    summed = own_wg.astype(F32)
    for step in range(1, 4):
        moves = [(z * 4 + y, z * 4 + (y + step) % 4) for z in range(16) for y in range(4)]
        summed = summed + lax.ppermute(sent_wg[step - 1], "rows", moves).astype(F32)
    summed = summed.astype(BF)
    z_groups = [[z * 4 + y for z in range(16)] for y in range(4)]
    (hidden,) = call(hidden_kernel, [(wide, BF)], [got, o_row], name="hidden")
    hidden = lax.all_gather(hidden, "heads", axis=0, tiled=True, axis_index_groups=pairs)
    encoded, sent = call(
        encode_kernel,
        [(wide, F32), ((3, N, 2 * N), BF)],
        [info, hidden, own, swapped],
        [SMEM] + [VMEM] * 3,
        flops=1_000_000_000,
        name="encode",
    )
    for step in range(1, 4):
        moves = [(i, ((i // 2 + step) % 4) * 2 + i % 2) for i in range(8)]
        encoded = encoded + lax.ppermute(sent[step - 1], "heads", moves).astype(F32)
    encoded = encoded.astype(BF)[None]
    grad_q, grad_k, grad_v, grad_rate, grad_gate = call(
        gradient_kernel,
        [(wide, BF)] * 3 + [((2, N), F32), ((8, N), F32)],
        [info, got, gq, gk, gv, gs],
        [SMEM] + [VMEM] * 5,
        flops=1_000_000_000,
        name="gradients",
    )

    pieces = exchange(summed, "rows", z_groups)
    weight_grad = jnp.sum(pieces.reshape(16, 32, 2 * N).astype(F32), axis=0)
    rate_grad = grad_rate.T[None]
    gate_grad = grad_gate.reshape(2, 4, N).transpose(2, 0, 1)[None]
    return (encoded, grad_q[None], grad_k[None], grad_v[None], rate_grad, gate_grad, weight_grad)


def solution(mesh):
    in_specs = (
        P("rows", None, "heads"),
        P("rows", None, "heads"),
        P("rows", None, "heads"),
        P("rows", None, "heads"),
        P("rows", None, "heads", None),
        P("rows"),
        P("heads", None),
        P("rows", None, "heads"),
    )
    out_specs = (
        P("rows", None, "heads"),
        P("rows", None, "heads"),
        P("rows", None, "heads"),
        P("rows", None, "heads"),
        P("rows", None, "heads"),
        P("rows", None, "heads", None),
        P("rows", "heads"),
    )
    return jax.shard_map(
        per_device, mesh=mesh, in_specs=in_specs, out_specs=out_specs, check_vma=False
    )
```

```python
import functools

import jax
import jax.numpy as jnp
from jax import lax
from jax.experimental import pallas as pl
from jax.experimental.pallas import tpu as pltpu
from jax.sharding import PartitionSpec as P

N = 128
F32 = jnp.float32
BF = jnp.bfloat16


def dot(a, b, ca=1, cb=0):
    return lax.dot_general(a.astype(BF), b.astype(BF), (((ca,), (cb,)), ((), ())), preferred_element_type=F32)


def iotas(rows=N, cols=N):
    return lax.broadcasted_iota(jnp.int32, (rows, cols), 0), lax.broadcasted_iota(jnp.int32, (rows, cols), 1)


def shr(x, n):
    return lax.shift_right_logical(x, jnp.int32(n))


def invert(systems, length):
    i, j = iotas()
    apart = i ^ j
    eye = jnp.where(apart == 0, 1.0, 0.0)
    solved = [eye - jnp.where(apart == 1, a, 0.0) for a in systems]
    level = 1
    while (2 << level) <= length:
        mask = shr(apart, level) == 1
        crossing = [jnp.where(mask, a, 0.0).astype(BF) for a in systems]
        halves = [t.astype(BF) for t in solved]
        inner = [dot(c, t) for c, t in zip(crossing, halves)]
        solved = [t - dot(h, m) for t, h, m in zip(solved, halves, inner)]
        level += 1
    return solved


def split3(x):
    hi = x.astype(BF)
    rest = x - hi.astype(F32)
    mid = rest.astype(BF)
    return hi, mid, (rest - mid.astype(F32)).astype(BF)


def prefix_sums(length):
    i, j = iotas()
    shift = length.bit_length() - 1
    same = shr(i, shift) == shr(j, shift)
    before = [same & (i >= j), same & (i <= j)]
    return [jnp.where(m, 1.0, 0.0).astype(BF) for m in before], before, i == j


def prepare(q, k, small, length, first):
    sums, before, eye = prefix_sums(length)
    cum = [dot(m, small, 1, 1) for m in sums]
    cum_t = [dot(small, m, 1, 1) for m in sums]
    heads = []
    for h in range(2):
        lanes = slice(h * N, (h + 1) * N)
        kh, qh = k[:, lanes], q[:, lanes]
        gram = dot(kh, kh, 1, 1)
        cross = dot(qh, kh, 1, 1)
        diag = jnp.where(eye, gram, 0.0)
        s_col = lax.rsqrt(jnp.sum(diag, axis=1, keepdims=True) + 1e-6)
        s_row = lax.rsqrt(jnp.sum(diag, axis=0, keepdims=True) + 1e-6)
        gram = gram * (s_col * s_row)
        cross = cross * (s_row * (N ** -0.5))
        rate_row = small[8 + h : 9 + h, :]
        per = []
        for d in range(2):
            g = 4 * h + first + d
            ratio = cum[d][:, g : g + 1] - cum_t[d][g : g + 1, :]
            weight = jnp.exp(jnp.where(before[d], ratio, -jnp.inf)) * rate_row
            strict = jnp.where(eye, 0.0, weight)
            per.append((weight, strict, strict * gram, weight * cross))
        heads.append((s_col, s_row, per))
    return sums, heads


def forward(prepared, v, length):
    sums, heads = prepared
    systems = [p[2] for hd in heads for p in hd[2]]
    solved = [t.astype(BF) for t in invert(systems, length)]
    outs, errors = [], []
    for h in range(2):
        vh = v[:, h * N : (h + 1) * N]
        es = [dot(solved[2 * h + d], vh).astype(BF) for d in range(2)]
        mix = jnp.concatenate([heads[h][2][0][3].astype(BF), heads[h][2][1][3].astype(BF)], axis=1)
        outs.append(dot(mix, jnp.concatenate(es, axis=0)))
        errors += es
    return outs, solved, errors


def backward(prepared, solved, errors, q, k, small, cot, first):
    sums, heads = prepared
    i, j = iotas()
    gq, gk, gv, rowsums, colsums = [], [], [], [], []
    for h in range(2):
        lanes = slice(h * N, (h + 1) * N)
        s_col, s_row, per = heads[h]
        c, kh, qh = cot[:, lanes], k[:, lanes], q[:, lanes]
        es = errors[2 * h : 2 * h + 2]
        d_mix = dot(c, jnp.concatenate(es, axis=0), 1, 1)
        mix = jnp.concatenate([per[0][3].astype(BF), per[1][3].astype(BF)], axis=1)
        d_err = dot(mix, c, 0, 0)
        d_val = [dot(solved[2 * h + d], d_err[d * N : (d + 1) * N], 0, 0) for d in range(2)]
        d_sys = [-dot(d_val[d], es[d], 1, 1) for d in range(2)]
        d_gram, d_cross = 0.0, 0.0
        for d in range(2):
            weight, strict, system, mixing = per[d]
            dm = d_mix[:, d * N : (d + 1) * N]
            d_gram = d_gram + d_sys[d] * strict
            d_cross = d_cross + dm * weight
            total = d_sys[d] * system + dm * mixing
            rowsums.append(jnp.sum(total, axis=1, keepdims=True))
            colsums.append(jnp.sum(total, axis=0, keepdims=True))
        both = d_gram + d_gram.T
        gq.append(dot(d_cross * (s_row * (N ** -0.5)), kh))
        kf = kh.astype(F32)
        d_kn = dot(both * s_row, kh) + dot(d_cross, qh, 0, 0) * (N ** -0.5)
        along = s_col * jnp.sum(kf * d_kn, axis=1, keepdims=True)
        gk.append(s_col * (d_kn - kf * (s_col * along)))
        gv.append(d_val[0] + d_val[1])
    across = jnp.zeros((N, N), F32)
    for s in range(4):
        across = jnp.where(j == s, rowsums[s], across)
    d_cum = across.T[:8, :] - jnp.concatenate(colsums + [jnp.zeros((4, N), F32)], axis=0)
    pieces = split3(d_cum)
    gates = [sum(dot(p, sums[1 - d], 1, 1) for p in pieces) for d in range(2)]
    zero = jnp.zeros((1, N), F32)
    out = [zero] * 16
    for h in range(2):
        rate = small[8 + h : 9 + h, :]
        whole = colsums[2 * h] + colsums[2 * h + 1]
        out[8 + h] = jnp.where(rate > 0, whole / jnp.where(rate > 0, rate, 1.0), 0.0)
        for d in range(2):
            s = 2 * h + d
            out[4 * h + first + d] = gates[d][s : s + 1, :]
    out = jnp.concatenate(out, axis=0)
    return jnp.concatenate(gq, axis=1), jnp.concatenate(gk, axis=1), jnp.concatenate(gv, axis=1), out


VMEM = pl.BlockSpec(memory_space=pltpu.VMEM)
SMEM = pl.BlockSpec(memory_space=pltpu.SMEM)


def one_hot(mask):
    return jnp.where(mask, 1.0, 0.0).astype(BF)


def call(kernel, outs, args, specs=None, flops=100_000_000, name=None, scratch=(), limit=48):
    return pl.pallas_call(
        kernel,
        out_shape=[jax.ShapeDtypeStruct(shape, dtype) for shape, dtype in outs],
        in_specs=specs or [VMEM] * len(args),
        out_specs=[VMEM] * len(outs),
        scratch_shapes=list(scratch),
        compiler_params=pltpu.CompilerParams(vmem_limit_bytes=limit * 1024 * 1024),
        cost_estimate=pl.CostEstimate(flops=flops, bytes_accessed=2_000_000, transcendentals=0),
        name=name,
    )(*args)


def small_rows(info_ref, rate_ref, gate_ref):
    rows = jnp.concatenate(
        [gate_ref[...].astype(F32), rate_ref[...].astype(F32), jnp.ones((6, N), F32)], axis=0
    )
    row, patch = iotas(16, N)
    return jnp.where((patch < info_ref[0]) & (row < 11), rows, 0.0)


def shuffle(by_column, inverse):
    i, j = iotas(144, 144)
    packed, plain = (j, i) if inverse else (i, j)
    peer = shr(packed * 3641, 16)
    rest = packed - 18 * peer
    c = rest & 1
    within = 8 * c + peer if by_column else 2 * peer + c
    return one_hot(plain == 16 * shr(rest, 1) + within)


def pack(parts, small, by_column, out_ref):
    parts = [part[:, h * N : (h + 1) * N].astype(F32) for part in parts for h in range(2)]
    parts.append(jnp.concatenate([small, jnp.zeros((N - 16, N), F32)], axis=0).T)
    order = shuffle(by_column, False)
    for b in range(8):
        if by_column:
            rows = [part[start + 8 * b : start + 8 * b + 8] for part in parts for start in (0, 64)]
        else:
            rows = [part[16 * b : 16 * b + 16] for part in parts]
        out_ref[144 * b : 144 * b + 144, :] = dot(order, jnp.concatenate(rows, axis=0)).astype(BF)


def unpack(got_ref, by_column, first=0, last=9):
    order = shuffle(by_column, True)[16 * first : 16 * last]
    blocks = [dot(order, got_ref[144 * b : 144 * b + 144, :]) for b in range(8)]
    parts = []
    for s in range(last - first):
        if by_column:
            rows = [block[16 * s + 8 * c : 16 * s + 8 * c + 8] for c in range(2) for block in blocks]
        else:
            rows = [block[16 * s : 16 * s + 16] for block in blocks]
        parts.append(jnp.concatenate(rows, axis=0))
    return parts


def heads_of(parts):
    return [jnp.concatenate(parts[2 * a : 2 * a + 2], axis=1) for a in range(len(parts) // 2)]


def pack_kernel(info_ref, rate_ref, gate_ref, q_ref, k_ref, v_ref, cot_ref, out_ref, held, sems):
    copies = [
        pltpu.make_async_copy(ref, held.at[a], sems.at[a])
        for a, ref in enumerate((q_ref, k_ref, v_ref, cot_ref))
    ]
    for copy in copies:
        copy.start()
    small = small_rows(info_ref, rate_ref, gate_ref)
    for copy in copies:
        copy.wait()
    pack([held[a] for a in range(4)], small, False, out_ref)


def row_kernel(
    info_ref, q_ref, k_ref, v_ref, rate_ref, gate_ref, cot_ref, w_ref, o_ref, gq_ref, gk_ref, gv_ref, gs_ref
):
    patch, unused = iotas(N, 2 * N)
    cot = jnp.where(patch < info_ref[0], dot(cot_ref[...], w_ref[...], 1, 1), 0.0).astype(BF)
    q, k, v = q_ref[...], k_ref[...], v_ref[...]
    small = small_rows(info_ref, rate_ref, gate_ref)
    ready = prepare(q, k, small, N, 0)
    outs, solved, errors = forward(ready, v, N)
    o_ref[...] = jnp.where(patch < info_ref[0], jnp.concatenate(outs, axis=1), 0.0)
    gq_ref[...], gk_ref[...], gv_ref[...], gs_ref[...] = backward(ready, solved, errors, q, k, small, cot, 0)


def unpack_kernel(got_ref, q_ref, k_ref, v_ref, copies_ref, small_ref):
    pieces = unpack(got_ref, True)
    parts, scalars = heads_of(pieces), pieces[8]
    for part, ref in zip(parts, (q_ref, k_ref, v_ref)):
        ref[...] = part.astype(BF)
    for x in range(4):
        copies_ref[x * N : (x + 1) * N, :] = parts[3].astype(BF)
    small_ref[...] = scalars.T[:16, :]


def tissue_of(small):
    return jnp.concatenate([small, jnp.zeros((N - 16, N), F32)], axis=0).T[:, 10:11] > 0.5


def column_forward_kernel(q_ref, k_ref, v_ref, small_ref, o_ref, t_ref, e_ref):
    small = small_ref[...]
    outs, solved, errors = forward(prepare(q_ref[...], k_ref[...], small, 64, 2), v_ref[...], 64)
    o_ref[...] = jnp.where(tissue_of(small), jnp.concatenate(outs, axis=1), 0.0).astype(BF)
    for s in range(4):
        t_ref[s], e_ref[s] = solved[s], errors[s]


def column_backward_kernel(q_ref, k_ref, small_ref, o_ref, t_ref, e_ref, cot_ref, w_ref, send_ref):
    total = 0.0
    for block in range(8):
        rows = ((block & 1) * 4 + (block >> 1)) * N
        total = total + dot(cot_ref[rows : rows + N, :], w_ref[:, block * 2 * N : (block + 1) * 2 * N], 1, 1)
    q, k, small = q_ref[...], k_ref[...], small_ref[...]
    cot = jnp.where(tissue_of(small), total, 0.0).astype(BF)
    solved = [t_ref[s] for s in range(4)]
    errors = [e_ref[s] for s in range(4)]
    gq, gk, gv, gs = backward(prepare(q, k, small, 64, 2), solved, errors, q, k, small, cot, 2)
    pack([o_ref[...], gq, gk, gv], gs, True, send_ref)


def weight_kernel(
    info_ref, row_cot_ref, row_o_ref, col_cot_ref, col_o_ref, own_ref, first_ref, second_ref, third_ref, part_ref
):
    hidden = jnp.concatenate([row_o_ref[...].astype(BF), col_o_ref[...]], axis=0)
    for z in range(16):
        block, half = z >> 1, z & 1
        rows = ((block & 1) * 4 + (block >> 1)) * N
        col_cot = col_cot_ref[rows : rows + N, half * N : (half + 1) * N]
        cot = jnp.concatenate([row_cot_ref[:, z * N : (z + 1) * N], col_cot], axis=0)
        part_ref[z] = dot(cot, hidden, 0, 0)
    for step, ref in enumerate((own_ref, first_ref, second_ref, third_ref)):
        start = pl.multiple_of(((info_ref[3] + step) & 3) * 32, 32)
        for z in range(16):
            ref[z * 32 : (z + 1) * 32, :] = part_ref[z, pl.ds(start, 32), :].astype(BF)


def projection_kernel(info_ref, w_ref, own_ref, other_ref):
    place, core = info_ref[1], info_ref[2]
    for step in range(4):
        for ref, side in ((own_ref, core), (other_ref, 1 - core)):
            block = 2 * ((place + step) & 3) + side
            lanes = pl.ds(pl.multiple_of(block * 2 * N, 2 * N), 2 * N)
            ref[step] = w_ref[:, lanes]


def hidden_kernel(got_ref, o_ref, hidden_ref):
    (col,) = heads_of(unpack(got_ref, False, 0, 2))
    hidden_ref[...] = (o_ref[...] + col).astype(BF)


def gradient_kernel(
    info_ref, got_ref, gq_ref, gk_ref, gv_ref, gs_ref, q_ref, k_ref, v_ref, rate_ref, gate_ref
):
    pieces = unpack(got_ref, False, 2, 9)
    parts, scalars = heads_of(pieces), pieces[6]
    for part, row_ref, out_ref in zip(parts, (gq_ref, gk_ref, gv_ref), (q_ref, k_ref, v_ref)):
        out_ref[...] = (row_ref[...] + part).astype(BF)
    unused, patch = iotas(16, N)
    small = jnp.where(patch < info_ref[0], gs_ref[...] + scalars.T[:16, :], 0.0)
    gate_ref[...] = small[:8, :]
    rate_ref[...] = small[8:10, :]


def encode_kernel(info_ref, hidden_ref, own_ref, swapped_ref, kept_ref, sent_ref):
    core = info_ref[2]
    mine = hidden_ref[pl.ds(pl.multiple_of(core * N, N), N), :]
    other = hidden_ref[pl.ds(pl.multiple_of((1 - core) * N, N), N), :]
    for step in range(4):
        part = dot(mine, own_ref[step]) + dot(other, swapped_ref[step])
        if step == 0:
            kept_ref[...] = part
        else:
            sent_ref[step - 1] = part.astype(BF)


def exchange(x, axis, groups=None):
    return lax.all_to_all(x, axis, split_axis=0, concat_axis=0, tiled=True, axis_index_groups=groups)


def swap_rows(x):
    return exchange(x.reshape(64, 9, 2, N), "rows").reshape(18 * 64, N)


def per_device(
    query_proj, key_proj, value_proj, write_rate, log_gate, tissue_lengths, out_weight, cotangent
):
    q, k, v = query_proj[0], key_proj[0], value_proj[0]
    rate = write_rate[0].T
    gate = log_gate[0].transpose(1, 2, 0).reshape(8, N)
    me = lax.axis_index("heads")
    info = jnp.stack([tissue_lengths[0], lax.shift_right_logical(me, 1), me & 1, lax.axis_index("rows") & 3])
    wide, few = (N, 2 * N), (16, N)

    (send,) = call(
        pack_kernel,
        [((18 * 64, N), BF)],
        [tissue_lengths, rate, gate, q, k, v, cotangent[0]],
        [SMEM, VMEM, VMEM] + [pl.BlockSpec(memory_space=pl.ANY)] * 4,
        name="pack",
        scratch=[pltpu.VMEM((4, N, 2 * N), BF), pltpu.SemaphoreType.DMA((4,))],
        limit=62,
    )
    got = swap_rows(send)
    row_cot = lax.all_gather(cotangent[0], "heads", axis=1, tiled=True)
    weight, unused = lax.optimization_barrier((out_weight, row_cot))
    block = (4, 2 * N, 2 * N)
    own, other = call(projection_kernel, [(block, BF)] * 2, [info, weight], [SMEM, VMEM], name="projection")
    swapped = lax.ppermute(other, "heads", [(i, i ^ 1) for i in range(8)])
    o_row, gq, gk, gv, gs = call(
        row_kernel,
        [(wide, F32)] * 4 + [(few, F32)],
        [info, q, k, v, rate, gate, row_cot, out_weight],
        [SMEM] + [VMEM] * 7,
        flops=6_000_000_000,
        name="row_directions",
    )
    got, swapped, o_row = lax.optimization_barrier((got, swapped, o_row))
    qc, kc, vc, copies, sc = call(
        unpack_kernel,
        [(wide, BF)] * 3 + [((4 * N, 2 * N), BF), (few, F32)],
        [got],
        name="unpack",
    )
    x_groups = [[2 * x + core for x in range(4)] for core in range(2)]
    pairs = [[2 * x, 2 * x + 1] for x in range(4)]
    along_x = exchange(copies, "heads", x_groups)
    col_cot = lax.all_gather(along_x, "heads", axis=0, tiled=True, axis_index_groups=pairs)
    o_col, tc, ec = call(
        column_forward_kernel,
        [(wide, BF)] + [((4, N, N), BF)] * 2,
        [qc, kc, vc, sc],
        flops=3_000_000_000,
        name="column_forward",
    )
    (send,) = call(
        column_backward_kernel,
        [((18 * 64, N), BF)],
        [qc, kc, sc, o_col, tc, ec, col_cot, out_weight],
        flops=3_000_000_000,
        name="column_backward",
    )
    got = swap_rows(send)
    own_wg, *sent_wg = call(
        weight_kernel,
        [((4 * N, 2 * N), BF)] * 4,
        [info, row_cot, o_row, col_cot, o_col],
        [SMEM] + [VMEM] * 4,
        flops=2_000_000_000,
        name="weight_gradient",
        scratch=[pltpu.VMEM((16, N, 2 * N), F32)],
    )
    summed = own_wg.astype(F32)
    for step in range(1, 4):
        moves = [(z * 4 + y, z * 4 + (y + step) % 4) for z in range(16) for y in range(4)]
        summed = summed + lax.ppermute(sent_wg[step - 1], "rows", moves).astype(F32)
    summed = summed.astype(BF)
    z_groups = [[z * 4 + y for z in range(16)] for y in range(4)]
    (hidden,) = call(hidden_kernel, [(wide, BF)], [got, o_row], name="hidden")
    hidden = lax.all_gather(hidden, "heads", axis=0, tiled=True, axis_index_groups=pairs)
    encoded, sent = call(
        encode_kernel,
        [(wide, F32), ((3, N, 2 * N), BF)],
        [info, hidden, own, swapped],
        [SMEM] + [VMEM] * 3,
        flops=1_000_000_000,
        name="encode",
    )
    for step in range(1, 4):
        moves = [(i, ((i // 2 + step) % 4) * 2 + i % 2) for i in range(8)]
        encoded = encoded + lax.ppermute(sent[step - 1], "heads", moves).astype(F32)
    encoded = encoded.astype(BF)[None]
    grad_q, grad_k, grad_v, grad_rate, grad_gate = call(
        gradient_kernel,
        [(wide, BF)] * 3 + [((2, N), F32), ((8, N), F32)],
        [info, got, gq, gk, gv, gs],
        [SMEM] + [VMEM] * 5,
        flops=1_000_000_000,
        name="gradients",
    )

    pieces = exchange(summed, "rows", z_groups)
    weight_grad = jnp.sum(pieces.reshape(16, 32, 2 * N).astype(F32), axis=0)
    rate_grad = grad_rate.T[None]
    gate_grad = grad_gate.reshape(2, 4, N).transpose(2, 0, 1)[None]
    return (encoded, grad_q[None], grad_k[None], grad_v[None], rate_grad, gate_grad, weight_grad)


def solution(mesh):
    in_specs = (
        P("rows", None, "heads"),
        P("rows", None, "heads"),
        P("rows", None, "heads"),
        P("rows", None, "heads"),
        P("rows", None, "heads", None),
        P("rows"),
        P("heads", None),
        P("rows", None, "heads"),
    )
    out_specs = (
        P("rows", None, "heads"),
        P("rows", None, "heads"),
        P("rows", None, "heads"),
        P("rows", None, "heads"),
        P("rows", None, "heads"),
        P("rows", None, "heads", None),
        P("rows", "heads"),
    )
    return jax.shard_map(
        per_device, mesh=mesh, in_specs=in_specs, out_specs=out_specs, check_vma=False
    )
```

```python
import functools

import jax
import jax.numpy as jnp
from jax import lax
from jax.experimental import pallas as pl
from jax.experimental.pallas import tpu as pltpu
from jax.sharding import PartitionSpec as P

N = 128
F32 = jnp.float32
BF = jnp.bfloat16


def dot(a, b, ca=1, cb=0):
    return lax.dot_general(a.astype(BF), b.astype(BF), (((ca,), (cb,)), ((), ())), preferred_element_type=F32)


def iotas(rows=N, cols=N):
    return lax.broadcasted_iota(jnp.int32, (rows, cols), 0), lax.broadcasted_iota(jnp.int32, (rows, cols), 1)


def shr(x, n):
    return lax.shift_right_logical(x, jnp.int32(n))


def invert(systems, length):
    i, j = iotas()
    apart = i ^ j
    eye = jnp.where(apart == 0, 1.0, 0.0)
    solved = [eye - jnp.where(apart == 1, a, 0.0) for a in systems]
    level = 1
    while (2 << level) <= length:
        mask = shr(apart, level) == 1
        crossing = [jnp.where(mask, a, 0.0).astype(BF) for a in systems]
        halves = [t.astype(BF) for t in solved]
        inner = [dot(c, t) for c, t in zip(crossing, halves)]
        solved = [t - dot(h, m) for t, h, m in zip(solved, halves, inner)]
        level += 1
    return solved


def split3(x):
    hi = x.astype(BF)
    rest = x - hi.astype(F32)
    mid = rest.astype(BF)
    return hi, mid, (rest - mid.astype(F32)).astype(BF)


def prefix_sums(length):
    i, j = iotas()
    shift = length.bit_length() - 1
    same = shr(i, shift) == shr(j, shift)
    before = [same & (i >= j), same & (i <= j)]
    return [jnp.where(m, 1.0, 0.0).astype(BF) for m in before], before, i == j


def prepare(q, k, small, length, first):
    sums, before, eye = prefix_sums(length)
    cum = [dot(m, small, 1, 1) for m in sums]
    cum_t = [dot(small, m, 1, 1) for m in sums]
    heads = []
    for h in range(2):
        lanes = slice(h * N, (h + 1) * N)
        kh, qh = k[:, lanes], q[:, lanes]
        gram = dot(kh, kh, 1, 1)
        cross = dot(qh, kh, 1, 1)
        diag = jnp.where(eye, gram, 0.0)
        s_col = lax.rsqrt(jnp.sum(diag, axis=1, keepdims=True) + 1e-6)
        s_row = lax.rsqrt(jnp.sum(diag, axis=0, keepdims=True) + 1e-6)
        gram = gram * (s_col * s_row)
        cross = cross * (s_row * (N ** -0.5))
        rate_row = small[8 + h : 9 + h, :]
        per = []
        for d in range(2):
            g = 4 * h + first + d
            ratio = cum[d][:, g : g + 1] - cum_t[d][g : g + 1, :]
            weight = jnp.exp(jnp.where(before[d], ratio, -jnp.inf)) * rate_row
            strict = jnp.where(eye, 0.0, weight)
            per.append((weight, strict, strict * gram, weight * cross))
        heads.append((s_col, s_row, per))
    return sums, heads


def forward(prepared, v, length):
    sums, heads = prepared
    systems = [p[2] for hd in heads for p in hd[2]]
    solved = [t.astype(BF) for t in invert(systems, length)]
    outs, errors = [], []
    for h in range(2):
        vh = v[:, h * N : (h + 1) * N]
        es = [dot(solved[2 * h + d], vh).astype(BF) for d in range(2)]
        mix = jnp.concatenate([heads[h][2][0][3].astype(BF), heads[h][2][1][3].astype(BF)], axis=1)
        outs.append(dot(mix, jnp.concatenate(es, axis=0)))
        errors += es
    return outs, solved, errors


def backward(prepared, solved, errors, q, k, small, cot, first):
    sums, heads = prepared
    i, j = iotas()
    gq, gk, gv, rowsums, colsums = [], [], [], [], []
    for h in range(2):
        lanes = slice(h * N, (h + 1) * N)
        s_col, s_row, per = heads[h]
        c, kh, qh = cot[:, lanes], k[:, lanes], q[:, lanes]
        es = errors[2 * h : 2 * h + 2]
        d_mix = dot(c, jnp.concatenate(es, axis=0), 1, 1)
        mix = jnp.concatenate([per[0][3].astype(BF), per[1][3].astype(BF)], axis=1)
        d_err = dot(mix, c, 0, 0)
        d_val = [dot(solved[2 * h + d], d_err[d * N : (d + 1) * N], 0, 0) for d in range(2)]
        d_sys = [-dot(d_val[d], es[d], 1, 1) for d in range(2)]
        d_gram, d_cross = 0.0, 0.0
        for d in range(2):
            weight, strict, system, mixing = per[d]
            dm = d_mix[:, d * N : (d + 1) * N]
            d_gram = d_gram + d_sys[d] * strict
            d_cross = d_cross + dm * weight
            total = d_sys[d] * system + dm * mixing
            rowsums.append(jnp.sum(total, axis=1, keepdims=True))
            colsums.append(jnp.sum(total, axis=0, keepdims=True))
        both = d_gram + d_gram.T
        gq.append(dot(d_cross * (s_row * (N ** -0.5)), kh))
        kf = kh.astype(F32)
        d_kn = dot(both * s_row, kh) + dot(d_cross, qh, 0, 0) * (N ** -0.5)
        along = s_col * jnp.sum(kf * d_kn, axis=1, keepdims=True)
        gk.append(s_col * (d_kn - kf * (s_col * along)))
        gv.append(d_val[0] + d_val[1])
    across = jnp.zeros((N, N), F32)
    for s in range(4):
        across = jnp.where(j == s, rowsums[s], across)
    d_cum = across.T[:8, :] - jnp.concatenate(colsums + [jnp.zeros((4, N), F32)], axis=0)
    pieces = split3(d_cum)
    gates = [sum(dot(p, sums[1 - d], 1, 1) for p in pieces) for d in range(2)]
    zero = jnp.zeros((1, N), F32)
    out = [zero] * 16
    for h in range(2):
        rate = small[8 + h : 9 + h, :]
        whole = colsums[2 * h] + colsums[2 * h + 1]
        out[8 + h] = jnp.where(rate > 0, whole / jnp.where(rate > 0, rate, 1.0), 0.0)
        for d in range(2):
            s = 2 * h + d
            out[4 * h + first + d] = gates[d][s : s + 1, :]
    out = jnp.concatenate(out, axis=0)
    return jnp.concatenate(gq, axis=1), jnp.concatenate(gk, axis=1), jnp.concatenate(gv, axis=1), out


VMEM = pl.BlockSpec(memory_space=pltpu.VMEM)
SMEM = pl.BlockSpec(memory_space=pltpu.SMEM)


def one_hot(mask):
    return jnp.where(mask, 1.0, 0.0).astype(BF)


def call(kernel, outs, args, specs=None, flops=100_000_000, name=None, scratch=(), limit=48):
    return pl.pallas_call(
        kernel,
        out_shape=[jax.ShapeDtypeStruct(shape, dtype) for shape, dtype in outs],
        in_specs=specs or [VMEM] * len(args),
        out_specs=[VMEM] * len(outs),
        scratch_shapes=list(scratch),
        compiler_params=pltpu.CompilerParams(vmem_limit_bytes=limit * 1024 * 1024),
        cost_estimate=pl.CostEstimate(flops=flops, bytes_accessed=2_000_000, transcendentals=0),
        name=name,
    )(*args)


def small_rows(info_ref, rate_ref, gate_ref):
    rows = jnp.concatenate(
        [gate_ref[...].astype(F32), rate_ref[...].astype(F32), jnp.ones((6, N), F32)], axis=0
    )
    row, patch = iotas(16, N)
    return jnp.where((patch < info_ref[0]) & (row < 11), rows, 0.0)


def shuffle(by_column, inverse):
    i, j = iotas(144, 144)
    packed, plain = (j, i) if inverse else (i, j)
    peer = shr(packed * 3641, 16)
    rest = packed - 18 * peer
    c = rest & 1
    within = 8 * c + peer if by_column else 2 * peer + c
    return one_hot(plain == 16 * shr(rest, 1) + within)


def pack(parts, small, by_column, out_ref):
    parts = [part[:, h * N : (h + 1) * N].astype(F32) for part in parts for h in range(2)]
    parts.append(jnp.concatenate([small, jnp.zeros((N - 16, N), F32)], axis=0).T)
    order = shuffle(by_column, False)
    for b in range(8):
        if by_column:
            rows = [part[start + 8 * b : start + 8 * b + 8] for part in parts for start in (0, 64)]
        else:
            rows = [part[16 * b : 16 * b + 16] for part in parts]
        out_ref[144 * b : 144 * b + 144, :] = dot(order, jnp.concatenate(rows, axis=0)).astype(BF)


def unpack(got_ref, by_column, first=0, last=9):
    order = shuffle(by_column, True)[16 * first : 16 * last]
    blocks = [dot(order, got_ref[144 * b : 144 * b + 144, :]) for b in range(8)]
    parts = []
    for s in range(last - first):
        if by_column:
            rows = [block[16 * s + 8 * c : 16 * s + 8 * c + 8] for c in range(2) for block in blocks]
        else:
            rows = [block[16 * s : 16 * s + 16] for block in blocks]
        parts.append(jnp.concatenate(rows, axis=0))
    return parts


def heads_of(parts):
    return [jnp.concatenate(parts[2 * a : 2 * a + 2], axis=1) for a in range(len(parts) // 2)]


def pack_kernel(info_ref, rate_ref, gate_ref, q_ref, k_ref, v_ref, cot_ref, out_ref, held, sems):
    copies = [
        pltpu.make_async_copy(ref, held.at[a], sems.at[a])
        for a, ref in enumerate((q_ref, k_ref, v_ref, cot_ref))
    ]
    for copy in copies:
        copy.start()
    small = small_rows(info_ref, rate_ref, gate_ref)
    for copy in copies:
        copy.wait()
    pack([held[a] for a in range(4)], small, False, out_ref)


def row_forward_kernel(info_ref, q_ref, k_ref, v_ref, rate_ref, gate_ref, o_ref, t_ref, e_ref):
    patch, unused = iotas(N, 2 * N)
    small = small_rows(info_ref, rate_ref, gate_ref)
    outs, solved, errors = forward(prepare(q_ref[...], k_ref[...], small, N, 0), v_ref[...], N)
    o_ref[...] = jnp.where(patch < info_ref[0], jnp.concatenate(outs, axis=1), 0.0)
    for s in range(4):
        t_ref[s], e_ref[s] = solved[s], errors[s]


def row_backward_kernel(
    info_ref, q_ref, k_ref, rate_ref, gate_ref, t_ref, e_ref, cot_ref, w_ref, gq_ref, gk_ref, gv_ref, gs_ref
):
    patch, unused = iotas(N, 2 * N)
    cot = jnp.where(patch < info_ref[0], dot(cot_ref[...], w_ref[...], 1, 1), 0.0).astype(BF)
    q, k = q_ref[...], k_ref[...]
    small = small_rows(info_ref, rate_ref, gate_ref)
    solved = [t_ref[s] for s in range(4)]
    errors = [e_ref[s] for s in range(4)]
    ready = prepare(q, k, small, N, 0)
    gq_ref[...], gk_ref[...], gv_ref[...], gs_ref[...] = backward(ready, solved, errors, q, k, small, cot, 0)


def unpack_kernel(got_ref, q_ref, k_ref, v_ref, copies_ref, small_ref):
    pieces = unpack(got_ref, True)
    parts, scalars = heads_of(pieces), pieces[8]
    for part, ref in zip(parts, (q_ref, k_ref, v_ref)):
        ref[...] = part.astype(BF)
    for x in range(4):
        copies_ref[x * N : (x + 1) * N, :] = parts[3].astype(BF)
    small_ref[...] = scalars.T[:16, :]


def tissue_of(small):
    return jnp.concatenate([small, jnp.zeros((N - 16, N), F32)], axis=0).T[:, 10:11] > 0.5


def column_forward_kernel(q_ref, k_ref, v_ref, small_ref, o_ref, t_ref, e_ref):
    small = small_ref[...]
    outs, solved, errors = forward(prepare(q_ref[...], k_ref[...], small, 64, 2), v_ref[...], 64)
    o_ref[...] = jnp.where(tissue_of(small), jnp.concatenate(outs, axis=1), 0.0).astype(BF)
    for s in range(4):
        t_ref[s], e_ref[s] = solved[s], errors[s]


def column_backward_kernel(q_ref, k_ref, small_ref, o_ref, t_ref, e_ref, cot_ref, w_ref, send_ref):
    total = 0.0
    for block in range(8):
        rows = ((block & 1) * 4 + (block >> 1)) * N
        total = total + dot(cot_ref[rows : rows + N, :], w_ref[:, block * 2 * N : (block + 1) * 2 * N], 1, 1)
    q, k, small = q_ref[...], k_ref[...], small_ref[...]
    cot = jnp.where(tissue_of(small), total, 0.0).astype(BF)
    solved = [t_ref[s] for s in range(4)]
    errors = [e_ref[s] for s in range(4)]
    gq, gk, gv, gs = backward(prepare(q, k, small, 64, 2), solved, errors, q, k, small, cot, 2)
    pack([o_ref[...], gq, gk, gv], gs, True, send_ref)


def weight_kernel(
    info_ref, row_cot_ref, row_o_ref, col_cot_ref, col_o_ref, own_ref, first_ref, second_ref, third_ref, part_ref
):
    hidden = jnp.concatenate([row_o_ref[...].astype(BF), col_o_ref[...]], axis=0)
    for z in range(16):
        block, half = z >> 1, z & 1
        rows = ((block & 1) * 4 + (block >> 1)) * N
        col_cot = col_cot_ref[rows : rows + N, half * N : (half + 1) * N]
        cot = jnp.concatenate([row_cot_ref[:, z * N : (z + 1) * N], col_cot], axis=0)
        part_ref[z] = dot(cot, hidden, 0, 0)
    for step, ref in enumerate((own_ref, first_ref, second_ref, third_ref)):
        start = pl.multiple_of(((info_ref[3] + step) & 3) * 32, 32)
        for z in range(16):
            ref[z * 32 : (z + 1) * 32, :] = part_ref[z, pl.ds(start, 32), :].astype(BF)


def projection_kernel(info_ref, w_ref, own_ref, other_ref):
    place, core = info_ref[1], info_ref[2]
    for step in range(4):
        for ref, side in ((own_ref, core), (other_ref, 1 - core)):
            block = 2 * ((place + step) & 3) + side
            lanes = pl.ds(pl.multiple_of(block * 2 * N, 2 * N), 2 * N)
            ref[step] = w_ref[:, lanes]


def hidden_kernel(got_ref, o_ref, hidden_ref):
    (col,) = heads_of(unpack(got_ref, False, 0, 2))
    hidden_ref[...] = (o_ref[...] + col).astype(BF)


def gradient_kernel(
    info_ref, got_ref, gq_ref, gk_ref, gv_ref, gs_ref, q_ref, k_ref, v_ref, rate_ref, gate_ref
):
    pieces = unpack(got_ref, False, 2, 9)
    parts, scalars = heads_of(pieces), pieces[6]
    for part, row_ref, out_ref in zip(parts, (gq_ref, gk_ref, gv_ref), (q_ref, k_ref, v_ref)):
        out_ref[...] = (row_ref[...] + part).astype(BF)
    unused, patch = iotas(16, N)
    small = jnp.where(patch < info_ref[0], gs_ref[...] + scalars.T[:16, :], 0.0)
    gate_ref[...] = small[:8, :]
    rate_ref[...] = small[8:10, :]


def encode_kernel(info_ref, hidden_ref, own_ref, swapped_ref, kept_ref, sent_ref):
    core = info_ref[2]
    mine = hidden_ref[pl.ds(pl.multiple_of(core * N, N), N), :]
    other = hidden_ref[pl.ds(pl.multiple_of((1 - core) * N, N), N), :]
    for step in range(4):
        part = dot(mine, own_ref[step]) + dot(other, swapped_ref[step])
        if step == 0:
            kept_ref[...] = part
        else:
            sent_ref[step - 1] = part.astype(BF)


def exchange(x, axis, groups=None):
    return lax.all_to_all(x, axis, split_axis=0, concat_axis=0, tiled=True, axis_index_groups=groups)


def swap_rows(x):
    return exchange(x.reshape(64, 9, 2, N), "rows").reshape(18 * 64, N)


def per_device(
    query_proj, key_proj, value_proj, write_rate, log_gate, tissue_lengths, out_weight, cotangent
):
    q, k, v = query_proj[0], key_proj[0], value_proj[0]
    rate = write_rate[0].T
    gate = log_gate[0].transpose(1, 2, 0).reshape(8, N)
    me = lax.axis_index("heads")
    info = jnp.stack([tissue_lengths[0], lax.shift_right_logical(me, 1), me & 1, lax.axis_index("rows") & 3])
    wide, few = (N, 2 * N), (16, N)

    (send,) = call(
        pack_kernel,
        [((18 * 64, N), BF)],
        [tissue_lengths, rate, gate, q, k, v, cotangent[0]],
        [SMEM, VMEM, VMEM] + [pl.BlockSpec(memory_space=pl.ANY)] * 4,
        name="pack",
        scratch=[pltpu.VMEM((4, N, 2 * N), BF), pltpu.SemaphoreType.DMA((4,))],
        limit=62,
    )
    got = swap_rows(send)
    row_cot = lax.all_gather(cotangent[0], "heads", axis=1, tiled=True)
    got, row_cot = lax.optimization_barrier((got, row_cot))
    qc, kc, vc, copies, sc = call(
        unpack_kernel,
        [(wide, BF)] * 3 + [((4 * N, 2 * N), BF), (few, F32)],
        [got],
        name="unpack",
    )
    x_groups = [[2 * x + core for x in range(4)] for core in range(2)]
    pairs = [[2 * x, 2 * x + 1] for x in range(4)]
    along_x = exchange(copies, "heads", x_groups)
    col_cot = lax.all_gather(along_x, "heads", axis=0, tiled=True, axis_index_groups=pairs)
    rate_late, unused = lax.optimization_barrier((rate, sc))
    o_row, tr, er = call(
        row_forward_kernel,
        [(wide, F32)] + [((4, N, N), BF)] * 2,
        [info, q, k, v, rate_late, gate],
        [SMEM] + [VMEM] * 5,
        flops=3_000_000_000,
        name="row_forward",
    )
    o_col, tc, ec = call(
        column_forward_kernel,
        [(wide, BF)] + [((4, N, N), BF)] * 2,
        [qc, kc, vc, sc],
        flops=3_000_000_000,
        name="column_forward",
    )
    (send,) = call(
        column_backward_kernel,
        [((18 * 64, N), BF)],
        [qc, kc, sc, o_col, tc, ec, col_cot, out_weight],
        flops=3_000_000_000,
        name="column_backward",
    )
    got = swap_rows(send)
    own_wg, *sent_wg = call(
        weight_kernel,
        [((4 * N, 2 * N), BF)] * 4,
        [info, row_cot, o_row, col_cot, o_col],
        [SMEM] + [VMEM] * 4,
        flops=2_000_000_000,
        name="weight_gradient",
        scratch=[pltpu.VMEM((16, N, 2 * N), F32)],
    )
    rate_late, weight, unused = lax.optimization_barrier((rate, out_weight, own_wg))
    gq, gk, gv, gs = call(
        row_backward_kernel,
        [(wide, F32)] * 3 + [(few, F32)],
        [info, q, k, rate_late, gate, tr, er, row_cot, out_weight],
        [SMEM] + [VMEM] * 8,
        flops=3_000_000_000,
        name="row_backward",
    )
    block = (4, 2 * N, 2 * N)
    own, other = call(projection_kernel, [(block, BF)] * 2, [info, weight], [SMEM, VMEM], name="projection")
    swapped = lax.ppermute(other, "heads", [(i, i ^ 1) for i in range(8)])
    summed = own_wg.astype(F32)
    for step in range(1, 4):
        moves = [(z * 4 + y, z * 4 + (y + step) % 4) for z in range(16) for y in range(4)]
        summed = summed + lax.ppermute(sent_wg[step - 1], "rows", moves).astype(F32)
    summed = summed.astype(BF)
    z_groups = [[z * 4 + y for z in range(16)] for y in range(4)]
    (hidden,) = call(hidden_kernel, [(wide, BF)], [got, o_row], name="hidden")
    hidden = lax.all_gather(hidden, "heads", axis=0, tiled=True, axis_index_groups=pairs)
    encoded, sent = call(
        encode_kernel,
        [(wide, F32), ((3, N, 2 * N), BF)],
        [info, hidden, own, swapped],
        [SMEM] + [VMEM] * 3,
        flops=1_000_000_000,
        name="encode",
    )
    for step in range(1, 4):
        moves = [(i, ((i // 2 + step) % 4) * 2 + i % 2) for i in range(8)]
        encoded = encoded + lax.ppermute(sent[step - 1], "heads", moves).astype(F32)
    encoded = encoded.astype(BF)[None]
    grad_q, grad_k, grad_v, grad_rate, grad_gate = call(
        gradient_kernel,
        [(wide, BF)] * 3 + [((2, N), F32), ((8, N), F32)],
        [info, got, gq, gk, gv, gs],
        [SMEM] + [VMEM] * 5,
        flops=1_000_000_000,
        name="gradients",
    )

    pieces = exchange(summed, "rows", z_groups)
    weight_grad = jnp.sum(pieces.reshape(16, 32, 2 * N).astype(F32), axis=0)
    rate_grad = grad_rate.T[None]
    gate_grad = grad_gate.reshape(2, 4, N).transpose(2, 0, 1)[None]
    return (encoded, grad_q[None], grad_k[None], grad_v[None], rate_grad, gate_grad, weight_grad)


def solution(mesh):
    in_specs = (
        P("rows", None, "heads"),
        P("rows", None, "heads"),
        P("rows", None, "heads"),
        P("rows", None, "heads"),
        P("rows", None, "heads", None),
        P("rows"),
        P("heads", None),
        P("rows", None, "heads"),
    )
    out_specs = (
        P("rows", None, "heads"),
        P("rows", None, "heads"),
        P("rows", None, "heads"),
        P("rows", None, "heads"),
        P("rows", None, "heads"),
        P("rows", None, "heads", None),
        P("rows", "heads"),
    )
    return jax.shard_map(
        per_device, mesh=mesh, in_specs=in_specs, out_specs=out_specs, check_vma=False
    )
```

```python
import functools

import jax
import jax.numpy as jnp
from jax import lax
from jax.experimental import pallas as pl
from jax.experimental.pallas import tpu as pltpu
from jax.sharding import PartitionSpec as P

N = 128
F32 = jnp.float32
BF = jnp.bfloat16


def dot(a, b, ca=1, cb=0):
    return lax.dot_general(a.astype(BF), b.astype(BF), (((ca,), (cb,)), ((), ())), preferred_element_type=F32)


def iotas(rows=N, cols=N):
    return lax.broadcasted_iota(jnp.int32, (rows, cols), 0), lax.broadcasted_iota(jnp.int32, (rows, cols), 1)


def shr(x, n):
    return lax.shift_right_logical(x, jnp.int32(n))


def invert(systems, length):
    i, j = iotas()
    apart = i ^ j
    eye = jnp.where(apart == 0, 1.0, 0.0)
    solved = [eye - jnp.where(apart == 1, a, 0.0) for a in systems]
    level = 1
    while (2 << level) <= length:
        mask = shr(apart, level) == 1
        crossing = [jnp.where(mask, a, 0.0).astype(BF) for a in systems]
        halves = [t.astype(BF) for t in solved]
        inner = [dot(c, t) for c, t in zip(crossing, halves)]
        solved = [t - dot(h, m) for t, h, m in zip(solved, halves, inner)]
        level += 1
    return solved


def split3(x):
    hi = x.astype(BF)
    rest = x - hi.astype(F32)
    mid = rest.astype(BF)
    return hi, mid, (rest - mid.astype(F32)).astype(BF)


def prefix_sums(length):
    i, j = iotas()
    shift = length.bit_length() - 1
    same = shr(i, shift) == shr(j, shift)
    before = [same & (i >= j), same & (i <= j)]
    return [jnp.where(m, 1.0, 0.0).astype(BF) for m in before], before, i == j


def prepare(q, k, small, length, first):
    sums, before, eye = prefix_sums(length)
    cum = [dot(m, small, 1, 1) for m in sums]
    cum_t = [dot(small, m, 1, 1) for m in sums]
    heads = []
    for h in range(2):
        lanes = slice(h * N, (h + 1) * N)
        kh, qh = k[:, lanes], q[:, lanes]
        gram = dot(kh, kh, 1, 1)
        cross = dot(qh, kh, 1, 1)
        diag = jnp.where(eye, gram, 0.0)
        s_col = lax.rsqrt(jnp.sum(diag, axis=1, keepdims=True) + 1e-6)
        s_row = lax.rsqrt(jnp.sum(diag, axis=0, keepdims=True) + 1e-6)
        gram = gram * (s_col * s_row)
        cross = cross * (s_row * (N ** -0.5))
        rate_row = small[8 + h : 9 + h, :]
        per = []
        for d in range(2):
            g = 4 * h + first + d
            ratio = cum[d][:, g : g + 1] - cum_t[d][g : g + 1, :]
            weight = jnp.exp(jnp.where(before[d], ratio, -jnp.inf)) * rate_row
            strict = jnp.where(eye, 0.0, weight)
            per.append((weight, strict, strict * gram, weight * cross))
        heads.append((s_col, s_row, per))
    return sums, heads


def forward(prepared, v, length):
    sums, heads = prepared
    systems = [p[2] for hd in heads for p in hd[2]]
    solved = [t.astype(BF) for t in invert(systems, length)]
    outs, errors = [], []
    for h in range(2):
        vh = v[:, h * N : (h + 1) * N]
        es = [dot(solved[2 * h + d], vh).astype(BF) for d in range(2)]
        mix = jnp.concatenate([heads[h][2][0][3].astype(BF), heads[h][2][1][3].astype(BF)], axis=1)
        outs.append(dot(mix, jnp.concatenate(es, axis=0)))
        errors += es
    return outs, solved, errors


def backward(prepared, solved, errors, q, k, small, cot, first):
    sums, heads = prepared
    i, j = iotas()
    gq, gk, gv, rowsums, colsums = [], [], [], [], []
    for h in range(2):
        lanes = slice(h * N, (h + 1) * N)
        s_col, s_row, per = heads[h]
        c, kh, qh = cot[:, lanes], k[:, lanes], q[:, lanes]
        es = errors[2 * h : 2 * h + 2]
        d_mix = dot(c, jnp.concatenate(es, axis=0), 1, 1)
        mix = jnp.concatenate([per[0][3].astype(BF), per[1][3].astype(BF)], axis=1)
        d_err = dot(mix, c, 0, 0)
        d_val = [dot(solved[2 * h + d], d_err[d * N : (d + 1) * N], 0, 0) for d in range(2)]
        d_sys = [-dot(d_val[d], es[d], 1, 1) for d in range(2)]
        d_gram, d_cross = 0.0, 0.0
        for d in range(2):
            weight, strict, system, mixing = per[d]
            dm = d_mix[:, d * N : (d + 1) * N]
            d_gram = d_gram + d_sys[d] * strict
            d_cross = d_cross + dm * weight
            total = d_sys[d] * system + dm * mixing
            rowsums.append(jnp.sum(total, axis=1, keepdims=True))
            colsums.append(jnp.sum(total, axis=0, keepdims=True))
        both = d_gram + d_gram.T
        gq.append(dot(d_cross * (s_row * (N ** -0.5)), kh))
        kf = kh.astype(F32)
        d_kn = dot(both * s_row, kh) + dot(d_cross, qh, 0, 0) * (N ** -0.5)
        along = s_col * jnp.sum(kf * d_kn, axis=1, keepdims=True)
        gk.append(s_col * (d_kn - kf * (s_col * along)))
        gv.append(d_val[0] + d_val[1])
    across = jnp.zeros((N, N), F32)
    for s in range(4):
        across = jnp.where(j == s, rowsums[s], across)
    d_cum = across.T[:8, :] - jnp.concatenate(colsums + [jnp.zeros((4, N), F32)], axis=0)
    pieces = split3(d_cum)
    gates = [sum(dot(p, sums[1 - d], 1, 1) for p in pieces) for d in range(2)]
    zero = jnp.zeros((1, N), F32)
    out = [zero] * 16
    for h in range(2):
        rate = small[8 + h : 9 + h, :]
        whole = colsums[2 * h] + colsums[2 * h + 1]
        out[8 + h] = jnp.where(rate > 0, whole / jnp.where(rate > 0, rate, 1.0), 0.0)
        for d in range(2):
            s = 2 * h + d
            out[4 * h + first + d] = gates[d][s : s + 1, :]
    out = jnp.concatenate(out, axis=0)
    return jnp.concatenate(gq, axis=1), jnp.concatenate(gk, axis=1), jnp.concatenate(gv, axis=1), out


VMEM = pl.BlockSpec(memory_space=pltpu.VMEM)
SMEM = pl.BlockSpec(memory_space=pltpu.SMEM)


def one_hot(mask):
    return jnp.where(mask, 1.0, 0.0).astype(BF)


def call(kernel, outs, args, specs=None, flops=100_000_000, name=None, scratch=(), limit=48):
    return pl.pallas_call(
        kernel,
        out_shape=[jax.ShapeDtypeStruct(shape, dtype) for shape, dtype in outs],
        in_specs=specs or [VMEM] * len(args),
        out_specs=[VMEM] * len(outs),
        scratch_shapes=list(scratch),
        compiler_params=pltpu.CompilerParams(vmem_limit_bytes=limit * 1024 * 1024),
        cost_estimate=pl.CostEstimate(flops=flops, bytes_accessed=2_000_000, transcendentals=0),
        name=name,
    )(*args)


def small_rows(info_ref, rate_ref, gate_ref):
    rows = jnp.concatenate(
        [gate_ref[...].astype(F32), rate_ref[...].astype(F32), jnp.ones((6, N), F32)], axis=0
    )
    row, patch = iotas(16, N)
    return jnp.where((patch < info_ref[0]) & (row < 11), rows, 0.0)


def shuffle(by_column, inverse):
    i, j = iotas(144, 144)
    packed, plain = (j, i) if inverse else (i, j)
    peer = shr(packed * 3641, 16)
    rest = packed - 18 * peer
    c = rest & 1
    within = 8 * c + peer if by_column else 2 * peer + c
    return one_hot(plain == 16 * shr(rest, 1) + within)


def pack(parts, small, by_column, out_ref):
    parts = [part[:, h * N : (h + 1) * N].astype(F32) for part in parts for h in range(2)]
    parts.append(jnp.concatenate([small, jnp.zeros((N - 16, N), F32)], axis=0).T)
    order = shuffle(by_column, False)
    for b in range(8):
        if by_column:
            rows = [part[start + 8 * b : start + 8 * b + 8] for part in parts for start in (0, 64)]
        else:
            rows = [part[16 * b : 16 * b + 16] for part in parts]
        out_ref[144 * b : 144 * b + 144, :] = dot(order, jnp.concatenate(rows, axis=0)).astype(BF)


def unpack(got_ref, by_column, first=0, last=9):
    order = shuffle(by_column, True)[16 * first : 16 * last]
    blocks = [dot(order, got_ref[144 * b : 144 * b + 144, :]) for b in range(8)]
    parts = []
    for s in range(last - first):
        if by_column:
            rows = [block[16 * s + 8 * c : 16 * s + 8 * c + 8] for c in range(2) for block in blocks]
        else:
            rows = [block[16 * s : 16 * s + 16] for block in blocks]
        parts.append(jnp.concatenate(rows, axis=0))
    return parts


def heads_of(parts):
    return [jnp.concatenate(parts[2 * a : 2 * a + 2], axis=1) for a in range(len(parts) // 2)]


def pack_kernel(info_ref, rate_ref, gate_ref, q_ref, k_ref, v_ref, cot_ref, out_ref, held, sems):
    copies = [
        pltpu.make_async_copy(ref, held.at[a], sems.at[a])
        for a, ref in enumerate((q_ref, k_ref, v_ref, cot_ref))
    ]
    for copy in copies:
        copy.start()
    small = small_rows(info_ref, rate_ref, gate_ref)
    for copy in copies:
        copy.wait()
    pack([held[a] for a in range(4)], small, False, out_ref)


def row_forward_kernel(info_ref, q_ref, k_ref, v_ref, rate_ref, gate_ref, o_ref, t_ref, e_ref):
    patch, unused = iotas(N, 2 * N)
    small = small_rows(info_ref, rate_ref, gate_ref)
    outs, solved, errors = forward(prepare(q_ref[...], k_ref[...], small, N, 0), v_ref[...], N)
    o_ref[...] = jnp.where(patch < info_ref[0], jnp.concatenate(outs, axis=1), 0.0)
    for s in range(4):
        t_ref[s], e_ref[s] = solved[s], errors[s]


def row_backward_kernel(
    info_ref, q_ref, k_ref, rate_ref, gate_ref, t_ref, e_ref, cot_ref, w_ref, gq_ref, gk_ref, gv_ref, gs_ref
):
    patch, unused = iotas(N, 2 * N)
    cot = jnp.where(patch < info_ref[0], dot(cot_ref[...], w_ref[...], 1, 1), 0.0).astype(BF)
    q, k = q_ref[...], k_ref[...]
    small = small_rows(info_ref, rate_ref, gate_ref)
    solved = [t_ref[s] for s in range(4)]
    errors = [e_ref[s] for s in range(4)]
    ready = prepare(q, k, small, N, 0)
    gq_ref[...], gk_ref[...], gv_ref[...], gs_ref[...] = backward(ready, solved, errors, q, k, small, cot, 0)


def unpack_kernel(got_ref, q_ref, k_ref, v_ref, copies_ref, small_ref):
    pieces = unpack(got_ref, True)
    parts, scalars = heads_of(pieces), pieces[8]
    for part, ref in zip(parts, (q_ref, k_ref, v_ref)):
        ref[...] = part.astype(BF)
    for x in range(4):
        copies_ref[x * N : (x + 1) * N, :] = parts[3].astype(BF)
    small_ref[...] = scalars.T[:16, :]


def tissue_of(small):
    return jnp.concatenate([small, jnp.zeros((N - 16, N), F32)], axis=0).T[:, 10:11] > 0.5


def column_forward_kernel(q_ref, k_ref, v_ref, small_ref, o_ref, t_ref, e_ref):
    small = small_ref[...]
    outs, solved, errors = forward(prepare(q_ref[...], k_ref[...], small, 64, 2), v_ref[...], 64)
    o_ref[...] = jnp.where(tissue_of(small), jnp.concatenate(outs, axis=1), 0.0).astype(BF)
    for s in range(4):
        t_ref[s], e_ref[s] = solved[s], errors[s]


def column_backward_kernel(q_ref, k_ref, small_ref, o_ref, t_ref, e_ref, cot_ref, w_ref, send_ref):
    total = 0.0
    for block in range(8):
        rows = ((block & 1) * 4 + (block >> 1)) * N
        total = total + dot(cot_ref[rows : rows + N, :], w_ref[:, block * 2 * N : (block + 1) * 2 * N], 1, 1)
    q, k, small = q_ref[...], k_ref[...], small_ref[...]
    cot = jnp.where(tissue_of(small), total, 0.0).astype(BF)
    solved = [t_ref[s] for s in range(4)]
    errors = [e_ref[s] for s in range(4)]
    gq, gk, gv, gs = backward(prepare(q, k, small, 64, 2), solved, errors, q, k, small, cot, 2)
    pack([o_ref[...], gq, gk, gv], gs, True, send_ref)


def weight_kernel(
    info_ref, row_cot_ref, row_o_ref, col_cot_ref, col_o_ref, own_ref, first_ref, second_ref, third_ref, part_ref
):
    hidden = jnp.concatenate([row_o_ref[...].astype(BF), col_o_ref[...]], axis=0)
    for z in range(16):
        block, half = z >> 1, z & 1
        rows = ((block & 1) * 4 + (block >> 1)) * N
        col_cot = col_cot_ref[rows : rows + N, half * N : (half + 1) * N]
        cot = jnp.concatenate([row_cot_ref[:, z * N : (z + 1) * N], col_cot], axis=0)
        part_ref[z] = dot(cot, hidden, 0, 0)
    for step, ref in enumerate((own_ref, first_ref, second_ref, third_ref)):
        start = pl.multiple_of(((info_ref[3] + step) & 3) * 32, 32)
        for z in range(16):
            ref[z * 32 : (z + 1) * 32, :] = part_ref[z, pl.ds(start, 32), :].astype(BF)


def projection_kernel(info_ref, w_ref, own_ref, other_ref):
    place, core = info_ref[1], info_ref[2]
    for step in range(4):
        for ref, side in ((own_ref, core), (other_ref, 1 - core)):
            block = 2 * ((place + step) & 3) + side
            lanes = pl.ds(pl.multiple_of(block * 2 * N, 2 * N), 2 * N)
            ref[step] = w_ref[:, lanes]


def hidden_kernel(got_ref, o_ref, hidden_ref):
    (col,) = heads_of(unpack(got_ref, False, 0, 2))
    hidden_ref[...] = (o_ref[...] + col).astype(BF)


def gradient_kernel(
    info_ref, got_ref, gq_ref, gk_ref, gv_ref, gs_ref, q_ref, k_ref, v_ref, rate_ref, gate_ref
):
    pieces = unpack(got_ref, False, 2, 9)
    parts, scalars = heads_of(pieces), pieces[6]
    for part, row_ref, out_ref in zip(parts, (gq_ref, gk_ref, gv_ref), (q_ref, k_ref, v_ref)):
        out_ref[...] = (row_ref[...] + part).astype(BF)
    unused, patch = iotas(16, N)
    small = jnp.where(patch < info_ref[0], gs_ref[...] + scalars.T[:16, :], 0.0)
    gate_ref[...] = small[:8, :]
    rate_ref[...] = small[8:10, :]


def encode_kernel(info_ref, hidden_ref, own_ref, swapped_ref, kept_ref, sent_ref):
    core = info_ref[2]
    mine = hidden_ref[pl.ds(pl.multiple_of(core * N, N), N), :]
    other = hidden_ref[pl.ds(pl.multiple_of((1 - core) * N, N), N), :]
    for step in range(4):
        part = dot(mine, own_ref[step]) + dot(other, swapped_ref[step])
        if step == 0:
            kept_ref[...] = part
        else:
            sent_ref[step - 1] = part.astype(BF)


def exchange(x, axis, groups=None):
    return lax.all_to_all(x, axis, split_axis=0, concat_axis=0, tiled=True, axis_index_groups=groups)


def swap_rows(x):
    return exchange(x.reshape(64, 9, 2, N), "rows").reshape(18 * 64, N)


def per_device(
    query_proj, key_proj, value_proj, write_rate, log_gate, tissue_lengths, out_weight, cotangent
):
    q, k, v = query_proj[0], key_proj[0], value_proj[0]
    rate = write_rate[0].T
    gate = log_gate[0].transpose(1, 2, 0).reshape(8, N)
    me = lax.axis_index("heads")
    info = jnp.stack([tissue_lengths[0], lax.shift_right_logical(me, 1), me & 1, lax.axis_index("rows") & 3])
    wide, few = (N, 2 * N), (16, N)

    (send,) = call(
        pack_kernel,
        [((18 * 64, N), BF)],
        [tissue_lengths, rate, gate, q, k, v, cotangent[0]],
        [SMEM, VMEM, VMEM] + [pl.BlockSpec(memory_space=pl.ANY)] * 4,
        name="pack",
        scratch=[pltpu.VMEM((4, N, 2 * N), BF), pltpu.SemaphoreType.DMA((4,))],
        limit=62,
    )
    got = swap_rows(send)
    row_cot = lax.all_gather(cotangent[0], "heads", axis=1, tiled=True)
    got, row_cot = lax.optimization_barrier((got, row_cot))
    qc, kc, vc, copies, sc = call(
        unpack_kernel,
        [(wide, BF)] * 3 + [((4 * N, 2 * N), BF), (few, F32)],
        [got],
        name="unpack",
    )
    x_groups = [[2 * x + core for x in range(4)] for core in range(2)]
    pairs = [[2 * x, 2 * x + 1] for x in range(4)]
    along_x = exchange(copies, "heads", x_groups)
    rate_late, unused = lax.optimization_barrier((rate, sc))
    o_row, tr, er = call(
        row_forward_kernel,
        [(wide, F32)] + [((4, N, N), BF)] * 2,
        [info, q, k, v, rate_late, gate],
        [SMEM] + [VMEM] * 5,
        flops=3_000_000_000,
        name="row_forward",
    )
    o_col, tc, ec = call(
        column_forward_kernel,
        [(wide, BF)] + [((4, N, N), BF)] * 2,
        [qc, kc, vc, sc],
        flops=3_000_000_000,
        name="column_forward",
    )
    along_x, o_row = lax.optimization_barrier((along_x, o_row))
    col_cot = lax.all_gather(along_x, "heads", axis=0, tiled=True, axis_index_groups=pairs)
    (send,) = call(
        column_backward_kernel,
        [((18 * 64, N), BF)],
        [qc, kc, sc, o_col, tc, ec, col_cot, out_weight],
        flops=3_000_000_000,
        name="column_backward",
    )
    got = swap_rows(send)
    own_wg, *sent_wg = call(
        weight_kernel,
        [((4 * N, 2 * N), BF)] * 4,
        [info, row_cot, o_row, col_cot, o_col],
        [SMEM] + [VMEM] * 4,
        flops=2_000_000_000,
        name="weight_gradient",
        scratch=[pltpu.VMEM((16, N, 2 * N), F32)],
    )
    rate_late, weight, unused = lax.optimization_barrier((rate, out_weight, own_wg))
    gq, gk, gv, gs = call(
        row_backward_kernel,
        [(wide, F32)] * 3 + [(few, F32)],
        [info, q, k, rate_late, gate, tr, er, row_cot, out_weight],
        [SMEM] + [VMEM] * 8,
        flops=3_000_000_000,
        name="row_backward",
    )
    block = (4, 2 * N, 2 * N)
    own, other = call(projection_kernel, [(block, BF)] * 2, [info, weight], [SMEM, VMEM], name="projection")
    swapped = lax.ppermute(other, "heads", [(i, i ^ 1) for i in range(8)])
    summed = own_wg.astype(F32)
    for step in range(1, 4):
        moves = [(z * 4 + y, z * 4 + (y + step) % 4) for z in range(16) for y in range(4)]
        summed = summed + lax.ppermute(sent_wg[step - 1], "rows", moves).astype(F32)
    summed, gs = lax.optimization_barrier((summed.astype(BF), gs))
    z_groups = [[z * 4 + y for z in range(16)] for y in range(4)]
    (hidden,) = call(hidden_kernel, [(wide, BF)], [got, o_row], name="hidden")
    hidden = lax.all_gather(hidden, "heads", axis=0, tiled=True, axis_index_groups=pairs)
    encoded, sent = call(
        encode_kernel,
        [(wide, F32), ((3, N, 2 * N), BF)],
        [info, hidden, own, swapped],
        [SMEM] + [VMEM] * 3,
        flops=1_000_000_000,
        name="encode",
    )
    for step in range(1, 4):
        moves = [(i, ((i // 2 + step) % 4) * 2 + i % 2) for i in range(8)]
        encoded = encoded + lax.ppermute(sent[step - 1], "heads", moves).astype(F32)
    encoded = encoded.astype(BF)[None]
    grad_q, grad_k, grad_v, grad_rate, grad_gate = call(
        gradient_kernel,
        [(wide, BF)] * 3 + [((2, N), F32), ((8, N), F32)],
        [info, got, gq, gk, gv, gs],
        [SMEM] + [VMEM] * 5,
        flops=1_000_000_000,
        name="gradients",
    )

    pieces = exchange(summed, "rows", z_groups)
    weight_grad = jnp.sum(pieces.reshape(16, 32, 2 * N).astype(F32), axis=0)
    rate_grad = grad_rate.T[None]
    gate_grad = grad_gate.reshape(2, 4, N).transpose(2, 0, 1)[None]
    return (encoded, grad_q[None], grad_k[None], grad_v[None], rate_grad, gate_grad, weight_grad)


def solution(mesh):
    in_specs = (
        P("rows", None, "heads"),
        P("rows", None, "heads"),
        P("rows", None, "heads"),
        P("rows", None, "heads"),
        P("rows", None, "heads", None),
        P("rows"),
        P("heads", None),
        P("rows", None, "heads"),
    )
    out_specs = (
        P("rows", None, "heads"),
        P("rows", None, "heads"),
        P("rows", None, "heads"),
        P("rows", None, "heads"),
        P("rows", None, "heads"),
        P("rows", None, "heads", None),
        P("rows", "heads"),
    )
    return jax.shard_map(
        per_device, mesh=mesh, in_specs=in_specs, out_specs=out_specs, check_vma=False
    )
```

```python
import functools

import jax
import jax.numpy as jnp
from jax import lax
from jax.experimental import pallas as pl
from jax.experimental.pallas import tpu as pltpu
from jax.sharding import PartitionSpec as P

N = 128
F32 = jnp.float32
BF = jnp.bfloat16


def dot(a, b, ca=1, cb=0):
    return lax.dot_general(a.astype(BF), b.astype(BF), (((ca,), (cb,)), ((), ())), preferred_element_type=F32)


def iotas(rows=N, cols=N):
    return lax.broadcasted_iota(jnp.int32, (rows, cols), 0), lax.broadcasted_iota(jnp.int32, (rows, cols), 1)


def shr(x, n):
    return lax.shift_right_logical(x, jnp.int32(n))


def invert(systems, length):
    i, j = iotas()
    apart = i ^ j
    eye = jnp.where(apart == 0, 1.0, 0.0)
    solved = [eye - jnp.where(apart == 1, a, 0.0) for a in systems]
    level = 1
    while (2 << level) <= length:
        mask = shr(apart, level) == 1
        crossing = [jnp.where(mask, a, 0.0).astype(BF) for a in systems]
        halves = [t.astype(BF) for t in solved]
        inner = [dot(c, t) for c, t in zip(crossing, halves)]
        solved = [t - dot(h, m) for t, h, m in zip(solved, halves, inner)]
        level += 1
    return solved


def split3(x):
    hi = x.astype(BF)
    rest = x - hi.astype(F32)
    mid = rest.astype(BF)
    return hi, mid, (rest - mid.astype(F32)).astype(BF)


def prefix_sums(length):
    i, j = iotas()
    shift = length.bit_length() - 1
    same = shr(i, shift) == shr(j, shift)
    before = [same & (i >= j), same & (i <= j)]
    return [jnp.where(m, 1.0, 0.0).astype(BF) for m in before], before, i == j


def prepare(q, k, small, length, first):
    sums, before, eye = prefix_sums(length)
    cum = [dot(m, small, 1, 1) for m in sums]
    cum_t = [dot(small, m, 1, 1) for m in sums]
    heads = []
    for h in range(2):
        lanes = slice(h * N, (h + 1) * N)
        kh, qh = k[:, lanes], q[:, lanes]
        gram = dot(kh, kh, 1, 1)
        cross = dot(qh, kh, 1, 1)
        diag = jnp.where(eye, gram, 0.0)
        s_col = lax.rsqrt(jnp.sum(diag, axis=1, keepdims=True) + 1e-6)
        s_row = lax.rsqrt(jnp.sum(diag, axis=0, keepdims=True) + 1e-6)
        gram = gram * (s_col * s_row)
        cross = cross * (s_row * (N ** -0.5))
        rate_row = small[8 + h : 9 + h, :]
        per = []
        for d in range(2):
            g = 4 * h + first + d
            ratio = cum[d][:, g : g + 1] - cum_t[d][g : g + 1, :]
            weight = jnp.exp(jnp.where(before[d], ratio, -jnp.inf)) * rate_row
            strict = jnp.where(eye, 0.0, weight)
            per.append((weight, strict, strict * gram, weight * cross))
        heads.append((s_col, s_row, per))
    return sums, heads


def forward(prepared, v, length):
    sums, heads = prepared
    systems = [p[2] for hd in heads for p in hd[2]]
    solved = [t.astype(BF) for t in invert(systems, length)]
    outs, errors = [], []
    for h in range(2):
        vh = v[:, h * N : (h + 1) * N]
        es = [dot(solved[2 * h + d], vh).astype(BF) for d in range(2)]
        mix = jnp.concatenate([heads[h][2][0][3].astype(BF), heads[h][2][1][3].astype(BF)], axis=1)
        outs.append(dot(mix, jnp.concatenate(es, axis=0)))
        errors += es
    return outs, solved, errors


def backward(prepared, solved, errors, q, k, small, cot, first):
    sums, heads = prepared
    i, j = iotas()
    gq, gk, gv, rowsums, colsums = [], [], [], [], []
    for h in range(2):
        lanes = slice(h * N, (h + 1) * N)
        s_col, s_row, per = heads[h]
        c, kh, qh = cot[:, lanes], k[:, lanes], q[:, lanes]
        es = errors[2 * h : 2 * h + 2]
        d_mix = dot(c, jnp.concatenate(es, axis=0), 1, 1)
        mix = jnp.concatenate([per[0][3].astype(BF), per[1][3].astype(BF)], axis=1)
        d_err = dot(mix, c, 0, 0)
        d_val = [dot(solved[2 * h + d], d_err[d * N : (d + 1) * N], 0, 0) for d in range(2)]
        d_sys = [-dot(d_val[d], es[d], 1, 1) for d in range(2)]
        d_gram, d_cross = 0.0, 0.0
        for d in range(2):
            weight, strict, system, mixing = per[d]
            dm = d_mix[:, d * N : (d + 1) * N]
            d_gram = d_gram + d_sys[d] * strict
            d_cross = d_cross + dm * weight
            total = d_sys[d] * system + dm * mixing
            rowsums.append(jnp.sum(total, axis=1, keepdims=True))
            colsums.append(jnp.sum(total, axis=0, keepdims=True))
        both = d_gram + d_gram.T
        gq.append(dot(d_cross * (s_row * (N ** -0.5)), kh))
        kf = kh.astype(F32)
        d_kn = dot(both * s_row, kh) + dot(d_cross, qh, 0, 0) * (N ** -0.5)
        along = s_col * jnp.sum(kf * d_kn, axis=1, keepdims=True)
        gk.append(s_col * (d_kn - kf * (s_col * along)))
        gv.append(d_val[0] + d_val[1])
    across = jnp.zeros((N, N), F32)
    for s in range(4):
        across = jnp.where(j == s, rowsums[s], across)
    d_cum = across.T[:8, :] - jnp.concatenate(colsums + [jnp.zeros((4, N), F32)], axis=0)
    pieces = split3(d_cum)
    gates = [sum(dot(p, sums[1 - d], 1, 1) for p in pieces) for d in range(2)]
    zero = jnp.zeros((1, N), F32)
    out = [zero] * 16
    for h in range(2):
        rate = small[8 + h : 9 + h, :]
        whole = colsums[2 * h] + colsums[2 * h + 1]
        out[8 + h] = jnp.where(rate > 0, whole / jnp.where(rate > 0, rate, 1.0), 0.0)
        for d in range(2):
            s = 2 * h + d
            out[4 * h + first + d] = gates[d][s : s + 1, :]
    out = jnp.concatenate(out, axis=0)
    return jnp.concatenate(gq, axis=1), jnp.concatenate(gk, axis=1), jnp.concatenate(gv, axis=1), out


VMEM = pl.BlockSpec(memory_space=pltpu.VMEM)
SMEM = pl.BlockSpec(memory_space=pltpu.SMEM)


def one_hot(mask):
    return jnp.where(mask, 1.0, 0.0).astype(BF)


def call(kernel, outs, args, specs=None, flops=100_000_000, name=None, scratch=(), limit=48):
    return pl.pallas_call(
        kernel,
        out_shape=[jax.ShapeDtypeStruct(shape, dtype) for shape, dtype in outs],
        in_specs=specs or [VMEM] * len(args),
        out_specs=[VMEM] * len(outs),
        scratch_shapes=list(scratch),
        compiler_params=pltpu.CompilerParams(vmem_limit_bytes=limit * 1024 * 1024),
        cost_estimate=pl.CostEstimate(flops=flops, bytes_accessed=2_000_000, transcendentals=0),
        name=name,
    )(*args)


def small_rows(info_ref, rate_ref, gate_ref):
    rows = jnp.concatenate(
        [gate_ref[...].astype(F32), rate_ref[...].astype(F32), jnp.ones((6, N), F32)], axis=0
    )
    row, patch = iotas(16, N)
    return jnp.where((patch < info_ref[0]) & (row < 11), rows, 0.0)


def shuffle(by_column, inverse):
    i, j = iotas(144, 144)
    packed, plain = (j, i) if inverse else (i, j)
    peer = shr(packed * 3641, 16)
    rest = packed - 18 * peer
    c = rest & 1
    within = 8 * c + peer if by_column else 2 * peer + c
    return one_hot(plain == 16 * shr(rest, 1) + within)


def pack(parts, small, by_column, out_ref):
    parts = [part[:, h * N : (h + 1) * N].astype(F32) for part in parts for h in range(2)]
    parts.append(jnp.concatenate([small, jnp.zeros((N - 16, N), F32)], axis=0).T)
    order = shuffle(by_column, False)
    for b in range(8):
        if by_column:
            rows = [part[start + 8 * b : start + 8 * b + 8] for part in parts for start in (0, 64)]
        else:
            rows = [part[16 * b : 16 * b + 16] for part in parts]
        out_ref[144 * b : 144 * b + 144, :] = dot(order, jnp.concatenate(rows, axis=0)).astype(BF)


def unpack(got_ref, by_column, first=0, last=9):
    order = shuffle(by_column, True)[16 * first : 16 * last]
    blocks = [dot(order, got_ref[144 * b : 144 * b + 144, :]) for b in range(8)]
    parts = []
    for s in range(last - first):
        if by_column:
            rows = [block[16 * s + 8 * c : 16 * s + 8 * c + 8] for c in range(2) for block in blocks]
        else:
            rows = [block[16 * s : 16 * s + 16] for block in blocks]
        parts.append(jnp.concatenate(rows, axis=0))
    return parts


def heads_of(parts):
    return [jnp.concatenate(parts[2 * a : 2 * a + 2], axis=1) for a in range(len(parts) // 2)]


def pack_kernel(info_ref, rate_ref, gate_ref, q_ref, k_ref, v_ref, cot_ref, out_ref, held, sems):
    copies = [
        pltpu.make_async_copy(ref, held.at[a], sems.at[a])
        for a, ref in enumerate((q_ref, k_ref, v_ref, cot_ref))
    ]
    for copy in copies:
        copy.start()
    small = small_rows(info_ref, rate_ref, gate_ref)
    for copy in copies:
        copy.wait()
    pack([held[a] for a in range(4)], small, False, out_ref)


def row_forward_kernel(info_ref, q_ref, k_ref, v_ref, rate_ref, gate_ref, o_ref, t_ref, e_ref):
    patch, unused = iotas(N, 2 * N)
    small = small_rows(info_ref, rate_ref, gate_ref)
    outs, solved, errors = forward(prepare(q_ref[...], k_ref[...], small, N, 0), v_ref[...], N)
    o_ref[...] = jnp.where(patch < info_ref[0], jnp.concatenate(outs, axis=1), 0.0)
    for s in range(4):
        t_ref[s], e_ref[s] = solved[s], errors[s]


def row_backward_kernel(
    info_ref, q_ref, k_ref, rate_ref, gate_ref, t_ref, e_ref, cot_ref, w_ref, gq_ref, gk_ref, gv_ref, gs_ref
):
    patch, unused = iotas(N, 2 * N)
    cot = jnp.where(patch < info_ref[0], dot(cot_ref[...], w_ref[...], 1, 1), 0.0).astype(BF)
    q, k = q_ref[...], k_ref[...]
    small = small_rows(info_ref, rate_ref, gate_ref)
    solved = [t_ref[s] for s in range(4)]
    errors = [e_ref[s] for s in range(4)]
    ready = prepare(q, k, small, N, 0)
    gq_ref[...], gk_ref[...], gv_ref[...], gs_ref[...] = backward(ready, solved, errors, q, k, small, cot, 0)


def unpack_kernel(got_ref, q_ref, k_ref, v_ref, copies_ref, small_ref):
    pieces = unpack(got_ref, True)
    parts, scalars = heads_of(pieces), pieces[8]
    for part, ref in zip(parts, (q_ref, k_ref, v_ref)):
        ref[...] = part.astype(BF)
    for x in range(4):
        copies_ref[x * N : (x + 1) * N, :] = parts[3].astype(BF)
    small_ref[...] = scalars.T[:16, :]


def tissue_of(small):
    return jnp.concatenate([small, jnp.zeros((N - 16, N), F32)], axis=0).T[:, 10:11] > 0.5


def column_forward_kernel(q_ref, k_ref, v_ref, small_ref, o_ref, t_ref, e_ref):
    small = small_ref[...]
    outs, solved, errors = forward(prepare(q_ref[...], k_ref[...], small, 64, 2), v_ref[...], 64)
    o_ref[...] = jnp.where(tissue_of(small), jnp.concatenate(outs, axis=1), 0.0).astype(BF)
    for s in range(4):
        t_ref[s], e_ref[s] = solved[s], errors[s]


def column_backward_kernel(q_ref, k_ref, small_ref, o_ref, t_ref, e_ref, cot_ref, w_ref, send_ref):
    total = 0.0
    for block in range(8):
        rows = ((block & 1) * 4 + (block >> 1)) * N
        total = total + dot(cot_ref[rows : rows + N, :], w_ref[:, block * 2 * N : (block + 1) * 2 * N], 1, 1)
    q, k, small = q_ref[...], k_ref[...], small_ref[...]
    cot = jnp.where(tissue_of(small), total, 0.0).astype(BF)
    solved = [t_ref[s] for s in range(4)]
    errors = [e_ref[s] for s in range(4)]
    gq, gk, gv, gs = backward(prepare(q, k, small, 64, 2), solved, errors, q, k, small, cot, 2)
    pack([o_ref[...], gq, gk, gv], gs, True, send_ref)


def weight_kernel(
    info_ref, row_cot_ref, row_o_ref, col_cot_ref, col_o_ref, own_ref, first_ref, second_ref, third_ref, part_ref
):
    hidden = jnp.concatenate([row_o_ref[...].astype(BF), col_o_ref[...]], axis=0)
    for z in range(16):
        block, half = z >> 1, z & 1
        rows = ((block & 1) * 4 + (block >> 1)) * N
        col_cot = col_cot_ref[rows : rows + N, half * N : (half + 1) * N]
        cot = jnp.concatenate([row_cot_ref[:, z * N : (z + 1) * N], col_cot], axis=0)
        part_ref[z] = dot(cot, hidden, 0, 0)
    for step, ref in enumerate((own_ref, first_ref, second_ref, third_ref)):
        start = pl.multiple_of(((info_ref[3] + step) & 3) * 32, 32)
        for z in range(16):
            ref[z * 32 : (z + 1) * 32, :] = part_ref[z, pl.ds(start, 32), :].astype(BF)


def hidden_kernel(info_ref, got_ref, o_ref, w_ref, own_ref, other_ref):
    (col,) = heads_of(unpack(got_ref, False, 0, 2))
    hidden = (o_ref[...] + col).astype(BF)
    place, core = info_ref[1], info_ref[2]
    for step in range(4):
        for ref, side in ((own_ref, core), (other_ref, 1 - core)):
            block = 2 * ((place + step) & 3) + side
            lanes = pl.ds(pl.multiple_of(block * 2 * N, 2 * N), 2 * N)
            ref[step * N : (step + 1) * N, :] = dot(hidden, w_ref[:, lanes]).astype(BF)


def gradient_kernel(
    info_ref, got_ref, gq_ref, gk_ref, gv_ref, gs_ref, q_ref, k_ref, v_ref, rate_ref, gate_ref
):
    pieces = unpack(got_ref, False, 2, 9)
    parts, scalars = heads_of(pieces), pieces[6]
    for part, row_ref, out_ref in zip(parts, (gq_ref, gk_ref, gv_ref), (q_ref, k_ref, v_ref)):
        out_ref[...] = (row_ref[...] + part).astype(BF)
    unused, patch = iotas(16, N)
    small = jnp.where(patch < info_ref[0], gs_ref[...] + scalars.T[:16, :], 0.0)
    gate_ref[...] = small[:8, :]
    rate_ref[...] = small[8:10, :]


def pair_kernel(info_ref, own_ref, pair_ref, kept_ref, sent_ref):
    start = (1 - info_ref[2]) * 4 * N
    for step in range(4):
        rows = pl.ds(pl.multiple_of(start + step * N, N), N)
        total = own_ref[step * N : (step + 1) * N, :].astype(F32) + pair_ref[rows, :].astype(F32)
        if step == 0:
            kept_ref[...] = total
        else:
            sent_ref[step - 1] = total.astype(BF)


def exchange(x, axis, groups=None):
    return lax.all_to_all(x, axis, split_axis=0, concat_axis=0, tiled=True, axis_index_groups=groups)


def swap_rows(x):
    return exchange(x.reshape(64, 9, 2, N), "rows").reshape(18 * 64, N)


def per_device(
    query_proj, key_proj, value_proj, write_rate, log_gate, tissue_lengths, out_weight, cotangent
):
    q, k, v = query_proj[0], key_proj[0], value_proj[0]
    rate = write_rate[0].T
    gate = log_gate[0].transpose(1, 2, 0).reshape(8, N)
    me = lax.axis_index("heads")
    info = jnp.stack([tissue_lengths[0], lax.shift_right_logical(me, 1), me & 1, lax.axis_index("rows") & 3])
    wide, few = (N, 2 * N), (16, N)

    (send,) = call(
        pack_kernel,
        [((18 * 64, N), BF)],
        [tissue_lengths, rate, gate, q, k, v, cotangent[0]],
        [SMEM, VMEM, VMEM] + [pl.BlockSpec(memory_space=pl.ANY)] * 4,
        name="pack",
        scratch=[pltpu.VMEM((4, N, 2 * N), BF), pltpu.SemaphoreType.DMA((4,))],
        limit=62,
    )
    got = swap_rows(send)
    row_cot = lax.all_gather(cotangent[0], "heads", axis=1, tiled=True)
    got, row_cot = lax.optimization_barrier((got, row_cot))
    qc, kc, vc, copies, sc = call(
        unpack_kernel,
        [(wide, BF)] * 3 + [((4 * N, 2 * N), BF), (few, F32)],
        [got],
        name="unpack",
    )
    x_groups = [[2 * x + core for x in range(4)] for core in range(2)]
    pairs = [[2 * x, 2 * x + 1] for x in range(4)]
    along_x = exchange(copies, "heads", x_groups)
    rate_late, unused = lax.optimization_barrier((rate, sc))
    o_row, tr, er = call(
        row_forward_kernel,
        [(wide, F32)] + [((4, N, N), BF)] * 2,
        [info, q, k, v, rate_late, gate],
        [SMEM] + [VMEM] * 5,
        flops=3_000_000_000,
        name="row_forward",
    )
    o_col, tc, ec = call(
        column_forward_kernel,
        [(wide, BF)] + [((4, N, N), BF)] * 2,
        [qc, kc, vc, sc],
        flops=3_000_000_000,
        name="column_forward",
    )
    along_x, o_row = lax.optimization_barrier((along_x, o_row))
    col_cot = lax.all_gather(along_x, "heads", axis=0, tiled=True, axis_index_groups=pairs)
    (send,) = call(
        column_backward_kernel,
        [((18 * 64, N), BF)],
        [qc, kc, sc, o_col, tc, ec, col_cot, out_weight],
        flops=3_000_000_000,
        name="column_backward",
    )
    got = swap_rows(send)
    own_wg, *sent_wg = call(
        weight_kernel,
        [((4 * N, 2 * N), BF)] * 4,
        [info, row_cot, o_row, col_cot, o_col],
        [SMEM] + [VMEM] * 4,
        flops=2_000_000_000,
        name="weight_gradient",
        scratch=[pltpu.VMEM((16, N, 2 * N), F32)],
    )
    rate_late, unused = lax.optimization_barrier((rate, own_wg))
    gq, gk, gv, gs = call(
        row_backward_kernel,
        [(wide, F32)] * 3 + [(few, F32)],
        [info, q, k, rate_late, gate, tr, er, row_cot, out_weight],
        [SMEM] + [VMEM] * 8,
        flops=3_000_000_000,
        name="row_backward",
    )
    summed = own_wg.astype(F32)
    for step in range(1, 4):
        moves = [(z * 4 + y, z * 4 + (y + step) % 4) for z in range(16) for y in range(4)]
        summed = summed + lax.ppermute(sent_wg[step - 1], "rows", moves).astype(F32)
    summed, gs = lax.optimization_barrier((summed.astype(BF), gs))
    z_groups = [[z * 4 + y for z in range(16)] for y in range(4)]
    own, other = call(
        hidden_kernel,
        [((4 * N, 2 * N), BF)] * 2,
        [info, got, o_row, out_weight],
        [SMEM] + [VMEM] * 3,
        flops=1_000_000_000,
        name="hidden",
    )
    pair = lax.all_gather(other, "heads", axis=0, tiled=True, axis_index_groups=pairs)
    encoded, sent = call(
        pair_kernel,
        [(wide, F32), ((3, N, 2 * N), BF)],
        [info, own, pair],
        [SMEM] + [VMEM] * 2,
        name="pair_sums",
    )
    for step in range(1, 4):
        moves = [(i, ((i // 2 + step) % 4) * 2 + i % 2) for i in range(8)]
        encoded = encoded + lax.ppermute(sent[step - 1], "heads", moves).astype(F32)
    encoded = encoded.astype(BF)[None]
    grad_q, grad_k, grad_v, grad_rate, grad_gate = call(
        gradient_kernel,
        [(wide, BF)] * 3 + [((2, N), F32), ((8, N), F32)],
        [info, got, gq, gk, gv, gs],
        [SMEM] + [VMEM] * 5,
        flops=1_000_000_000,
        name="gradients",
    )

    pieces = exchange(summed, "rows", z_groups)
    weight_grad = jnp.sum(pieces.reshape(16, 32, 2 * N).astype(F32), axis=0)
    rate_grad = grad_rate.T[None]
    gate_grad = grad_gate.reshape(2, 4, N).transpose(2, 0, 1)[None]
    return (encoded, grad_q[None], grad_k[None], grad_v[None], rate_grad, gate_grad, weight_grad)


def solution(mesh):
    in_specs = (
        P("rows", None, "heads"),
        P("rows", None, "heads"),
        P("rows", None, "heads"),
        P("rows", None, "heads"),
        P("rows", None, "heads", None),
        P("rows"),
        P("heads", None),
        P("rows", None, "heads"),
    )
    out_specs = (
        P("rows", None, "heads"),
        P("rows", None, "heads"),
        P("rows", None, "heads"),
        P("rows", None, "heads"),
        P("rows", None, "heads"),
        P("rows", None, "heads", None),
        P("rows", "heads"),
    )
    return jax.shard_map(
        per_device, mesh=mesh, in_specs=in_specs, out_specs=out_specs, check_vma=False
    )
```

```python
import functools

import jax
import jax.numpy as jnp
from jax import lax
from jax.experimental import pallas as pl
from jax.experimental.pallas import tpu as pltpu
from jax.sharding import PartitionSpec as P

N = 128
F32 = jnp.float32
BF = jnp.bfloat16


def dot(a, b, ca=1, cb=0):
    return lax.dot_general(a.astype(BF), b.astype(BF), (((ca,), (cb,)), ((), ())), preferred_element_type=F32)


def iotas(rows=N, cols=N):
    return lax.broadcasted_iota(jnp.int32, (rows, cols), 0), lax.broadcasted_iota(jnp.int32, (rows, cols), 1)


def shr(x, n):
    return lax.shift_right_logical(x, jnp.int32(n))


def invert(systems, length):
    i, j = iotas()
    apart = i ^ j
    eye = jnp.where(apart == 0, 1.0, 0.0)
    solved = [eye - jnp.where(apart == 1, a, 0.0) for a in systems]
    level = 1
    while (2 << level) <= length:
        mask = shr(apart, level) == 1
        crossing = [jnp.where(mask, a, 0.0).astype(BF) for a in systems]
        halves = [t.astype(BF) for t in solved]
        inner = [dot(c, t) for c, t in zip(crossing, halves)]
        solved = [t - dot(h, m) for t, h, m in zip(solved, halves, inner)]
        level += 1
    return solved


def split3(x):
    hi = x.astype(BF)
    rest = x - hi.astype(F32)
    mid = rest.astype(BF)
    return hi, mid, (rest - mid.astype(F32)).astype(BF)


def prefix_sums(length):
    i, j = iotas()
    shift = length.bit_length() - 1
    same = shr(i, shift) == shr(j, shift)
    before = [same & (i >= j), same & (i <= j)]
    return [jnp.where(m, 1.0, 0.0).astype(BF) for m in before], before, i == j


def prepare(q, k, small, length, first):
    sums, before, eye = prefix_sums(length)
    cum = [dot(m, small, 1, 1) for m in sums]
    cum_t = [dot(small, m, 1, 1) for m in sums]
    heads = []
    for h in range(2):
        lanes = slice(h * N, (h + 1) * N)
        kh, qh = k[:, lanes], q[:, lanes]
        gram = dot(kh, kh, 1, 1)
        cross = dot(qh, kh, 1, 1)
        diag = jnp.where(eye, gram, 0.0)
        s_col = lax.rsqrt(jnp.sum(diag, axis=1, keepdims=True) + 1e-6)
        s_row = lax.rsqrt(jnp.sum(diag, axis=0, keepdims=True) + 1e-6)
        gram = gram * (s_col * s_row)
        cross = cross * (s_row * (N ** -0.5))
        rate_row = small[8 + h : 9 + h, :]
        per = []
        for d in range(2):
            g = 4 * h + first + d
            ratio = cum[d][:, g : g + 1] - cum_t[d][g : g + 1, :]
            weight = jnp.exp(jnp.where(before[d], ratio, -jnp.inf)) * rate_row
            strict = jnp.where(eye, 0.0, weight)
            per.append((weight, strict, strict * gram, weight * cross))
        heads.append((s_col, s_row, per))
    return sums, heads


def forward(prepared, v, length):
    sums, heads = prepared
    systems = [p[2] for hd in heads for p in hd[2]]
    solved = [t.astype(BF) for t in invert(systems, length)]
    outs, errors = [], []
    for h in range(2):
        vh = v[:, h * N : (h + 1) * N]
        es = [dot(solved[2 * h + d], vh).astype(BF) for d in range(2)]
        mix = jnp.concatenate([heads[h][2][0][3].astype(BF), heads[h][2][1][3].astype(BF)], axis=1)
        outs.append(dot(mix, jnp.concatenate(es, axis=0)))
        errors += es
    return outs, solved, errors


def backward(prepared, solved, errors, q, k, small, cot, first):
    sums, heads = prepared
    i, j = iotas()
    gq, gk, gv, rowsums, colsums = [], [], [], [], []
    for h in range(2):
        lanes = slice(h * N, (h + 1) * N)
        s_col, s_row, per = heads[h]
        c, kh, qh = cot[:, lanes], k[:, lanes], q[:, lanes]
        es = errors[2 * h : 2 * h + 2]
        d_mix = dot(c, jnp.concatenate(es, axis=0), 1, 1)
        mix = jnp.concatenate([per[0][3].astype(BF), per[1][3].astype(BF)], axis=1)
        d_err = dot(mix, c, 0, 0)
        d_val = [dot(solved[2 * h + d], d_err[d * N : (d + 1) * N], 0, 0) for d in range(2)]
        d_sys = [-dot(d_val[d], es[d], 1, 1) for d in range(2)]
        d_gram, d_cross = 0.0, 0.0
        for d in range(2):
            weight, strict, system, mixing = per[d]
            dm = d_mix[:, d * N : (d + 1) * N]
            d_gram = d_gram + d_sys[d] * strict
            d_cross = d_cross + dm * weight
            total = d_sys[d] * system + dm * mixing
            rowsums.append(jnp.sum(total, axis=1, keepdims=True))
            colsums.append(jnp.sum(total, axis=0, keepdims=True))
        both = d_gram + d_gram.T
        gq.append(dot(d_cross * (s_row * (N ** -0.5)), kh))
        kf = kh.astype(F32)
        d_kn = dot(both * s_row, kh) + dot(d_cross, qh, 0, 0) * (N ** -0.5)
        along = s_col * jnp.sum(kf * d_kn, axis=1, keepdims=True)
        gk.append(s_col * (d_kn - kf * (s_col * along)))
        gv.append(d_val[0] + d_val[1])
    across = jnp.zeros((N, N), F32)
    for s in range(4):
        across = jnp.where(j == s, rowsums[s], across)
    d_cum = across.T[:8, :] - jnp.concatenate(colsums + [jnp.zeros((4, N), F32)], axis=0)
    pieces = split3(d_cum)
    gates = [sum(dot(p, sums[1 - d], 1, 1) for p in pieces) for d in range(2)]
    zero = jnp.zeros((1, N), F32)
    out = [zero] * 16
    for h in range(2):
        rate = small[8 + h : 9 + h, :]
        whole = colsums[2 * h] + colsums[2 * h + 1]
        out[8 + h] = jnp.where(rate > 0, whole / jnp.where(rate > 0, rate, 1.0), 0.0)
        for d in range(2):
            s = 2 * h + d
            out[4 * h + first + d] = gates[d][s : s + 1, :]
    out = jnp.concatenate(out, axis=0)
    return jnp.concatenate(gq, axis=1), jnp.concatenate(gk, axis=1), jnp.concatenate(gv, axis=1), out


VMEM = pl.BlockSpec(memory_space=pltpu.VMEM)
SMEM = pl.BlockSpec(memory_space=pltpu.SMEM)


def one_hot(mask):
    return jnp.where(mask, 1.0, 0.0).astype(BF)


def call(kernel, outs, args, specs=None, flops=100_000_000, name=None, scratch=(), limit=48):
    return pl.pallas_call(
        kernel,
        out_shape=[jax.ShapeDtypeStruct(shape, dtype) for shape, dtype in outs],
        in_specs=specs or [VMEM] * len(args),
        out_specs=[VMEM] * len(outs),
        scratch_shapes=list(scratch),
        compiler_params=pltpu.CompilerParams(vmem_limit_bytes=limit * 1024 * 1024),
        cost_estimate=pl.CostEstimate(flops=flops, bytes_accessed=2_000_000, transcendentals=0),
        name=name,
    )(*args)


def small_rows(info_ref, rate_ref, gate_ref):
    rows = jnp.concatenate(
        [gate_ref[...].astype(F32), rate_ref[...].astype(F32), jnp.ones((6, N), F32)], axis=0
    )
    row, patch = iotas(16, N)
    return jnp.where((patch < info_ref[0]) & (row < 11), rows, 0.0)


def shuffle(by_column, inverse, flip):
    i, j = iotas(144, 144)
    packed, plain = (j, i) if inverse else (i, j)
    peer = shr(packed * 3641, 16)
    rest = packed - 18 * peer
    c = rest & 1
    if flip:
        peer = 7 - peer
    within = 8 * c + peer if by_column else 2 * peer + c
    return one_hot(plain == 16 * shr(rest, 1) + within)


def pack(parts, small, by_column, out_ref, flip=False):
    parts = [part[:, h * N : (h + 1) * N].astype(F32) for part in parts for h in range(2)]
    parts.append(jnp.concatenate([small, jnp.zeros((N - 16, N), F32)], axis=0).T)
    order = shuffle(by_column, False, flip)
    for b in range(8):
        if by_column:
            rows = [part[start + 8 * b : start + 8 * b + 8] for part in parts for start in (0, 64)]
        else:
            rows = [part[16 * b : 16 * b + 16] for part in parts]
        place = 7 - b if flip else b
        out_ref[144 * place : 144 * place + 144, :] = dot(order, jnp.concatenate(rows, axis=0)).astype(BF)


def unpack(got_ref, by_column, first=0, last=9, flip=False):
    order = shuffle(by_column, True, flip)[16 * first : 16 * last]
    places = range(7, -1, -1) if flip else range(8)
    blocks = [dot(order, got_ref[144 * b : 144 * b + 144, :]) for b in places]
    parts = []
    for s in range(last - first):
        if by_column:
            rows = [block[16 * s + 8 * c : 16 * s + 8 * c + 8] for c in range(2) for block in blocks]
        else:
            rows = [block[16 * s : 16 * s + 16] for block in blocks]
        parts.append(jnp.concatenate(rows, axis=0))
    return parts


def heads_of(parts):
    return [jnp.concatenate(parts[2 * a : 2 * a + 2], axis=1) for a in range(len(parts) // 2)]


def pack_kernel(info_ref, rate_ref, gate_ref, q_ref, k_ref, v_ref, cot_ref, out_ref, held, sems):
    copies = [
        pltpu.make_async_copy(ref, held.at[a], sems.at[a])
        for a, ref in enumerate((q_ref, k_ref, v_ref, cot_ref))
    ]
    for copy in copies:
        copy.start()
    small = small_rows(info_ref, rate_ref, gate_ref)
    for copy in copies:
        copy.wait()
    pack([held[a] for a in range(4)], small, False, out_ref, flip=True)


def row_forward_kernel(info_ref, q_ref, k_ref, v_ref, rate_ref, gate_ref, o_ref, t_ref, e_ref):
    patch, unused = iotas(N, 2 * N)
    small = small_rows(info_ref, rate_ref, gate_ref)
    outs, solved, errors = forward(prepare(q_ref[...], k_ref[...], small, N, 0), v_ref[...], N)
    o_ref[...] = jnp.where(patch < info_ref[0], jnp.concatenate(outs, axis=1), 0.0)
    for s in range(4):
        t_ref[s], e_ref[s] = solved[s], errors[s]


def row_backward_kernel(
    info_ref, q_ref, k_ref, rate_ref, gate_ref, t_ref, e_ref, cot_ref, w_ref, gq_ref, gk_ref, gv_ref, gs_ref
):
    patch, unused = iotas(N, 2 * N)
    cot = jnp.where(patch < info_ref[0], dot(cot_ref[...], w_ref[...], 1, 1), 0.0).astype(BF)
    q, k = q_ref[...], k_ref[...]
    small = small_rows(info_ref, rate_ref, gate_ref)
    solved = [t_ref[s] for s in range(4)]
    errors = [e_ref[s] for s in range(4)]
    ready = prepare(q, k, small, N, 0)
    gq_ref[...], gk_ref[...], gv_ref[...], gs_ref[...] = backward(ready, solved, errors, q, k, small, cot, 0)


def unpack_kernel(got_ref, q_ref, k_ref, v_ref, copies_ref, small_ref):
    pieces = unpack(got_ref, True, flip=True)
    parts, scalars = heads_of(pieces), pieces[8]
    for part, ref in zip(parts, (q_ref, k_ref, v_ref)):
        ref[...] = part.astype(BF)
    for x in range(4):
        copies_ref[x * N : (x + 1) * N, :] = parts[3].astype(BF)
    small_ref[...] = scalars.T[:16, :]


def tissue_of(small):
    return jnp.concatenate([small, jnp.zeros((N - 16, N), F32)], axis=0).T[:, 10:11] > 0.5


def column_forward_kernel(q_ref, k_ref, v_ref, small_ref, o_ref, t_ref, e_ref):
    small = small_ref[...]
    outs, solved, errors = forward(prepare(q_ref[...], k_ref[...], small, 64, 2), v_ref[...], 64)
    o_ref[...] = jnp.where(tissue_of(small), jnp.concatenate(outs, axis=1), 0.0).astype(BF)
    for s in range(4):
        t_ref[s], e_ref[s] = solved[s], errors[s]


def column_backward_kernel(q_ref, k_ref, small_ref, o_ref, t_ref, e_ref, cot_ref, w_ref, send_ref):
    total = 0.0
    for block in range(8):
        rows = ((block & 1) * 4 + (block >> 1)) * N
        total = total + dot(cot_ref[rows : rows + N, :], w_ref[:, block * 2 * N : (block + 1) * 2 * N], 1, 1)
    q, k, small = q_ref[...], k_ref[...], small_ref[...]
    cot = jnp.where(tissue_of(small), total, 0.0).astype(BF)
    solved = [t_ref[s] for s in range(4)]
    errors = [e_ref[s] for s in range(4)]
    gq, gk, gv, gs = backward(prepare(q, k, small, 64, 2), solved, errors, q, k, small, cot, 2)
    pack([o_ref[...], gq, gk, gv], gs, True, send_ref)


def weight_kernel(
    info_ref, row_cot_ref, row_o_ref, col_cot_ref, col_o_ref, own_ref, first_ref, second_ref, third_ref, part_ref
):
    hidden = jnp.concatenate([row_o_ref[...].astype(BF), col_o_ref[...]], axis=0)
    for z in range(16):
        block, half = z >> 1, z & 1
        rows = ((block & 1) * 4 + (block >> 1)) * N
        col_cot = col_cot_ref[rows : rows + N, half * N : (half + 1) * N]
        cot = jnp.concatenate([row_cot_ref[:, z * N : (z + 1) * N], col_cot], axis=0)
        part_ref[z] = dot(cot, hidden, 0, 0)
    for step, ref in enumerate((own_ref, first_ref, second_ref, third_ref)):
        start = pl.multiple_of(((info_ref[3] + step) & 3) * 32, 32)
        for z in range(16):
            ref[z * 32 : (z + 1) * 32, :] = part_ref[z, pl.ds(start, 32), :].astype(BF)


def projection_kernel(info_ref, w_ref, own_ref, other_ref):
    place, core = info_ref[1], info_ref[2]
    for step in range(4):
        for ref, side in ((own_ref, core), (other_ref, 1 - core)):
            block = 2 * ((place + step) & 3) + side
            lanes = pl.ds(pl.multiple_of(block * 2 * N, 2 * N), 2 * N)
            ref[step] = w_ref[:, lanes]


def hidden_kernel(got_ref, o_ref, hidden_ref):
    (col,) = heads_of(unpack(got_ref, False, 0, 2))
    hidden_ref[...] = (o_ref[...] + col).astype(BF)


def gradient_kernel(
    info_ref, got_ref, gq_ref, gk_ref, gv_ref, gs_ref, q_ref, k_ref, v_ref, rate_ref, gate_ref
):
    pieces = unpack(got_ref, False, 2, 9)
    parts, scalars = heads_of(pieces), pieces[6]
    for part, row_ref, out_ref in zip(parts, (gq_ref, gk_ref, gv_ref), (q_ref, k_ref, v_ref)):
        out_ref[...] = (row_ref[...] + part).astype(BF)
    unused, patch = iotas(16, N)
    small = jnp.where(patch < info_ref[0], gs_ref[...] + scalars.T[:16, :], 0.0)
    gate_ref[...] = small[:8, :]
    rate_ref[...] = small[8:10, :]


def encode_kernel(info_ref, hidden_ref, own_ref, swapped_ref, kept_ref, sent_ref):
    core = info_ref[2]
    mine = hidden_ref[pl.ds(pl.multiple_of(core * N, N), N), :]
    other = hidden_ref[pl.ds(pl.multiple_of((1 - core) * N, N), N), :]
    for step in range(4):
        part = dot(mine, own_ref[step]) + dot(other, swapped_ref[step])
        if step == 0:
            kept_ref[...] = part
        else:
            sent_ref[step - 1] = part.astype(BF)


def exchange(x, axis, groups=None):
    return lax.all_to_all(x, axis, split_axis=0, concat_axis=0, tiled=True, axis_index_groups=groups)


def swap_rows(x, flip):
    groups = [list(range(63, -1, -1))] if flip else None
    return exchange(x.reshape(64, 9, 2, N), "rows", groups).reshape(18 * 64, N)


def per_device(
    query_proj, key_proj, value_proj, write_rate, log_gate, tissue_lengths, out_weight, cotangent
):
    q, k, v = query_proj[0], key_proj[0], value_proj[0]
    rate = write_rate[0].T
    gate = log_gate[0].transpose(1, 2, 0).reshape(8, N)
    me = lax.axis_index("heads")
    info = jnp.stack([tissue_lengths[0], lax.shift_right_logical(me, 1), me & 1, lax.axis_index("rows") & 3])
    wide, few = (N, 2 * N), (16, N)

    (send,) = call(
        pack_kernel,
        [((18 * 64, N), BF)],
        [tissue_lengths, rate, gate, q, k, v, cotangent[0]],
        [SMEM, VMEM, VMEM] + [pl.BlockSpec(memory_space=pl.ANY)] * 4,
        name="pack",
        scratch=[pltpu.VMEM((4, N, 2 * N), BF), pltpu.SemaphoreType.DMA((4,))],
        limit=62,
    )
    got = swap_rows(send, True)
    row_cot = lax.all_gather(cotangent[0], "heads", axis=1, tiled=True)
    got, row_cot = lax.optimization_barrier((got, row_cot))
    qc, kc, vc, copies, sc = call(
        unpack_kernel,
        [(wide, BF)] * 3 + [((4 * N, 2 * N), BF), (few, F32)],
        [got],
        name="unpack",
    )
    x_groups = [[2 * x + core for x in range(4)] for core in range(2)]
    pairs = [[2 * x, 2 * x + 1] for x in range(4)]
    along_x = exchange(copies, "heads", x_groups)
    rate_late, unused = lax.optimization_barrier((rate, sc))
    o_row, tr, er = call(
        row_forward_kernel,
        [(wide, F32)] + [((4, N, N), BF)] * 2,
        [info, q, k, v, rate_late, gate],
        [SMEM] + [VMEM] * 5,
        flops=3_000_000_000,
        name="row_forward",
    )
    o_col, tc, ec = call(
        column_forward_kernel,
        [(wide, BF)] + [((4, N, N), BF)] * 2,
        [qc, kc, vc, sc],
        flops=3_000_000_000,
        name="column_forward",
    )
    along_x, o_row = lax.optimization_barrier((along_x, o_row))
    col_cot = lax.all_gather(along_x, "heads", axis=0, tiled=True, axis_index_groups=pairs)
    (send,) = call(
        column_backward_kernel,
        [((18 * 64, N), BF)],
        [qc, kc, sc, o_col, tc, ec, col_cot, out_weight],
        flops=3_000_000_000,
        name="column_backward",
    )
    got = swap_rows(send, False)
    own_wg, *sent_wg = call(
        weight_kernel,
        [((4 * N, 2 * N), BF)] * 4,
        [info, row_cot, o_row, col_cot, o_col],
        [SMEM] + [VMEM] * 4,
        flops=2_000_000_000,
        name="weight_gradient",
        scratch=[pltpu.VMEM((16, N, 2 * N), F32)],
    )
    rate_late, weight, unused = lax.optimization_barrier((rate, out_weight, own_wg))
    gq, gk, gv, gs = call(
        row_backward_kernel,
        [(wide, F32)] * 3 + [(few, F32)],
        [info, q, k, rate_late, gate, tr, er, row_cot, out_weight],
        [SMEM] + [VMEM] * 8,
        flops=3_000_000_000,
        name="row_backward",
    )
    block = (4, 2 * N, 2 * N)
    own, other = call(projection_kernel, [(block, BF)] * 2, [info, weight], [SMEM, VMEM], name="projection")
    swapped = lax.ppermute(other, "heads", [(i, i ^ 1) for i in range(8)])
    summed = own_wg.astype(F32)
    for step in range(1, 4):
        moves = [(z * 4 + y, z * 4 + (y + step) % 4) for z in range(16) for y in range(4)]
        summed = summed + lax.ppermute(sent_wg[step - 1], "rows", moves).astype(F32)
    summed, gs = lax.optimization_barrier((summed.astype(BF), gs))
    z_groups = [[z * 4 + y for z in range(16)] for y in range(4)]
    (hidden,) = call(hidden_kernel, [(wide, BF)], [got, o_row], name="hidden")
    hidden = lax.all_gather(hidden, "heads", axis=0, tiled=True, axis_index_groups=pairs)
    encoded, sent = call(
        encode_kernel,
        [(wide, F32), ((3, N, 2 * N), BF)],
        [info, hidden, own, swapped],
        [SMEM] + [VMEM] * 3,
        flops=1_000_000_000,
        name="encode",
    )
    for step in range(1, 4):
        moves = [(i, ((i // 2 + step) % 4) * 2 + i % 2) for i in range(8)]
        encoded = encoded + lax.ppermute(sent[step - 1], "heads", moves).astype(F32)
    encoded = encoded.astype(BF)[None]
    grad_q, grad_k, grad_v, grad_rate, grad_gate = call(
        gradient_kernel,
        [(wide, BF)] * 3 + [((2, N), F32), ((8, N), F32)],
        [info, got, gq, gk, gv, gs],
        [SMEM] + [VMEM] * 5,
        flops=1_000_000_000,
        name="gradients",
    )

    pieces = exchange(summed, "rows", z_groups)
    weight_grad = jnp.sum(pieces.reshape(16, 32, 2 * N).astype(F32), axis=0)
    rate_grad = grad_rate.T[None]
    gate_grad = grad_gate.reshape(2, 4, N).transpose(2, 0, 1)[None]
    return (encoded, grad_q[None], grad_k[None], grad_v[None], rate_grad, gate_grad, weight_grad)


def solution(mesh):
    in_specs = (
        P("rows", None, "heads"),
        P("rows", None, "heads"),
        P("rows", None, "heads"),
        P("rows", None, "heads"),
        P("rows", None, "heads", None),
        P("rows"),
        P("heads", None),
        P("rows", None, "heads"),
    )
    out_specs = (
        P("rows", None, "heads"),
        P("rows", None, "heads"),
        P("rows", None, "heads"),
        P("rows", None, "heads"),
        P("rows", None, "heads"),
        P("rows", None, "heads", None),
        P("rows", "heads"),
    )
    return jax.shard_map(
        per_device, mesh=mesh, in_specs=in_specs, out_specs=out_specs, check_vma=False
    )
```

```python
import functools

import jax
import jax.numpy as jnp
from jax import lax
from jax.experimental import pallas as pl
from jax.experimental.pallas import tpu as pltpu
from jax.sharding import PartitionSpec as P

N = 128
F32 = jnp.float32
BF = jnp.bfloat16


def dot(a, b, ca=1, cb=0):
    return lax.dot_general(a.astype(BF), b.astype(BF), (((ca,), (cb,)), ((), ())), preferred_element_type=F32)


def iotas(rows=N, cols=N):
    return lax.broadcasted_iota(jnp.int32, (rows, cols), 0), lax.broadcasted_iota(jnp.int32, (rows, cols), 1)


def shr(x, n):
    return lax.shift_right_logical(x, jnp.int32(n))


def invert(systems, length):
    i, j = iotas()
    apart = i ^ j
    eye = jnp.where(apart == 0, 1.0, 0.0)
    solved = [eye - jnp.where(apart == 1, a, 0.0) for a in systems]
    level = 1
    while (2 << level) <= length:
        mask = shr(apart, level) == 1
        crossing = [jnp.where(mask, a, 0.0).astype(BF) for a in systems]
        halves = [t.astype(BF) for t in solved]
        inner = [dot(c, t) for c, t in zip(crossing, halves)]
        solved = [t - dot(h, m) for t, h, m in zip(solved, halves, inner)]
        level += 1
    return solved


def split3(x):
    hi = x.astype(BF)
    rest = x - hi.astype(F32)
    mid = rest.astype(BF)
    return hi, mid, (rest - mid.astype(F32)).astype(BF)


def prefix_sums(length):
    i, j = iotas()
    shift = length.bit_length() - 1
    same = shr(i, shift) == shr(j, shift)
    before = [same & (i >= j), same & (i <= j)]
    return [jnp.where(m, 1.0, 0.0).astype(BF) for m in before], before, i == j


def prepare(q, k, small, length, first):
    sums, before, eye = prefix_sums(length)
    cum = [dot(m, small, 1, 1) for m in sums]
    cum_t = [dot(small, m, 1, 1) for m in sums]
    heads = []
    for h in range(2):
        lanes = slice(h * N, (h + 1) * N)
        kh, qh = k[:, lanes], q[:, lanes]
        gram = dot(kh, kh, 1, 1)
        cross = dot(qh, kh, 1, 1)
        diag = jnp.where(eye, gram, 0.0)
        s_col = lax.rsqrt(jnp.sum(diag, axis=1, keepdims=True) + 1e-6)
        s_row = lax.rsqrt(jnp.sum(diag, axis=0, keepdims=True) + 1e-6)
        gram = gram * (s_col * s_row)
        cross = cross * (s_row * (N ** -0.5))
        rate_row = small[8 + h : 9 + h, :]
        per = []
        for d in range(2):
            g = 4 * h + first + d
            ratio = cum[d][:, g : g + 1] - cum_t[d][g : g + 1, :]
            weight = jnp.exp(jnp.where(before[d], ratio, -jnp.inf)) * rate_row
            strict = jnp.where(eye, 0.0, weight)
            per.append((weight, strict, strict * gram, weight * cross))
        heads.append((s_col, s_row, per))
    return sums, heads


def forward(prepared, v, length):
    sums, heads = prepared
    systems = [p[2] for hd in heads for p in hd[2]]
    solved = [t.astype(BF) for t in invert(systems, length)]
    outs, errors = [], []
    for h in range(2):
        vh = v[:, h * N : (h + 1) * N]
        es = [dot(solved[2 * h + d], vh).astype(BF) for d in range(2)]
        mix = jnp.concatenate([heads[h][2][0][3].astype(BF), heads[h][2][1][3].astype(BF)], axis=1)
        outs.append(dot(mix, jnp.concatenate(es, axis=0)))
        errors += es
    return outs, solved, errors


def backward(prepared, solved, errors, q, k, small, cot, first):
    sums, heads = prepared
    i, j = iotas()
    gq, gk, gv, rowsums, colsums = [], [], [], [], []
    for h in range(2):
        lanes = slice(h * N, (h + 1) * N)
        s_col, s_row, per = heads[h]
        c, kh, qh = cot[:, lanes], k[:, lanes], q[:, lanes]
        es = errors[2 * h : 2 * h + 2]
        d_mix = dot(c, jnp.concatenate(es, axis=0), 1, 1)
        mix = jnp.concatenate([per[0][3].astype(BF), per[1][3].astype(BF)], axis=1)
        d_err = dot(mix, c, 0, 0)
        d_val = [dot(solved[2 * h + d], d_err[d * N : (d + 1) * N], 0, 0) for d in range(2)]
        d_sys = [-dot(d_val[d], es[d], 1, 1) for d in range(2)]
        d_gram, d_cross = 0.0, 0.0
        for d in range(2):
            weight, strict, system, mixing = per[d]
            dm = d_mix[:, d * N : (d + 1) * N]
            d_gram = d_gram + d_sys[d] * strict
            d_cross = d_cross + dm * weight
            total = d_sys[d] * system + dm * mixing
            rowsums.append(jnp.sum(total, axis=1, keepdims=True))
            colsums.append(jnp.sum(total, axis=0, keepdims=True))
        both = d_gram + d_gram.T
        gq.append(dot(d_cross * (s_row * (N ** -0.5)), kh))
        kf = kh.astype(F32)
        d_kn = dot(both * s_row, kh) + dot(d_cross, qh, 0, 0) * (N ** -0.5)
        along = s_col * jnp.sum(kf * d_kn, axis=1, keepdims=True)
        gk.append(s_col * (d_kn - kf * (s_col * along)))
        gv.append(d_val[0] + d_val[1])
    across = jnp.zeros((N, N), F32)
    for s in range(4):
        across = jnp.where(j == s, rowsums[s], across)
    d_cum = across.T[:8, :] - jnp.concatenate(colsums + [jnp.zeros((4, N), F32)], axis=0)
    pieces = split3(d_cum)
    gates = [sum(dot(p, sums[1 - d], 1, 1) for p in pieces) for d in range(2)]
    zero = jnp.zeros((1, N), F32)
    out = [zero] * 16
    for h in range(2):
        rate = small[8 + h : 9 + h, :]
        whole = colsums[2 * h] + colsums[2 * h + 1]
        out[8 + h] = jnp.where(rate > 0, whole / jnp.where(rate > 0, rate, 1.0), 0.0)
        for d in range(2):
            s = 2 * h + d
            out[4 * h + first + d] = gates[d][s : s + 1, :]
    out = jnp.concatenate(out, axis=0)
    return jnp.concatenate(gq, axis=1), jnp.concatenate(gk, axis=1), jnp.concatenate(gv, axis=1), out


VMEM = pl.BlockSpec(memory_space=pltpu.VMEM)
SMEM = pl.BlockSpec(memory_space=pltpu.SMEM)


def one_hot(mask):
    return jnp.where(mask, 1.0, 0.0).astype(BF)


def call(kernel, outs, args, specs=None, flops=100_000_000, name=None, scratch=(), limit=48):
    return pl.pallas_call(
        kernel,
        out_shape=[jax.ShapeDtypeStruct(shape, dtype) for shape, dtype in outs],
        in_specs=specs or [VMEM] * len(args),
        out_specs=[VMEM] * len(outs),
        scratch_shapes=list(scratch),
        compiler_params=pltpu.CompilerParams(vmem_limit_bytes=limit * 1024 * 1024),
        cost_estimate=pl.CostEstimate(flops=flops, bytes_accessed=2_000_000, transcendentals=0),
        name=name,
    )(*args)


def small_rows(info_ref, rate_ref, gate_ref):
    rows = jnp.concatenate(
        [gate_ref[...].astype(F32), rate_ref[...].astype(F32), jnp.ones((6, N), F32)], axis=0
    )
    row, patch = iotas(16, N)
    return jnp.where((patch < info_ref[0]) & (row < 11), rows, 0.0)


def shuffle(by_column, inverse, flip):
    i, j = iotas(144, 144)
    packed, plain = (j, i) if inverse else (i, j)
    peer = shr(packed * 3641, 16)
    rest = packed - 18 * peer
    c = rest & 1
    if flip:
        peer = 7 - peer
    within = 8 * c + peer if by_column else 2 * peer + c
    return one_hot(plain == 16 * shr(rest, 1) + within)


def pack(parts, small, out_ref):
    parts = [part[:, h * N : (h + 1) * N].astype(F32) for part in parts for h in range(2)]
    parts.append(jnp.concatenate([small, jnp.zeros((N - 16, N), F32)], axis=0).T)
    order = shuffle(True, False, False)
    for b in range(8):
        rows = [part[start + 8 * b : start + 8 * b + 8] for part in parts for start in (0, 64)]
        out_ref[144 * b : 144 * b + 144, :] = dot(order, jnp.concatenate(rows, axis=0)).astype(BF)


def unpack(got_ref, by_column, first=0, last=9, flip=False):
    order = shuffle(by_column, True, flip)[16 * first : 16 * last]
    places = range(7, -1, -1) if flip else range(8)
    blocks = [dot(order, got_ref[144 * b : 144 * b + 144, :]) for b in places]
    parts = []
    for s in range(last - first):
        if by_column:
            rows = [block[16 * s + 8 * c : 16 * s + 8 * c + 8] for c in range(2) for block in blocks]
        else:
            rows = [block[16 * s : 16 * s + 16] for block in blocks]
        parts.append(jnp.concatenate(rows, axis=0))
    return parts


def heads_of(parts):
    return [jnp.concatenate(parts[2 * a : 2 * a + 2], axis=1) for a in range(len(parts) // 2)]


def pack_kernel(info_ref, rate_ref, gate_ref, q_ref, k_ref, v_ref, cot_ref, out_ref, held, sems):
    copies = [
        pltpu.make_async_copy(ref, held.at[a], sems.at[a])
        for a, ref in enumerate((q_ref, k_ref, v_ref, cot_ref))
    ]
    for copy in copies:
        copy.start()
    small = small_rows(info_ref, rate_ref, gate_ref)
    scalars = jnp.concatenate([small, jnp.zeros((N - 16, N), F32)], axis=0).T.astype(BF)
    order = shuffle(False, False, True)
    for copy in copies:
        copy.wait()
    for b in range(8):
        rows = [held[a, 16 * b : 16 * b + 16, h * N : (h + 1) * N] for a in range(4) for h in range(2)]
        rows.append(scalars[16 * b : 16 * b + 16])
        out_ref[144 * (7 - b) : 144 * (8 - b), :] = dot(order, jnp.concatenate(rows, axis=0)).astype(BF)


def row_forward_kernel(info_ref, q_ref, k_ref, v_ref, rate_ref, gate_ref, o_ref, t_ref, e_ref):
    patch, unused = iotas(N, 2 * N)
    small = small_rows(info_ref, rate_ref, gate_ref)
    outs, solved, errors = forward(prepare(q_ref[...], k_ref[...], small, N, 0), v_ref[...], N)
    o_ref[...] = jnp.where(patch < info_ref[0], jnp.concatenate(outs, axis=1), 0.0)
    for s in range(4):
        t_ref[s], e_ref[s] = solved[s], errors[s]


def row_backward_kernel(
    info_ref, q_ref, k_ref, rate_ref, gate_ref, t_ref, e_ref, cot_ref, w_ref, gq_ref, gk_ref, gv_ref, gs_ref
):
    patch, unused = iotas(N, 2 * N)
    cot = jnp.where(patch < info_ref[0], dot(cot_ref[...], w_ref[...], 1, 1), 0.0).astype(BF)
    q, k = q_ref[...], k_ref[...]
    small = small_rows(info_ref, rate_ref, gate_ref)
    solved = [t_ref[s] for s in range(4)]
    errors = [e_ref[s] for s in range(4)]
    ready = prepare(q, k, small, N, 0)
    gq_ref[...], gk_ref[...], gv_ref[...], gs_ref[...] = backward(ready, solved, errors, q, k, small, cot, 0)


def unpack_kernel(got_ref, q_ref, k_ref, v_ref, copies_ref, small_ref):
    pieces = unpack(got_ref, True, flip=True)
    parts, scalars = heads_of(pieces), pieces[8]
    for part, ref in zip(parts, (q_ref, k_ref, v_ref)):
        ref[...] = part.astype(BF)
    for x in range(4):
        copies_ref[x * N : (x + 1) * N, :] = parts[3].astype(BF)
    small_ref[...] = scalars.T[:16, :]


def tissue_of(small):
    return jnp.concatenate([small, jnp.zeros((N - 16, N), F32)], axis=0).T[:, 10:11] > 0.5


def column_forward_kernel(q_ref, k_ref, v_ref, small_ref, o_ref, t_ref, e_ref):
    small = small_ref[...]
    outs, solved, errors = forward(prepare(q_ref[...], k_ref[...], small, 64, 2), v_ref[...], 64)
    o_ref[...] = jnp.where(tissue_of(small), jnp.concatenate(outs, axis=1), 0.0).astype(BF)
    for s in range(4):
        t_ref[s], e_ref[s] = solved[s], errors[s]


def column_backward_kernel(q_ref, k_ref, small_ref, o_ref, t_ref, e_ref, cot_ref, w_ref, send_ref):
    total = 0.0
    for block in range(8):
        rows = ((block & 1) * 4 + (block >> 1)) * N
        total = total + dot(cot_ref[rows : rows + N, :], w_ref[:, block * 2 * N : (block + 1) * 2 * N], 1, 1)
    q, k, small = q_ref[...], k_ref[...], small_ref[...]
    cot = jnp.where(tissue_of(small), total, 0.0).astype(BF)
    solved = [t_ref[s] for s in range(4)]
    errors = [e_ref[s] for s in range(4)]
    gq, gk, gv, gs = backward(prepare(q, k, small, 64, 2), solved, errors, q, k, small, cot, 2)
    pack([o_ref[...], gq, gk, gv], gs, send_ref)


def weight_kernel(
    info_ref, row_cot_ref, row_o_ref, col_cot_ref, col_o_ref, own_ref, first_ref, second_ref, third_ref, part_ref
):
    hidden = jnp.concatenate([row_o_ref[...].astype(BF), col_o_ref[...]], axis=0)
    for z in range(16):
        block, half = z >> 1, z & 1
        rows = ((block & 1) * 4 + (block >> 1)) * N
        col_cot = col_cot_ref[rows : rows + N, half * N : (half + 1) * N]
        cot = jnp.concatenate([row_cot_ref[:, z * N : (z + 1) * N], col_cot], axis=0)
        part_ref[z] = dot(cot, hidden, 0, 0)
    for step, ref in enumerate((own_ref, first_ref, second_ref, third_ref)):
        start = pl.multiple_of(((info_ref[3] + step) & 3) * 32, 32)
        for z in range(16):
            ref[z * 32 : (z + 1) * 32, :] = part_ref[z, pl.ds(start, 32), :].astype(BF)


def projection_kernel(info_ref, w_ref, own_ref, other_ref):
    place, core = info_ref[1], info_ref[2]
    for step in range(4):
        for ref, side in ((own_ref, core), (other_ref, 1 - core)):
            block = 2 * ((place + step) & 3) + side
            lanes = pl.ds(pl.multiple_of(block * 2 * N, 2 * N), 2 * N)
            ref[step] = w_ref[:, lanes]


def hidden_kernel(got_ref, o_ref, hidden_ref):
    (col,) = heads_of(unpack(got_ref, False, 0, 2))
    hidden_ref[...] = (o_ref[...] + col).astype(BF)


def gradient_kernel(
    info_ref, got_ref, gq_ref, gk_ref, gv_ref, gs_ref, q_ref, k_ref, v_ref, rate_ref, gate_ref
):
    pieces = unpack(got_ref, False, 2, 9)
    parts, scalars = heads_of(pieces), pieces[6]
    for part, row_ref, out_ref in zip(parts, (gq_ref, gk_ref, gv_ref), (q_ref, k_ref, v_ref)):
        out_ref[...] = (row_ref[...] + part).astype(BF)
    unused, patch = iotas(16, N)
    small = jnp.where(patch < info_ref[0], gs_ref[...] + scalars.T[:16, :], 0.0)
    gate_ref[...] = small[:8, :]
    rate_ref[...] = small[8:10, :]


def encode_kernel(info_ref, hidden_ref, own_ref, swapped_ref, kept_ref, sent_ref):
    core = info_ref[2]
    mine = hidden_ref[pl.ds(pl.multiple_of(core * N, N), N), :]
    other = hidden_ref[pl.ds(pl.multiple_of((1 - core) * N, N), N), :]
    for step in range(4):
        part = dot(mine, own_ref[step]) + dot(other, swapped_ref[step])
        if step == 0:
            kept_ref[...] = part
        else:
            sent_ref[step - 1] = part.astype(BF)


def exchange(x, axis, groups=None):
    return lax.all_to_all(x, axis, split_axis=0, concat_axis=0, tiled=True, axis_index_groups=groups)


def swap_rows(x, flip):
    groups = [list(range(63, -1, -1))] if flip else None
    return exchange(x.reshape(64, 9, 2, N), "rows", groups).reshape(18 * 64, N)


def per_device(
    query_proj, key_proj, value_proj, write_rate, log_gate, tissue_lengths, out_weight, cotangent
):
    q, k, v = query_proj[0], key_proj[0], value_proj[0]
    rate = write_rate[0].T
    gate = log_gate[0].transpose(1, 2, 0).reshape(8, N)
    me = lax.axis_index("heads")
    info = jnp.stack([tissue_lengths[0], lax.shift_right_logical(me, 1), me & 1, lax.axis_index("rows") & 3])
    wide, few = (N, 2 * N), (16, N)

    (send,) = call(
        pack_kernel,
        [((18 * 64, N), BF)],
        [tissue_lengths, rate, gate, q, k, v, cotangent[0]],
        [SMEM, VMEM, VMEM] + [pl.BlockSpec(memory_space=pl.ANY)] * 4,
        name="pack",
        scratch=[pltpu.VMEM((4, N, 2 * N), BF), pltpu.SemaphoreType.DMA((4,))],
        limit=62,
    )
    got = swap_rows(send, True)
    row_cot = lax.all_gather(cotangent[0], "heads", axis=1, tiled=True)
    got, row_cot = lax.optimization_barrier((got, row_cot))
    qc, kc, vc, copies, sc = call(
        unpack_kernel,
        [(wide, BF)] * 3 + [((4 * N, 2 * N), BF), (few, F32)],
        [got],
        name="unpack",
    )
    x_groups = [[2 * x + core for x in range(4)] for core in range(2)]
    pairs = [[2 * x, 2 * x + 1] for x in range(4)]
    along_x = exchange(copies, "heads", x_groups)
    rate_late, unused = lax.optimization_barrier((rate, sc))
    o_row, tr, er = call(
        row_forward_kernel,
        [(wide, F32)] + [((4, N, N), BF)] * 2,
        [info, q, k, v, rate_late, gate],
        [SMEM] + [VMEM] * 5,
        flops=3_000_000_000,
        name="row_forward",
    )
    o_col, tc, ec = call(
        column_forward_kernel,
        [(wide, BF)] + [((4, N, N), BF)] * 2,
        [qc, kc, vc, sc],
        flops=3_000_000_000,
        name="column_forward",
    )
    along_x, o_row = lax.optimization_barrier((along_x, o_row))
    col_cot = lax.all_gather(along_x, "heads", axis=0, tiled=True, axis_index_groups=pairs)
    (send,) = call(
        column_backward_kernel,
        [((18 * 64, N), BF)],
        [qc, kc, sc, o_col, tc, ec, col_cot, out_weight],
        flops=3_000_000_000,
        name="column_backward",
    )
    got = swap_rows(send, False)
    own_wg, *sent_wg = call(
        weight_kernel,
        [((4 * N, 2 * N), BF)] * 4,
        [info, row_cot, o_row, col_cot, o_col],
        [SMEM] + [VMEM] * 4,
        flops=2_000_000_000,
        name="weight_gradient",
        scratch=[pltpu.VMEM((16, N, 2 * N), F32)],
    )
    rate_late, weight, unused = lax.optimization_barrier((rate, out_weight, own_wg))
    gq, gk, gv, gs = call(
        row_backward_kernel,
        [(wide, F32)] * 3 + [(few, F32)],
        [info, q, k, rate_late, gate, tr, er, row_cot, out_weight],
        [SMEM] + [VMEM] * 8,
        flops=3_000_000_000,
        name="row_backward",
    )
    block = (4, 2 * N, 2 * N)
    own, other = call(projection_kernel, [(block, BF)] * 2, [info, weight], [SMEM, VMEM], name="projection")
    swapped = lax.ppermute(other, "heads", [(i, i ^ 1) for i in range(8)])
    summed = own_wg.astype(F32)
    for step in (2, 1, 3):
        moves = [(z * 4 + y, z * 4 + (y + step) % 4) for z in range(16) for y in range(4)]
        summed = summed + lax.ppermute(sent_wg[step - 1], "rows", moves).astype(F32)
    summed, gs = lax.optimization_barrier((summed.astype(BF), gs))
    z_groups = [[z * 4 + y for z in range(16)] for y in range(4)]
    (hidden,) = call(hidden_kernel, [(wide, BF)], [got, o_row], name="hidden")
    hidden = lax.all_gather(hidden, "heads", axis=0, tiled=True, axis_index_groups=pairs)
    encoded, sent = call(
        encode_kernel,
        [(wide, F32), ((3, N, 2 * N), BF)],
        [info, hidden, own, swapped],
        [SMEM] + [VMEM] * 3,
        flops=1_000_000_000,
        name="encode",
    )
    for step in range(1, 4):
        moves = [(i, ((i // 2 + step) % 4) * 2 + i % 2) for i in range(8)]
        encoded = encoded + lax.ppermute(sent[step - 1], "heads", moves).astype(F32)
    encoded = encoded.astype(BF)[None]
    grad_q, grad_k, grad_v, grad_rate, grad_gate = call(
        gradient_kernel,
        [(wide, BF)] * 3 + [((2, N), F32), ((8, N), F32)],
        [info, got, gq, gk, gv, gs],
        [SMEM] + [VMEM] * 5,
        flops=1_000_000_000,
        name="gradients",
    )

    pieces = exchange(summed, "rows", z_groups)
    weight_grad = jnp.sum(pieces.reshape(16, 32, 2 * N).astype(F32), axis=0)
    rate_grad = grad_rate.T[None]
    gate_grad = grad_gate.reshape(2, 4, N).transpose(2, 0, 1)[None]
    return (encoded, grad_q[None], grad_k[None], grad_v[None], rate_grad, gate_grad, weight_grad)


def solution(mesh):
    in_specs = (
        P("rows", None, "heads"),
        P("rows", None, "heads"),
        P("rows", None, "heads"),
        P("rows", None, "heads"),
        P("rows", None, "heads", None),
        P("rows"),
        P("heads", None),
        P("rows", None, "heads"),
    )
    out_specs = (
        P("rows", None, "heads"),
        P("rows", None, "heads"),
        P("rows", None, "heads"),
        P("rows", None, "heads"),
        P("rows", None, "heads"),
        P("rows", None, "heads", None),
        P("rows", "heads"),
    )
    return jax.shard_map(
        per_device, mesh=mesh, in_specs=in_specs, out_specs=out_specs, check_vma=False
    )
```

```python
import functools

import jax
import jax.numpy as jnp
from jax import lax
from jax.experimental import pallas as pl
from jax.experimental.pallas import tpu as pltpu
from jax.sharding import PartitionSpec as P

N = 128
F32 = jnp.float32
BF = jnp.bfloat16


def dot(a, b, ca=1, cb=0):
    return lax.dot_general(a.astype(BF), b.astype(BF), (((ca,), (cb,)), ((), ())), preferred_element_type=F32)


def iotas(rows=N, cols=N):
    return lax.broadcasted_iota(jnp.int32, (rows, cols), 0), lax.broadcasted_iota(jnp.int32, (rows, cols), 1)


def shr(x, n):
    return lax.shift_right_logical(x, jnp.int32(n))


def invert(systems, length):
    i, j = iotas()
    apart = i ^ j
    eye = jnp.where(apart == 0, 1.0, 0.0)
    solved = [eye - jnp.where(apart == 1, a, 0.0) for a in systems]
    level = 1
    while (2 << level) <= length:
        mask = shr(apart, level) == 1
        crossing = [jnp.where(mask, a, 0.0).astype(BF) for a in systems]
        halves = [t.astype(BF) for t in solved]
        inner = [dot(c, t) for c, t in zip(crossing, halves)]
        solved = [t - dot(h, m) for t, h, m in zip(solved, halves, inner)]
        level += 1
    return solved


def split3(x):
    hi = x.astype(BF)
    rest = x - hi.astype(F32)
    mid = rest.astype(BF)
    return hi, mid, (rest - mid.astype(F32)).astype(BF)


def prefix_sums(length):
    i, j = iotas()
    shift = length.bit_length() - 1
    same = shr(i, shift) == shr(j, shift)
    before = [same & (i >= j), same & (i <= j)]
    return [jnp.where(m, 1.0, 0.0).astype(BF) for m in before], before, i == j


def prepare(q, k, small, length, first):
    sums, before, eye = prefix_sums(length)
    cum = [dot(m, small, 1, 1) for m in sums]
    cum_t = [dot(small, m, 1, 1) for m in sums]
    heads = []
    for h in range(2):
        lanes = slice(h * N, (h + 1) * N)
        kh, qh = k[:, lanes], q[:, lanes]
        gram = dot(kh, kh, 1, 1)
        cross = dot(qh, kh, 1, 1)
        diag = jnp.where(eye, gram, 0.0)
        s_col = lax.rsqrt(jnp.sum(diag, axis=1, keepdims=True) + 1e-6)
        s_row = lax.rsqrt(jnp.sum(diag, axis=0, keepdims=True) + 1e-6)
        gram = gram * (s_col * s_row)
        cross = cross * (s_row * (N ** -0.5))
        rate_row = small[8 + h : 9 + h, :]
        per = []
        for d in range(2):
            g = 4 * h + first + d
            ratio = cum[d][:, g : g + 1] - cum_t[d][g : g + 1, :]
            weight = jnp.exp(jnp.where(before[d], ratio, -jnp.inf)) * rate_row
            strict = jnp.where(eye, 0.0, weight)
            per.append((weight, strict, strict * gram, weight * cross))
        heads.append((s_col, s_row, per))
    return sums, heads


def forward(prepared, v, length):
    sums, heads = prepared
    systems = [p[2] for hd in heads for p in hd[2]]
    solved = [t.astype(BF) for t in invert(systems, length)]
    outs, errors = [], []
    for h in range(2):
        vh = v[:, h * N : (h + 1) * N]
        es = [dot(solved[2 * h + d], vh).astype(BF) for d in range(2)]
        mix = jnp.concatenate([heads[h][2][0][3].astype(BF), heads[h][2][1][3].astype(BF)], axis=1)
        outs.append(dot(mix, jnp.concatenate(es, axis=0)))
        errors += es
    return outs, solved, errors


def backward(prepared, solved, errors, q, k, small, cot, first):
    sums, heads = prepared
    i, j = iotas()
    gq, gk, gv, rowsums, colsums = [], [], [], [], []
    for h in range(2):
        lanes = slice(h * N, (h + 1) * N)
        s_col, s_row, per = heads[h]
        c, kh, qh = cot[:, lanes], k[:, lanes], q[:, lanes]
        es = errors[2 * h : 2 * h + 2]
        d_mix = dot(c, jnp.concatenate(es, axis=0), 1, 1)
        mix = jnp.concatenate([per[0][3].astype(BF), per[1][3].astype(BF)], axis=1)
        d_err = dot(mix, c, 0, 0)
        d_val = [dot(solved[2 * h + d], d_err[d * N : (d + 1) * N], 0, 0) for d in range(2)]
        d_sys = [-dot(d_val[d], es[d], 1, 1) for d in range(2)]
        d_gram, d_cross = 0.0, 0.0
        for d in range(2):
            weight, strict, system, mixing = per[d]
            dm = d_mix[:, d * N : (d + 1) * N]
            d_gram = d_gram + d_sys[d] * strict
            d_cross = d_cross + dm * weight
            total = d_sys[d] * system + dm * mixing
            rowsums.append(jnp.sum(total, axis=1, keepdims=True))
            colsums.append(jnp.sum(total, axis=0, keepdims=True))
        both = d_gram + d_gram.T
        gq.append(dot(d_cross * (s_row * (N ** -0.5)), kh))
        kf = kh.astype(F32)
        d_kn = dot(both * s_row, kh) + dot(d_cross, qh, 0, 0) * (N ** -0.5)
        along = s_col * jnp.sum(kf * d_kn, axis=1, keepdims=True)
        gk.append(s_col * (d_kn - kf * (s_col * along)))
        gv.append(d_val[0] + d_val[1])
    across = jnp.zeros((N, N), F32)
    for s in range(4):
        across = jnp.where(j == s, rowsums[s], across)
    d_cum = across.T[:8, :] - jnp.concatenate(colsums + [jnp.zeros((4, N), F32)], axis=0)
    pieces = split3(d_cum)
    gates = [sum(dot(p, sums[1 - d], 1, 1) for p in pieces) for d in range(2)]
    zero = jnp.zeros((1, N), F32)
    out = [zero] * 16
    for h in range(2):
        rate = small[8 + h : 9 + h, :]
        whole = colsums[2 * h] + colsums[2 * h + 1]
        out[8 + h] = jnp.where(rate > 0, whole / jnp.where(rate > 0, rate, 1.0), 0.0)
        for d in range(2):
            s = 2 * h + d
            out[4 * h + first + d] = gates[d][s : s + 1, :]
    out = jnp.concatenate(out, axis=0)
    return jnp.concatenate(gq, axis=1), jnp.concatenate(gk, axis=1), jnp.concatenate(gv, axis=1), out


VMEM = pl.BlockSpec(memory_space=pltpu.VMEM)
SMEM = pl.BlockSpec(memory_space=pltpu.SMEM)


def one_hot(mask):
    return jnp.where(mask, 1.0, 0.0).astype(BF)


def call(kernel, outs, args, specs=None, flops=100_000_000, name=None, scratch=(), limit=48):
    return pl.pallas_call(
        kernel,
        out_shape=[jax.ShapeDtypeStruct(shape, dtype) for shape, dtype in outs],
        in_specs=specs or [VMEM] * len(args),
        out_specs=[VMEM] * len(outs),
        scratch_shapes=list(scratch),
        compiler_params=pltpu.CompilerParams(vmem_limit_bytes=limit * 1024 * 1024),
        cost_estimate=pl.CostEstimate(flops=flops, bytes_accessed=2_000_000, transcendentals=0),
        name=name,
    )(*args)


def small_rows(info_ref, rate_ref, gate_ref):
    rows = jnp.concatenate(
        [gate_ref[...].astype(F32), rate_ref[...].astype(F32), jnp.ones((6, N), F32)], axis=0
    )
    row, patch = iotas(16, N)
    return jnp.where((patch < info_ref[0]) & (row < 11), rows, 0.0)


def shuffle(by_column, inverse, flip):
    i, j = iotas(144, 144)
    packed, plain = (j, i) if inverse else (i, j)
    peer = shr(packed * 3641, 16)
    rest = packed - 18 * peer
    c = rest & 1
    if flip:
        peer = 7 - peer
    within = 8 * c + peer if by_column else 2 * peer + c
    return one_hot(plain == 16 * shr(rest, 1) + within)


def pack(parts, small, out_ref):
    parts = [part[:, h * N : (h + 1) * N].astype(F32) for part in parts for h in range(2)]
    parts.append(jnp.concatenate([small, jnp.zeros((N - 16, N), F32)], axis=0).T)
    order = shuffle(True, False, False)
    for b in range(8):
        rows = [part[start + 8 * b : start + 8 * b + 8] for part in parts for start in (0, 64)]
        out_ref[144 * b : 144 * b + 144, :] = dot(order, jnp.concatenate(rows, axis=0)).astype(BF)


def unpack(got_ref, by_column, first=0, last=9, flip=False):
    order = shuffle(by_column, True, flip)[16 * first : 16 * last]
    places = range(7, -1, -1) if flip else range(8)
    blocks = [dot(order, got_ref[144 * b : 144 * b + 144, :]) for b in places]
    parts = []
    for s in range(last - first):
        if by_column:
            rows = [block[16 * s + 8 * c : 16 * s + 8 * c + 8] for c in range(2) for block in blocks]
        else:
            rows = [block[16 * s : 16 * s + 16] for block in blocks]
        parts.append(jnp.concatenate(rows, axis=0))
    return parts


def heads_of(parts):
    return [jnp.concatenate(parts[2 * a : 2 * a + 2], axis=1) for a in range(len(parts) // 2)]


def pack_kernel(info_ref, rate_ref, gate_ref, q_ref, k_ref, v_ref, cot_ref, out_ref, held, sems):
    copies = [
        pltpu.make_async_copy(ref, held.at[a], sems.at[a])
        for a, ref in enumerate((q_ref, k_ref, v_ref, cot_ref))
    ]
    for copy in copies:
        copy.start()
    small = small_rows(info_ref, rate_ref, gate_ref)
    scalars = jnp.concatenate([small, jnp.zeros((N - 16, N), F32)], axis=0).T.astype(BF)
    order = shuffle(False, False, True)
    for copy in copies:
        copy.wait()
    for b in range(8):
        rows = [held[a, 16 * b : 16 * b + 16, h * N : (h + 1) * N] for a in range(4) for h in range(2)]
        rows.append(scalars[16 * b : 16 * b + 16])
        out_ref[144 * (7 - b) : 144 * (8 - b), :] = dot(order, jnp.concatenate(rows, axis=0)).astype(BF)


def row_forward_kernel(info_ref, q_ref, k_ref, v_ref, rate_ref, gate_ref, o_ref, t_ref, e_ref):
    patch, unused = iotas(N, 2 * N)
    small = small_rows(info_ref, rate_ref, gate_ref)
    outs, solved, errors = forward(prepare(q_ref[...], k_ref[...], small, N, 0), v_ref[...], N)
    o_ref[...] = jnp.where(patch < info_ref[0], jnp.concatenate(outs, axis=1), 0.0)
    for s in range(4):
        t_ref[s], e_ref[s] = solved[s], errors[s]


def row_backward_kernel(
    info_ref, q_ref, k_ref, rate_ref, gate_ref, t_ref, e_ref, cot_ref, w_ref, gq_ref, gk_ref, gv_ref, gs_ref
):
    patch, unused = iotas(N, 2 * N)
    cot = jnp.where(patch < info_ref[0], dot(cot_ref[...], w_ref[...], 1, 1), 0.0).astype(BF)
    q, k = q_ref[...], k_ref[...]
    small = small_rows(info_ref, rate_ref, gate_ref)
    solved = [t_ref[s] for s in range(4)]
    errors = [e_ref[s] for s in range(4)]
    ready = prepare(q, k, small, N, 0)
    gq_ref[...], gk_ref[...], gv_ref[...], gs_ref[...] = backward(ready, solved, errors, q, k, small, cot, 0)


def unpack_kernel(got_ref, q_ref, k_ref, v_ref, copies_ref, small_ref):
    pieces = unpack(got_ref, True, flip=True)
    parts, scalars = heads_of(pieces), pieces[8]
    for part, ref in zip(parts, (q_ref, k_ref, v_ref)):
        ref[...] = part.astype(BF)
    for x in range(4):
        copies_ref[x * N : (x + 1) * N, :] = parts[3].astype(BF)
    small_ref[...] = scalars.T[:16, :]


def tissue_of(small):
    return jnp.concatenate([small, jnp.zeros((N - 16, N), F32)], axis=0).T[:, 10:11] > 0.5


def column_forward_kernel(q_ref, k_ref, v_ref, small_ref, o_ref, t_ref, e_ref):
    small = small_ref[...]
    outs, solved, errors = forward(prepare(q_ref[...], k_ref[...], small, 64, 2), v_ref[...], 64)
    o_ref[...] = jnp.where(tissue_of(small), jnp.concatenate(outs, axis=1), 0.0).astype(BF)
    for s in range(4):
        t_ref[s], e_ref[s] = solved[s], errors[s]


def column_backward_kernel(q_ref, k_ref, small_ref, o_ref, t_ref, e_ref, cot_ref, w_ref, send_ref):
    total = 0.0
    for block in range(8):
        rows = ((block & 1) * 4 + (block >> 1)) * N
        total = total + dot(cot_ref[rows : rows + N, :], w_ref[:, block * 2 * N : (block + 1) * 2 * N], 1, 1)
    q, k, small = q_ref[...], k_ref[...], small_ref[...]
    cot = jnp.where(tissue_of(small), total, 0.0).astype(BF)
    solved = [t_ref[s] for s in range(4)]
    errors = [e_ref[s] for s in range(4)]
    gq, gk, gv, gs = backward(prepare(q, k, small, 64, 2), solved, errors, q, k, small, cot, 2)
    pack([o_ref[...], gq, gk, gv], gs, send_ref)


def weight_kernel(
    info_ref, row_cot_ref, row_o_ref, col_cot_ref, col_o_ref, own_ref, first_ref, second_ref, third_ref, part_ref
):
    hidden = jnp.concatenate([row_o_ref[...].astype(BF), col_o_ref[...]], axis=0)
    for z in range(16):
        block, half = z >> 1, z & 1
        rows = ((block & 1) * 4 + (block >> 1)) * N
        col_cot = col_cot_ref[rows : rows + N, half * N : (half + 1) * N]
        cot = jnp.concatenate([row_cot_ref[:, z * N : (z + 1) * N], col_cot], axis=0)
        part_ref[z] = dot(cot, hidden, 0, 0)
    for step, ref in enumerate((own_ref, first_ref, second_ref, third_ref)):
        start = pl.multiple_of(((info_ref[3] + step) & 3) * 32, 32)
        for z in range(16):
            ref[z * 32 : (z + 1) * 32, :] = part_ref[z, pl.ds(start, 32), :].astype(BF)


def side_lanes(info_ref, step, side):
    block = 2 * ((info_ref[1] + step) & 3) + side
    return pl.ds(pl.multiple_of(block * 2 * N, 2 * N), 2 * N)


def projection_kernel(info_ref, w_ref, other_ref):
    for step in range(4):
        other_ref[step] = w_ref[:, side_lanes(info_ref, step, 1 - info_ref[2])]


def hidden_kernel(got_ref, o_ref, hidden_ref):
    (col,) = heads_of(unpack(got_ref, False, 0, 2))
    hidden_ref[...] = (o_ref[...] + col).astype(BF)


def gradient_kernel(
    info_ref, got_ref, gq_ref, gk_ref, gv_ref, gs_ref, q_ref, k_ref, v_ref, rate_ref, gate_ref
):
    pieces = unpack(got_ref, False, 2, 9)
    parts, scalars = heads_of(pieces), pieces[6]
    for part, row_ref, out_ref in zip(parts, (gq_ref, gk_ref, gv_ref), (q_ref, k_ref, v_ref)):
        out_ref[...] = (row_ref[...] + part).astype(BF)
    unused, patch = iotas(16, N)
    small = jnp.where(patch < info_ref[0], gs_ref[...] + scalars.T[:16, :], 0.0)
    gate_ref[...] = small[:8, :]
    rate_ref[...] = small[8:10, :]


def encode_kernel(info_ref, hidden_ref, w_ref, swapped_ref, kept_ref, sent_ref):
    core = info_ref[2]
    mine = hidden_ref[pl.ds(pl.multiple_of(core * N, N), N), :]
    other = hidden_ref[pl.ds(pl.multiple_of((1 - core) * N, N), N), :]
    for step in range(4):
        part = dot(mine, w_ref[:, side_lanes(info_ref, step, core)]) + dot(other, swapped_ref[step])
        if step == 0:
            kept_ref[...] = part
        else:
            sent_ref[step - 1] = part.astype(BF)


def exchange(x, axis, groups=None):
    return lax.all_to_all(x, axis, split_axis=0, concat_axis=0, tiled=True, axis_index_groups=groups)


def swap_rows(x, flip):
    groups = [list(range(63, -1, -1))] if flip else None
    return exchange(x.reshape(64, 9, 2, N), "rows", groups).reshape(18 * 64, N)


def per_device(
    query_proj, key_proj, value_proj, write_rate, log_gate, tissue_lengths, out_weight, cotangent
):
    q, k, v = query_proj[0], key_proj[0], value_proj[0]
    rate = write_rate[0].T
    gate = log_gate[0].transpose(1, 2, 0).reshape(8, N)
    me = lax.axis_index("heads")
    info = jnp.stack([tissue_lengths[0], lax.shift_right_logical(me, 1), me & 1, lax.axis_index("rows") & 3])
    wide, few = (N, 2 * N), (16, N)

    (send,) = call(
        pack_kernel,
        [((18 * 64, N), BF)],
        [tissue_lengths, rate, gate, q, k, v, cotangent[0]],
        [SMEM, VMEM, VMEM] + [pl.BlockSpec(memory_space=pl.ANY)] * 4,
        name="pack",
        scratch=[pltpu.VMEM((4, N, 2 * N), BF), pltpu.SemaphoreType.DMA((4,))],
        limit=62,
    )
    got = swap_rows(send, True)
    row_cot = lax.all_gather(cotangent[0], "heads", axis=1, tiled=True)
    got, row_cot = lax.optimization_barrier((got, row_cot))
    qc, kc, vc, copies, sc = call(
        unpack_kernel,
        [(wide, BF)] * 3 + [((4 * N, 2 * N), BF), (few, F32)],
        [got],
        name="unpack",
    )
    x_groups = [[2 * x + core for x in range(4)] for core in range(2)]
    pairs = [[2 * x, 2 * x + 1] for x in range(4)]
    along_x = exchange(copies, "heads", x_groups)
    rate_late, unused = lax.optimization_barrier((rate, sc))
    o_row, tr, er = call(
        row_forward_kernel,
        [(wide, F32)] + [((4, N, N), BF)] * 2,
        [info, q, k, v, rate_late, gate],
        [SMEM] + [VMEM] * 5,
        flops=3_000_000_000,
        name="row_forward",
    )
    o_col, tc, ec = call(
        column_forward_kernel,
        [(wide, BF)] + [((4, N, N), BF)] * 2,
        [qc, kc, vc, sc],
        flops=3_000_000_000,
        name="column_forward",
    )
    along_x, o_row = lax.optimization_barrier((along_x, o_row))
    col_cot = lax.all_gather(along_x, "heads", axis=0, tiled=True, axis_index_groups=pairs)
    (send,) = call(
        column_backward_kernel,
        [((18 * 64, N), BF)],
        [qc, kc, sc, o_col, tc, ec, col_cot, out_weight],
        flops=3_000_000_000,
        name="column_backward",
    )
    got = swap_rows(send, False)
    own_wg, *sent_wg = call(
        weight_kernel,
        [((4 * N, 2 * N), BF)] * 4,
        [info, row_cot, o_row, col_cot, o_col],
        [SMEM] + [VMEM] * 4,
        flops=2_000_000_000,
        name="weight_gradient",
        scratch=[pltpu.VMEM((16, N, 2 * N), F32)],
    )
    rate_late, weight, unused = lax.optimization_barrier((rate, out_weight, own_wg))
    gq, gk, gv, gs = call(
        row_backward_kernel,
        [(wide, F32)] * 3 + [(few, F32)],
        [info, q, k, rate_late, gate, tr, er, row_cot, out_weight],
        [SMEM] + [VMEM] * 8,
        flops=3_000_000_000,
        name="row_backward",
    )
    block = (4, 2 * N, 2 * N)
    (other,) = call(projection_kernel, [(block, BF)], [info, weight], [SMEM, VMEM], name="projection")
    swapped = lax.ppermute(other, "heads", [(i, i ^ 1) for i in range(8)])
    summed = own_wg.astype(F32)
    for step in (2, 1, 3):
        moves = [(z * 4 + y, z * 4 + (y + step) % 4) for z in range(16) for y in range(4)]
        summed = summed + lax.ppermute(sent_wg[step - 1], "rows", moves).astype(F32)
    summed, gs = lax.optimization_barrier((summed.astype(BF), gs))
    z_groups = [[z * 4 + y for z in range(16)] for y in range(4)]
    (hidden,) = call(hidden_kernel, [(wide, BF)], [got, o_row], name="hidden")
    hidden = lax.all_gather(hidden, "heads", axis=0, tiled=True, axis_index_groups=pairs)
    encoded, sent = call(
        encode_kernel,
        [(wide, F32), ((3, N, 2 * N), BF)],
        [info, hidden, out_weight, swapped],
        [SMEM] + [VMEM] * 3,
        flops=1_000_000_000,
        name="encode",
    )
    for step in range(1, 4):
        moves = [(i, ((i // 2 + step) % 4) * 2 + i % 2) for i in range(8)]
        encoded = encoded + lax.ppermute(sent[step - 1], "heads", moves).astype(F32)
    encoded = encoded.astype(BF)[None]
    grad_q, grad_k, grad_v, grad_rate, grad_gate = call(
        gradient_kernel,
        [(wide, BF)] * 3 + [((2, N), F32), ((8, N), F32)],
        [info, got, gq, gk, gv, gs],
        [SMEM] + [VMEM] * 5,
        flops=1_000_000_000,
        name="gradients",
    )

    pieces = exchange(summed, "rows", z_groups)
    weight_grad = jnp.sum(pieces.reshape(16, 32, 2 * N).astype(F32), axis=0)
    rate_grad = grad_rate.T[None]
    gate_grad = grad_gate.reshape(2, 4, N).transpose(2, 0, 1)[None]
    return (encoded, grad_q[None], grad_k[None], grad_v[None], rate_grad, gate_grad, weight_grad)


def solution(mesh):
    in_specs = (
        P("rows", None, "heads"),
        P("rows", None, "heads"),
        P("rows", None, "heads"),
        P("rows", None, "heads"),
        P("rows", None, "heads", None),
        P("rows"),
        P("heads", None),
        P("rows", None, "heads"),
    )
    out_specs = (
        P("rows", None, "heads"),
        P("rows", None, "heads"),
        P("rows", None, "heads"),
        P("rows", None, "heads"),
        P("rows", None, "heads"),
        P("rows", None, "heads", None),
        P("rows", "heads"),
    )
    return jax.shard_map(
        per_device, mesh=mesh, in_specs=in_specs, out_specs=out_specs, check_vma=False
    )
```
